512 devices in a mesh: ctx: 32 (over z, x), tp: 16 (over y, core).
Axes of the slice: x: 4, y: 8, z: 8, core: 2. Of those that a mesh axis runs over, the one named last changes fastest.
Arguments:
- q_slab: bfloat16 [2048, 8192], P(('ctx', 'tp')), may hold values from -6 to 6, as said below
- k_cache: bfloat16 [16384, 1024], P('ctx'), may hold values from -6 to 6, as said below
- v_cache: bfloat16 [16384, 1024], P('ctx'), may hold values from -6 to 6
- out_weight: bfloat16 [8192, 8192], P('ctx', 'tp'), may hold values from -0.0625 to 0.0625
- pattern_type: int32 [64], replicated, may hold values 0 or 1
- block_count: int32 [64], replicated, may hold values from 1 to 16, as said below
- kv_blocks: int32 [64, 32, 16], replicated, may hold values from 0 to 255, as said below
- vertical_cols: int32 [64, 1024], replicated, may hold values from 0 to 13823, as said below
- slash_offsets: int32 [64, 128], replicated, may hold values from 0 to 511, as said below
Outputs:
- projected: bfloat16 [2048, 8192], P(('ctx', 'tp'))
The draws below stay inside these ranges and needn't reach their ends.
Inputs may be any that keep to these rules, and one draw needn't show every extreme that they name: `q_slab`: entries are at most 6 in magnitude. `k_cache`: entries are at most 6 in magnitude. `block_count`: some head has 16 and some head has 1. kv_blocks[h, b, 0] is the query block's own key block (14336) / 64 + b; kv_blocks[h, b, 1] is key block 0; entries 1 to 15 of a row are distinct key blocks below the own one. `vertical_cols`: the columns of one head are distinct and include 0 and 13823. `slash_offsets`: the offsets of one head are distinct; its first two are 0 and 1, and 511 is among them.
All inputs are finite; a program needn't handle non-finite values.
Results may differ from the reference program's by a relative error of at most 0.02.
Values may be sent and summed in bfloat16 or wider, within the bound.
A program may use at most 64 MiB of HBM per device.

```python
import math
import jax
import jax.numpy as jnp
from jax import lax

H = 64
KVH = 8
HD = 128
D = 8192
NSEL = 16
NV = 1024
NS = 128
SMAX = 512
BLK = 64
SQ = 2048
L = 16384
QB = 32
N_CTX = 32


def draw_q_slab(key, part):
    key = jax.random.fold_in(key, 11)
    first_key, second_key = jax.random.split(key)
    scales = jnp.exp(jax.random.uniform(first_key, (SQ, 1), minval=math.log(0.3), maxval=math.log(3.0)))
    base_values = jax.random.normal(second_key, (SQ, H * HD))
    values = jnp.clip(base_values * scales, -6.0, 6.0)
    return values.astype(jnp.bfloat16)


def draw_k_cache(key, part):
    key = jax.random.fold_in(key, 12)
    first_key, second_key = jax.random.split(key)
    scales = jnp.exp(jax.random.uniform(first_key, (L, 1), minval=math.log(0.3), maxval=math.log(3.0)))
    base_values = jax.random.normal(second_key, (L, KVH * HD))
    values = jnp.clip(base_values * scales, -6.0, 6.0)
    return values.astype(jnp.bfloat16)


def draw_block_count(key, part):
    key = jax.random.fold_in(key, 21)
    first_key, second_key, third_key = jax.random.split(key, 3)
    counts = jax.random.randint(first_key, (H,), 1, NSEL + 1)
    largest_head = jax.random.randint(second_key, (), 0, H)
    smallest_head = (largest_head + 1 + jax.random.randint(third_key, (), 0, H - 1)) % H
    head_index = jnp.arange(H, dtype=jnp.int32)
    counts = jnp.where(head_index == largest_head, NSEL, counts)
    counts = jnp.where(head_index == smallest_head, 1, counts)
    return counts.astype(jnp.int32)


def draw_kv_blocks(key, part):
    key = jax.random.fold_in(key, 22)
    block_total = L // BLK
    first_block = (L - SQ) // BLK
    own_block = first_block + jnp.arange(SQ // BLK, dtype=jnp.int32)
    rank_values = jax.random.randint(key, (H, SQ // BLK, block_total), 0, max(2 ** 29 // block_total, 1))
    block_index = jnp.arange(block_total, dtype=jnp.int32)
    rank_values = rank_values * block_total + block_index
    rank_values = jnp.where(block_index[None, None, :] == 0, rank_values + 2 ** 30, rank_values)
    below_own = block_index[None, None, :] < own_block[None, :, None]
    rank_values = jnp.where(below_own, rank_values, -1)
    picked = lax.top_k(rank_values, NSEL - 1)[1].astype(jnp.int32)
    own_column = jnp.broadcast_to(own_block[None, :, None], (H, SQ // BLK, 1))
    return jnp.concatenate([own_column, picked], axis=2).astype(jnp.int32)


def draw_vertical_cols(key, part):
    key = jax.random.fold_in(key, 23)
    column_span = L - SQ - SMAX
    rank_values = jax.random.randint(key, (H, column_span), 0, max(2 ** 29 // column_span, 1))
    position_index = jnp.arange(column_span, dtype=jnp.int32)
    rank_values = rank_values * column_span + position_index
    boundary = (position_index == 0) | (position_index == column_span - 1)
    rank_values = jnp.where(boundary[None, :], rank_values + 2 ** 30, rank_values)
    return lax.top_k(rank_values, NV)[1].astype(jnp.int32)


def draw_slash_offsets(key, part):
    key = jax.random.fold_in(key, 24)
    rank_values = jax.random.randint(key, (H, SMAX), 0, max(2 ** 28 // SMAX, 1))
    offset_index = jnp.arange(SMAX, dtype=jnp.int32)
    rank_values = rank_values * SMAX + offset_index
    rank_values = jnp.where(offset_index[None, :] == SMAX - 1, 2 ** 30, rank_values)
    rank_values = jnp.where(offset_index[None, :] == 1, 2 ** 30 + 2 ** 28, rank_values)
    rank_values = jnp.where(offset_index[None, :] == 0, 2 ** 30 + 2 ** 29, rank_values)
    return lax.top_k(rank_values, NS)[1].astype(jnp.int32)


def touch_ends(drawn, key, low, largest):
    shape = drawn.shape
    place = [jax.random.randint(jax.random.fold_in(key, axis), (), 0, shape[axis]) for axis in range(len(shape))]
    drawn = drawn.at[tuple(place)].set(low)
    longest = shape.index(max(shape))
    place[longest] = (place[longest] + 1) % shape[longest]
    return drawn.at[tuple(place)].set(largest)


def level_of(key, shape, cuts, least, largest):
    gain = 1.0
    for dim, shards_of in cuts:
        heights = jax.random.uniform(jax.random.fold_in(jax.random.fold_in(key, 6), dim), (shards_of,), jnp.float32, least / len(cuts), largest / len(cuts))
        gain = gain * jnp.repeat(jnp.exp(heights), shape[dim] // shards_of).reshape((-1,) + (1,) * (len(shape) - 1 - dim))
    return gain


def normal_values(own_key, shape, width, limit, shards=(), kind=jnp.bfloat16):
    factor_of = level_of(own_key, shape, shards, -0.22, 0.18) if shards else 1.0
    values = jax.random.normal(own_key, shape, jnp.float32) * width * factor_of
    return jnp.minimum(jnp.maximum(values, -limit), limit).astype(kind)


def setup_inputs(seed: int = 0) -> dict:
    key_list = jax.random.split(jax.random.key(seed), 10)
    q_slab = draw_q_slab(jax.random.fold_in(key_list[9], 71), 0)
    k_cache = draw_k_cache(jax.random.fold_in(key_list[9], 71), 0)
    v_cache = normal_values(key_list[2], (L, KVH * HD), 1.0, 6.0, ((0, 32),))
    out_weight = normal_values(key_list[3], (H * HD, D), (H * HD) ** -0.5, 0.0625, ((0, 32), (1, 16)))
    pattern_type = touch_ends((jax.random.randint(key_list[4], (H,), 0, 2) < 1).astype(jnp.int32), jax.random.fold_in(key_list[4], 1), 0, 1)
    block_count = draw_block_count(jax.random.fold_in(key_list[9], 71), 0)
    kv_blocks = draw_kv_blocks(jax.random.fold_in(key_list[9], 71), 0)
    vertical_cols = draw_vertical_cols(jax.random.fold_in(key_list[9], 71), 0)
    slash_offsets = draw_slash_offsets(jax.random.fold_in(key_list[9], 71), 0)
    return {"q_slab": q_slab, "k_cache": k_cache, "v_cache": v_cache, "out_weight": out_weight, "pattern_type": pattern_type, "block_count": block_count, "kv_blocks": kv_blocks, "vertical_cols": vertical_cols, "slash_offsets": slash_offsets}


masked_score = -1e+30

def block_head(query_rows, key_head, value_head, chosen, tile_count, first_position):
    score_scale = 1.0 / math.sqrt(HD)
    offset_inner = jnp.arange(BLK, dtype=jnp.int32)
    key_index = (chosen[:, None] * BLK + offset_inner[None, :]).reshape(NSEL * BLK)
    tile_number = jnp.repeat(jnp.arange(NSEL, dtype=jnp.int32), BLK)
    positions = first_position + offset_inner
    usable = (tile_number < tile_count)[None, :] & (key_index[None, :] <= positions[:, None])
    key_rows = key_head[key_index]
    value_rows = value_head[key_index]
    scores = jnp.dot(query_rows, key_rows.T, preferred_element_type=jnp.float32) * score_scale
    scores = jnp.where(usable, scores, masked_score)
    row_max = lax.optimization_barrier(jnp.max(scores, axis=1, keepdims=True))
    weights = jnp.where(usable, jnp.exp(scores - row_max), 0.0)
    weight_total = lax.optimization_barrier(jnp.sum(weights, axis=1, keepdims=True))
    mixed_sum = jnp.dot(weights.astype(jnp.bfloat16), value_rows, preferred_element_type=jnp.float32)
    return (mixed_sum / weight_total).astype(jnp.bfloat16)

def slash_head(query_rows, key_head, value_head, columns, offsets, first_position):
    score_scale = 1.0 / math.sqrt(HD)
    positions = first_position + jnp.arange(BLK, dtype=jnp.int32)
    diagonal = positions[:, None] - offsets[None, :]
    column_keys = key_head[columns]
    column_values = value_head[columns]
    diagonal_keys = key_head[diagonal].astype(jnp.float32)
    diagonal_values = value_head[diagonal].astype(jnp.float32)
    column_scores = jnp.dot(query_rows, column_keys.T, preferred_element_type=jnp.float32) * score_scale
    diagonal_scores = jnp.einsum('rd,rsd->rs', query_rows.astype(jnp.float32), diagonal_keys, precision=lax.Precision.HIGHEST) * score_scale
    row_max = jnp.maximum(lax.optimization_barrier(jnp.max(column_scores, axis=1)), lax.optimization_barrier(jnp.max(diagonal_scores, axis=1)))[:, None]
    column_weights = jnp.exp(column_scores - row_max)
    diagonal_weights = jnp.exp(diagonal_scores - row_max)
    weight_total = lax.optimization_barrier(jnp.sum(column_weights, axis=1, keepdims=True)) + lax.optimization_barrier(jnp.sum(diagonal_weights, axis=1, keepdims=True))
    rounded_diagonal = lax.optimization_barrier(diagonal_weights.astype(jnp.bfloat16)).astype(jnp.float32)
    mixed_sum = jnp.dot(column_weights.astype(jnp.bfloat16), column_values, preferred_element_type=jnp.float32)
    mixed_sum = mixed_sum + jnp.einsum('rs,rsd->rd', rounded_diagonal, diagonal_values, precision=lax.Precision.HIGHEST)
    return (mixed_sum / weight_total).astype(jnp.bfloat16)

def reference(q_slab, k_cache, v_cache, out_weight, pattern_type, block_count, kv_blocks, vertical_cols, slash_offsets):
    group_size = H // KVH
    slab_start = L - SQ

    def one_head(head_index):
        group_index = head_index // group_size
        key_head = lax.dynamic_slice_in_dim(k_cache, group_index * HD, HD, 1)
        value_head = lax.dynamic_slice_in_dim(v_cache, group_index * HD, HD, 1)
        query_head = lax.dynamic_slice_in_dim(q_slab, head_index * HD, HD, 1).reshape(QB, BLK, HD)
        head_blocks = kv_blocks[head_index]
        tile_count = block_count[head_index]
        columns = vertical_cols[head_index]
        offsets = slash_offsets[head_index]
        kind_flag = pattern_type[head_index]

        def one_block(block_number):
            query_rows = query_head[block_number]
            first_position = jnp.int32(slab_start) + block_number * BLK
            return lax.cond(kind_flag == 0, lambda: block_head(query_rows, key_head, value_head, head_blocks[block_number], tile_count, first_position), lambda: slash_head(query_rows, key_head, value_head, columns, offsets, first_position))
        return lax.map(one_block, jnp.arange(QB, dtype=jnp.int32)).reshape(SQ, HD)
    heads_out = lax.map(one_head, jnp.arange(H, dtype=jnp.int32))
    attended = jnp.transpose(heads_out, (1, 0, 2)).reshape(SQ, H * HD)
    group_width = H * HD // N_CTX

    def add_group(running, group_number):
        rows_part = lax.dynamic_slice_in_dim(attended, group_number * group_width, group_width, 1)
        weight_part = lax.dynamic_slice_in_dim(out_weight, group_number * group_width, group_width, 0)
        partial_sum = jnp.dot(rows_part, weight_part, preferred_element_type=jnp.float32)
        partial_sum = lax.optimization_barrier(partial_sum.astype(jnp.bfloat16)).astype(jnp.float32)
        return (running + partial_sum, None)
    projected, _ = lax.scan(add_group, jnp.zeros((SQ, D), jnp.float32), jnp.arange(N_CTX, dtype=jnp.int32))
    return projected.astype(jnp.bfloat16)
```

```python
import math

import jax
import jax.numpy as jnp
from jax import lax
from jax.experimental import pallas as pl
from jax.experimental.pallas import tpu as pltpu
from jax.sharding import PartitionSpec as P

H = 64
KVH = 8
HD = 128
BLK = 64
SLAB0 = 14336
NX, NZ, NY = 4, 8, 8
NT = 2 * NY
PART = 4096
MASKED = -1e30
MESH = pl.DeviceIdType.MESH
VMEM_LIMIT = 48 * 1024 * 1024
F32 = jnp.float32
BF16 = jnp.bfloat16


def place():
    ctx = lax.axis_index("ctx")
    tp = lax.axis_index("tp")
    return ctx, tp, ctx // NX, ctx % NX, tp // 2, tp % 2


def remote(src, dst, send_sem, recv_sem, ctx, tp):
    return pltpu.make_async_remote_copy(
        src_ref=src,
        dst_ref=dst,
        send_sem=send_sem,
        recv_sem=recv_sem,
        device_id=(ctx, tp),
        device_id_type=MESH,
    )


def arrived(ref, sem):
    pltpu.make_async_copy(ref, ref, sem).wait()


def ring_gather(view, ctx, y, c, sends, right_recv, left_recv, on_arrival):
    right = ((y + 1) % NY) * 2 + c
    left = ((y + NY - 1) % NY) * 2 + c
    started = []
    for s in range(4):
        from_left = (y + NY - s) % NY
        from_right = (y + s) % NY
        for h in range(2):
            here_r = view(from_left, h)
            here_l = view(from_right, h)
            if s > 0:
                arrived(here_r, right_recv.at[2 * (s - 1) + h])
                on_arrival(here_r)
            if s < 3 or h == 0:
                copy = remote(here_r, here_r, sends.at[4 * s + h], right_recv.at[2 * s + h], ctx, right)
                copy.start()
                started.append(copy)
            if s > 0:
                arrived(here_l, left_recv.at[2 * (s - 1) + h])
                on_arrival(here_l)
            if s < 3 or h == 1:
                copy = remote(here_l, here_l, sends.at[4 * s + 2 + h], left_recv.at[2 * s + h], ctx, left)
                copy.start()
                started.append(copy)
    across = (y + 4) % NY
    for h in range(2):
        ref = view(across, h)
        arrived(ref, (right_recv if h == 0 else left_recv).at[6 + h])
        on_arrival(ref)
    return started


def spread_kernel(
    q_ref, k_ref, v_ref, w_ref,
    qb, kvb, wb,
    qt, qs, q2, qf,
    q1_send, q1_recv, q2_send, q2_recv, qx_send, qx_recv,
    kz_send, kz_recv, ring_send, right_recv, left_recv, core_send, core_recv,
    w_send, w_recv, wc_send, wc_recv, local_sem,
):
    ctx, t, z, x, y, c = place()
    zc = z // 4
    partner = 2 * y + 1 - c

    barrier = pltpu.get_barrier_semaphore()
    for d in range(1, NT):
        pl.semaphore_signal(barrier, inc=1, device_id=(ctx, (t + d) % NT), device_id_type=MESH)
    for d in range(1, NZ):
        pl.semaphore_signal(barrier, inc=1, device_id=(((z + d) % NZ) * NX + x, t), device_id_type=MESH)
    for d in range(1, NX):
        pl.semaphore_signal(barrier, inc=1, device_id=(z * NX + (x + d) % NX, t), device_id_type=MESH)

    for yy in range(NY):
        for g in range(KVH):
            head = 8 * g + yy
            qt[yy, g] = q_ref[:, head * HD : (head + 1) * HD].astype(F32)

    pl.semaphore_wait(barrier, NT - 1 + NZ - 1 + NX - 1)

    q1 = [
        remote(qt.at[(y + d) % NY], qs.at[t], q1_send.at[d], q1_recv, ctx, ((y + d) % NY) * 2 + zc)
        for d in range(NY)
    ]
    for d in range(1, NY):
        q1[d].start()

    @pl.when(zc == c)
    def _():
        pltpu.make_async_copy(qt.at[y], qs.at[t], q1_recv).start()

    @pl.when(zc != c)
    def _():
        q1[0].start()

    rows = pl.ds(pl.multiple_of(32 * t, 32), 32)
    kz = []
    for d in (4, 3, 5, 2, 6, 1, 7):
        g = (z + d) % NZ
        cols = pl.ds(pl.multiple_of(HD * g, HD), HD)
        for i, ref in enumerate((k_ref, v_ref)):
            copy = remote(ref.at[rows, cols], kvb.at[t, i, z], kz_send.at[2 * d + i], kz_recv, g * NX + x, t)
            copy.start()
            kz.append(copy)
    own = pl.ds(pl.multiple_of(HD * z, HD), HD)
    for i, ref in enumerate((k_ref, v_ref)):
        pltpu.make_async_copy(ref.at[rows, own], kvb.at[t, i, z], kz_recv).start()

    def w_view(xx, cc):
        return wb.at[
            pl.ds(pl.multiple_of(256 * xx, 256), 256), pl.ds(pl.multiple_of(512 * cc, 512), 512)
        ]

    wx = [
        remote(w_ref, w_view(x, c), w_send.at[d], w_recv.at[d], z * NX + (x + d) % NX, t)
        for d in range(1, NX)
    ]
    for copy in wx:
        copy.start()
    w_own = pltpu.make_async_copy(w_ref, w_view(x, c), local_sem)
    w_own.start()
    wc = [remote(w_ref, w_view(x, c), wc_send.at[0], wc_recv, ctx, partner)]
    wc[0].start()

    @pl.when(zc == c)
    def _():
        arrived(qs, q1_recv)
        for d in range(1, NZ):
            g = (z + d) % NZ
            remote(qs.at[:, g], q2.at[z % 4], q2_send.at[d], q2_recv, g * NX + x, t).start()
        pltpu.make_async_copy(qs.at[:, z], q2.at[z % 4], q2_recv).start()

    arrived(kvb.at[t], kz_recv)
    to_core = []

    def on_core(ref):
        copy = remote(ref, ref, core_send.at[len(to_core)], core_recv, ctx, partner)
        copy.start()
        to_core.append(copy)

    for h in range(2):
        on_core(kvb.at[t, h])

    arrived(q2, q2_recv)
    for i in range(64):
        qf[4 * i : 4 * i + 4, :] = q2[i // 16, i % 16]
    qb[x] = qf[...].astype(BF16)
    qx = [
        remote(qb.at[x], qb.at[x], qx_send.at[d], qx_recv.at[d], z * NX + (x + d) % NX, t)
        for d in range(1, NX)
    ]
    for copy in qx:
        copy.start()

    ring = ring_gather(
        lambda yy, h: kvb.at[2 * yy + c, h], ctx, y, c, ring_send, right_recv, left_recv, on_core
    )

    for d in range(1, NX):
        xx = (x + NX - d) % NX
        ref = w_view(xx, c)
        arrived(ref, w_recv.at[d])
        copy = remote(ref, ref, wc_send.at[d], wc_recv, ctx, partner)
        copy.start()
        wc.append(copy)
    for d in range(1, NX):
        arrived(qb.at[(x + NX - d) % NX], qx_recv.at[d])
    arrived(kvb.at[pl.ds(0, NY)], core_recv)
    arrived(wb.at[:, pl.ds(0, 512)], wc_recv)
    w_own.wait()
    for copy in q1[1:] + kz + wx + wc + qx + ring + to_core:
        copy.wait_send()

    @pl.when(zc != c)
    def _():
        q1[0].wait_send()

    @pl.when(zc == c)
    def _():
        for d in range(1, NZ):
            g = (z + d) % NZ
            remote(qs.at[:, g], q2.at[z % 4], q2_send.at[d], q2_recv, g * NX + x, t).wait_send()


def spread(q, k, v, w):
    dma = pltpu.SemaphoreType.DMA
    any_spec = pl.BlockSpec(memory_space=pl.ANY)
    vmem = pl.BlockSpec(memory_space=pltpu.VMEM)
    return pl.pallas_call(
        spread_kernel,
        out_shape=(
            jax.ShapeDtypeStruct((NX, 256, HD), BF16),
            jax.ShapeDtypeStruct((NT, 2, NZ, 32, HD), BF16),
            jax.ShapeDtypeStruct((1024, 1024), BF16),
        ),
        in_specs=[vmem, any_spec, any_spec, any_spec],
        out_specs=(vmem, vmem, any_spec),
        scratch_shapes=[
            pltpu.VMEM((NY, KVH, 4, HD), F32),
            pltpu.VMEM((NT, KVH, 4, HD), F32),
            pltpu.VMEM((4, NT, 4, HD), F32),
            pltpu.VMEM((256, HD), F32),
            dma((8,)), dma, dma((8,)), dma, dma((4,)), dma((4,)),
            dma((16,)), dma, dma((16,)), dma((8,)), dma((8,)), dma((16,)), dma,
            dma((4,)), dma((4,)), dma((4,)), dma, dma,
        ],
        compiler_params=pltpu.CompilerParams(
            collective_id=0, has_side_effects=True, vmem_limit_bytes=VMEM_LIMIT
        ),
        name="spread",
    )(q, k, v, w)


def attend_kernel(
    kind_ref, count_ref, blocks_ref, cols_ref, offs_ref, qb, kvb,
    o_ref, st_ref,
    row_bias, tile_bias, scores,
):
    ctx, t, z, x, y, c = place()
    head = 8 * z + y
    slash = kind_ref[head] == 1
    count = count_ref[head]

    def lanes(shape):
        return lax.broadcasted_iota(jnp.int32, shape, len(shape) - 1)

    def subs(shape):
        return lax.broadcasted_iota(jnp.int32, shape, 0)

    @pl.when(slash)
    def _():
        cols = cols_ref[pl.ds(head, 1), :]
        tile = subs((32, 1024))
        tile = 16 * (tile // 4) + 4 * x + tile % 4
        hi = jnp.where(cols // 128 == tile, 1.0, 0.0).astype(BF16)
        lo = jnp.where(cols % 128 == subs((128, 1024)), 1.0, 0.0).astype(BF16)
        member = lax.dot_general(hi, lo, (((1,), (1,)), ((), ())), preferred_element_type=F32)
        bias = jnp.where(member > 0.5, 0.0, MASKED)
        for i in range(32):
            row_bias[i] = jnp.broadcast_to(bias[i : i + 1, :], (32, 128))
        rev = 511 - offs_ref[pl.ds(head, 1), :]
        lo_row = subs((128, 128))
        hi_row = subs((8, 128))
        rows = []
        for phase in range(2):
            place_of = rev + 128 + 64 * phase
            hi = jnp.where(place_of // 128 == hi_row, 1.0, 0.0).astype(BF16)
            lo = jnp.where(place_of % 128 == lo_row, 1.0, 0.0).astype(BF16)
            found = lax.dot_general(hi, lo, (((1,), (1,)), ((), ())), preferred_element_type=F32)
            rows.append(jnp.where(found > 0.5, 0.0, MASKED))
        tile_bias[0] = jnp.full((64, 128), MASKED, F32)
        tile_bias[11] = jnp.full((64, 128), MASKED, F32)
        for i in range(10):
            start = 448 - 64 * i + 128
            phase = (start // 64) % 2
            first = (start + 64 * phase) // 128
            pair = jnp.concatenate(
                [rows[phase][first : first + 1, :], rows[phase][first + 1 : first + 2, :]], axis=1
            )
            wide = jnp.broadcast_to(pair, (64, 256))
            rolled = pltpu.roll(wide, 256 - 63, 1, stride=1, stride_axis=0)
            tile_bias[i + 1] = rolled[:, :128]

    @pl.when(jnp.logical_not(slash))
    def _():
        chosen = blocks_ref[head]
        place_of = lanes((32, 128))
        block = 8 * (4 * (place_of // 8) + x) + place_of % 8
        found = jnp.full((32, 128), MASKED, F32)
        for k in range(16):
            hit = jnp.logical_and(chosen[:, k : k + 1] == block, k < count)
            found = jnp.where(hit, 0.0, found)
        left = lanes((32, 128)) < 64
        for i in range(32):
            row_bias[i] = jnp.where(left, found[:, 2 * i : 2 * i + 1], found[:, 2 * i + 1 : 2 * i + 2])
        back = subs((64, 128)) - lanes((64, 128))
        for i in range(12):
            tile_bias[i] = jnp.where(back + 64 * (i - 1) >= 0, 0.0, MASKED)

    scale = math.log2(math.e) / math.sqrt(HD)

    def group(xx, carry):
        q = qb[xx]
        highest = [jnp.full((64, 128), -3e38, F32) for _ in range(4)]
        for zz in range(NZ):
            keys = kvb[:, 0, zz].reshape(512, HD)
            s = lax.dot_general(q, keys, (((1,), (1,)), ((), ())), preferred_element_type=F32)
            for zl in range(4):
                b = 16 * c + 4 * zl + xx
                for w in range(4):
                    bias = row_bias[4 * zz + w, pl.ds(b, 1), :]
                    if zz >= 6:
                        which = 224 + b - 8 * (4 * zz + x) - 2 * w + 1
                        band = tile_bias[jnp.clip(which, 0, 11)]
                        bias = jnp.where(slash, jnp.maximum(bias, band), jnp.minimum(bias, band))
                    part = s[64 * zl : 64 * zl + 64, 128 * w : 128 * w + 128] * scale + bias
                    scores[64 * zl : 64 * zl + 64, 512 * zz + 128 * w : 512 * zz + 128 * w + 128] = part
                    highest[zl] = jnp.maximum(highest[zl], part)
        top = [jnp.max(h, axis=1, keepdims=True) for h in highest]
        top = jnp.concatenate(top, axis=0)
        total = jnp.zeros((256, 128), F32)
        mixed = jnp.zeros((256, HD), F32)
        for zz in range(NZ):
            values = kvb[:, 1, zz].reshape(512, HD)
            weight = jnp.exp2(scores[:, 512 * zz : 512 * zz + 512] - top)
            for w in range(4):
                total = total + weight[:, 128 * w : 128 * w + 128]
            mixed = mixed + jnp.dot(weight.astype(BF16), values, preferred_element_type=F32)
        total = jnp.sum(total, axis=1, keepdims=True)
        o_ref[xx] = (mixed / total).astype(BF16)
        level = jnp.broadcast_to(top + jnp.log2(total), (256, 128))
        st_ref[xx] = level.T[:8, :]
        return carry

    lax.fori_loop(0, NX, group, 0)


def attend(kinds, counts, blocks, cols, offs, qb, kvb):
    vmem = pl.BlockSpec(memory_space=pltpu.VMEM)
    smem = pl.BlockSpec(memory_space=pltpu.SMEM)
    return pl.pallas_call(
        attend_kernel,
        out_shape=(
            jax.ShapeDtypeStruct((NX, 256, HD), BF16),
            jax.ShapeDtypeStruct((NX, 8, 256), F32),
        ),
        in_specs=[smem, smem, vmem, vmem, vmem, vmem, vmem],
        out_specs=(vmem, vmem),
        scratch_shapes=[
            pltpu.VMEM((32, 32, 128), F32),
            pltpu.VMEM((12, 64, 128), F32),
            pltpu.VMEM((256, PART), F32),
        ],
        compiler_params=pltpu.CompilerParams(vmem_limit_bytes=VMEM_LIMIT),
        name="attend",
    )(kinds, counts, blocks, cols, offs, qb, kvb)


def project_kernel(
    o_ref, st_ref, w_ref,
    out_ref,
    ob, sb, wv, ab, part, rb, fb, fr,
    ox_send, ox_recv, ring_send, right_recv, left_recv,
    z_send, z_recv, f_send, f_recv, w_sem,
):
    ctx, t, z, x, y, c = place()
    zc = z // 4

    w_copy = pltpu.make_async_copy(w_ref, wv, w_sem)
    w_copy.start()
    barrier = pltpu.get_barrier_semaphore()
    for d in range(1, NT):
        pl.semaphore_signal(barrier, inc=1, device_id=(ctx, (t + d) % NT), device_id_type=MESH)
    for d in range(1, NZ):
        for cc in range(2):
            pl.semaphore_signal(
                barrier, inc=1, device_id=(((z + d) % NZ) * NX + x, 2 * y + cc), device_id_type=MESH
            )
    for d in range(1, NX):
        pl.semaphore_signal(barrier, inc=1, device_id=(z * NX + (x + d) % NX, t), device_id_type=MESH)
    pl.semaphore_wait(barrier, NT - 1 + 2 * (NZ - 1) + NX - 1)

    sends = []
    for d in (2, 1, 3):
        xx = (x + d) % NX
        for i, (src, dst) in enumerate(((st_ref, sb), (o_ref, ob))):
            copy = remote(src.at[xx], dst.at[d], ox_send.at[2 * d + i], ox_recv.at[2 * d + i], z * NX + xx, t)
            copy.start()
            sends.append(copy)
    for d in range(1, NX):
        arrived(sb.at[d], ox_recv.at[2 * d])
    levels = [st_ref[x]] + [sb[d] for d in range(1, NX)]
    top = jnp.maximum(jnp.maximum(levels[0], levels[1]), jnp.maximum(levels[2], levels[3]))
    shares = [jnp.exp2(level - top) for level in levels]
    total = (shares[0] + shares[1]) + (shares[2] + shares[3])
    shares = [share / total for share in shares]
    table = jnp.concatenate(shares + [jnp.zeros((96, 256), F32)], axis=0).T
    for d in range(1, NX):
        arrived(ob.at[d], ox_recv.at[2 * d + 1])
    mixed = table[:, 0:1] * o_ref[x].astype(F32)
    for d in range(1, NX):
        mixed = mixed + table[:, 8 * d : 8 * d + 1] * ob[d].astype(F32)

    def view(yy, h):
        return ab.at[pl.ds(128 * h, 128), pl.ds(pl.multiple_of(HD * yy, HD), HD)]

    ab[:, pl.ds(pl.multiple_of(HD * y, HD), HD)] = mixed.astype(BF16)
    sends += ring_gather(view, ctx, y, c, ring_send, right_recv, left_recv, lambda ref: None)
    w_copy.wait()

    to_z = []
    for i in range(4):
        rows = jnp.dot(ab[64 * i : 64 * i + 64, :], wv[...], preferred_element_type=F32).astype(BF16)
        for cc in range(2):
            part[i, cc] = rows[:, 512 * cc : 512 * cc + 512]
    for i in range(4):
        zz = 4 * c + i
        for cc in range(2):
            copy = remote(part.at[i, cc], rb.at[z], z_send.at[2 * i + cc], z_recv, zz * NX + x, 2 * y + cc)
            to_z.append((zz, cc, i, copy))
            mine = jnp.logical_and(zz == z, cc == c)

            @pl.when(jnp.logical_not(mine))
            def _():
                copy.start()

            @pl.when(mine)
            def _():
                pltpu.make_async_copy(part.at[i, cc], rb.at[z], z_recv).start()

    arrived(rb, z_recv)
    summed = rb[0].astype(F32)
    for g in range(1, NZ):
        summed = summed + rb[g].astype(F32)
    for tt in range(NT):
        fb[tt] = summed[4 * tt : 4 * tt + 4, :]
    for d in range(1, NT):
        tt = (t + d) % NT
        copy = remote(fb.at[tt], fr.at[t], f_send.at[d], f_recv, ctx, tt)
        copy.start()
        sends.append(copy)
    pltpu.make_async_copy(fb.at[t], fr.at[t], f_recv).start()
    arrived(fr, f_recv)
    for tt in range(NT):
        out_ref[:, 512 * tt : 512 * tt + 512] = fr[tt].astype(BF16)
    for copy in sends:
        copy.wait_send()
    for zz, cc, i, copy in to_z:
        mine = jnp.logical_and(zz == z, cc == c)

        @pl.when(jnp.logical_not(mine))
        def _():
            copy.wait_send()


def project(o, st, w):
    dma = pltpu.SemaphoreType.DMA
    any_spec = pl.BlockSpec(memory_space=pl.ANY)
    vmem = pl.BlockSpec(memory_space=pltpu.VMEM)
    return pl.pallas_call(
        project_kernel,
        out_shape=jax.ShapeDtypeStruct((4, 8192), BF16),
        in_specs=[vmem, vmem, any_spec],
        out_specs=vmem,
        scratch_shapes=[
            pltpu.VMEM((NX, 256, HD), BF16),
            pltpu.VMEM((NX, 8, 256), F32),
            pltpu.VMEM((1024, 1024), BF16),
            pltpu.VMEM((256, 1024), BF16),
            pltpu.VMEM((4, 2, 64, 512), BF16),
            pltpu.VMEM((NZ, 64, 512), BF16),
            pltpu.VMEM((NT, 4, 512), F32),
            pltpu.VMEM((NT, 4, 512), F32),
            dma((8,)), dma((8,)), dma((16,)), dma((8,)), dma((8,)),
            dma((8,)), dma, dma((16,)), dma, dma,
        ],
        compiler_params=pltpu.CompilerParams(
            collective_id=1, has_side_effects=True, vmem_limit_bytes=VMEM_LIMIT
        ),
        name="project",
    )(o, st, w)


def shards(q, k, v, w, kinds, counts, blocks, cols, offs):
    qb, kvb, wb = spread(q, k, v, w)
    o, st = attend(kinds, counts, blocks, cols, offs, qb, kvb)
    return project(o, st, wb)


def solution(mesh):
    return jax.shard_map(
        shards,
        mesh=mesh,
        in_specs=(
            P(("ctx", "tp"), None),
            P("ctx", None),
            P("ctx", None),
            P("ctx", "tp"),
            P(),
            P(),
            P(),
            P(),
            P(),
        ),
        out_specs=P(("ctx", "tp"), None),
        check_vma=False,
    )
```

```python
import math

import jax
import jax.numpy as jnp
from jax import lax
from jax.experimental import pallas as pl
from jax.experimental.pallas import tpu as pltpu
from jax.sharding import PartitionSpec as P

H = 64
KVH = 8
HD = 128
NX, NZ, NY = 4, 8, 8
NT = 2 * NY
MASKED = -1e30
MESH = pl.DeviceIdType.MESH
F32 = jnp.float32
BF16 = jnp.bfloat16
SCALE = math.log2(math.e) / math.sqrt(HD)


def remote(src, dst, send_sem, recv_sem, ctx, tp):
    return pltpu.make_async_remote_copy(
        src_ref=src,
        dst_ref=dst,
        send_sem=send_sem,
        recv_sem=recv_sem,
        device_id=(ctx, tp),
        device_id_type=MESH,
    )


def arrived(ref, sem):
    pltpu.make_async_copy(ref, ref, sem).wait()


def lanes(shape):
    return lax.broadcasted_iota(jnp.int32, shape, len(shape) - 1)


def subs(shape):
    return lax.broadcasted_iota(jnp.int32, shape, 0)


def aligned(start, size):
    return pl.ds(pl.multiple_of(start, size), size)


def by_distance(i):
    odd = i % 2
    return odd * ((i + 1) // 2) + (1 - odd) * ((8 - i // 2) % 8)


def member_rows(values, rows, first_row):
    high = jnp.where(values // 128 == first_row, 1.0, 0.0).astype(BF16)
    low = jnp.where(values % 128 == subs((128, values.shape[1])), 1.0, 0.0).astype(BF16)
    found = lax.dot_general(high, low, (((1,), (1,)), ((), ())), preferred_element_type=F32)
    return jnp.where(found > 0.5, 0.0, MASKED)


def fill_masks(slash, count, head, x, y, blocks, cols8, offs8, row_bias, tile_bias):
    tile = subs((32, 1024))
    tile = 16 * (tile // 4) + 4 * x + tile % 4
    vertical = member_rows(cols8[pl.ds(y, 1), :], 32, tile)
    ids = jnp.where(lanes((32, 16, H)) == head, blocks[...].astype(F32), 0.0)
    ids = jnp.sum(ids, axis=2, keepdims=True)
    at = lanes((1, 1, 128))
    block = (8 * (4 * (at // 8) + x) + at % 8).astype(F32)
    turn = lax.broadcasted_iota(jnp.int32, (32, 16, 128), 1)
    hit = jnp.where(ids == block, 0.0, MASKED)
    hit = jnp.where(turn >= 1, jnp.where(turn < count, hit, MASKED), MASKED)
    chosen = jnp.max(hit, axis=1)
    left = lanes((32, 128)) < 64
    for i in range(32):
        pair = jnp.where(left, chosen[:, 2 * i : 2 * i + 1], chosen[:, 2 * i + 1 : 2 * i + 2])
        row_bias[i] = jnp.where(slash, jnp.broadcast_to(vertical[i : i + 1, :], (32, 128)), pair)
    rev = 511 - offs8[pl.ds(y, 1), :]
    phases = [member_rows(rev + 128 + 64 * phase, 8, subs((8, 128))) for phase in range(2)]
    back = subs((64, 128)) - lanes((64, 128))
    right = lanes((64, 128)) >= 64
    nothing = jnp.full((64, 128), MASKED, F32)
    tile_bias[0] = nothing
    tile_bias[11] = nothing
    for i in range(10):
        start = 576 - 64 * i
        phase = (start // 64) % 2
        first = (start + 64 * phase) // 128
        pair = jnp.concatenate(
            [phases[phase][first : first + 1, :], phases[phase][first + 1 : first + 2, :]], axis=1
        )
        rolled = pltpu.roll(jnp.broadcast_to(pair, (64, 256)), 256 - 63, 1, stride=1, stride_axis=0)
        own = nothing
        if i == 0:
            own = jnp.where(right, MASKED, jnp.where(back >= 0, 0.0, MASKED))
        if i == 1:
            own = jnp.where(right, jnp.where(back + 64 >= 0, 0.0, MASKED), MASKED)
        tile_bias[i + 1] = jnp.where(slash, rolled[:, :128], own)


def layer_kernel(
    q_ref, k_ref, v_ref, w_ref, kind_ref, count_ref, blocks_ref, cols_ref, offs_ref,
    out_ref,
    qv, qt, qs, q2, qf, qb, kvb, wv, blocks, cols8, offs8, row_bias, tile_bias,
    top, total, mixed, o_out, st_out, ob, sb, ab, part, rb, fb, fr,
    in_sem, q1_send, q1_recv, q2_send, q2_recv, qx_send, qx_recv,
    kz_send, kz_recv, ky_send, ky_recv, kc_send, kc_recv,
    w_send, w_recv, wc_send, wc_recv, ox_send, ox_recv,
    a_send, a_recv, z_send, z_recv, f_send, f_recv,
):
    ctx = lax.axis_index("ctx")
    t = lax.axis_index("tp")
    z, x, y, c = ctx // NX, ctx % NX, t // 2, t % 2
    zc = z // 4
    partner = 2 * y + 1 - c
    head = 8 * z + y

    loads = [
        pltpu.make_async_copy(q_ref, qv, in_sem.at[0]),
        pltpu.make_async_copy(blocks_ref, blocks, in_sem.at[1]),
        pltpu.make_async_copy(cols_ref.at[aligned(8 * z, 8)], cols8, in_sem.at[2]),
        pltpu.make_async_copy(offs_ref.at[aligned(8 * z, 8)], offs8, in_sem.at[3]),
    ]
    for copy in loads:
        copy.start()

    barrier = pltpu.get_barrier_semaphore()

    def greet(to_ctx, to_tp):
        pl.semaphore_signal(barrier, inc=1, device_id=(to_ctx, to_tp), device_id_type=MESH)

    for d in range(1, NT):
        greet(ctx, (t + d) % NT)
    for d in range(1, NZ):
        for cc in range(2):
            greet(((z + d) % NZ) * NX + x, 2 * y + cc)
    for d in range(1, NX):
        greet(z * NX + (x + d) % NX, t)

    loads[0].wait()
    for yy in range(NY):
        for g in range(KVH):
            at = (8 * g + yy) * HD
            qt[yy, g] = qv[:, at : at + HD]
    share = 2 * (y % 2) + c
    other = 2 * (1 - y % 2) + c

    def piece(zz, i, s):
        return kvb.at[zz, i, aligned(128 * s, 128)]

    rows = aligned(128 * share, 128)
    for i, ref in enumerate((k_ref, v_ref)):
        own = pltpu.make_async_copy(ref.at[rows, aligned(HD * z, HD)], piece(z, i, share), kz_recv.at[2 * z + i])
        own.start()
    w_own = pltpu.make_async_copy(w_ref, wv.at[aligned(256 * x, 256), aligned(512 * c, 512)], in_sem.at[4])
    w_own.start()

    pl.semaphore_wait(barrier, NT - 1 + 2 * (NZ - 1) + NX - 1)

    q1 = [
        remote(qt.at[(y + d) % NY], qs.at[t], q1_send.at[d], q1_recv, ctx, ((y + d) % NY) * 2 + zc)
        for d in range(NY)
    ]
    for d in range(1, NY):
        q1[d].start()

    @pl.when(zc == c)
    def _():
        pltpu.make_async_copy(qt.at[y], qs.at[t], q1_recv).start()

    @pl.when(zc != c)
    def _():
        q1[0].start()

    kz = []
    for d in (1, 7, 2, 6, 3, 5, 4):
        g = (z + d) % NZ
        for i, ref in enumerate((k_ref, v_ref)):
            copy = remote(
                ref.at[rows, aligned(HD * g, HD)], piece(z, i, share),
                kz_send.at[2 * d + i], kz_recv.at[2 * z + i], g * NX + x, t,
            )
            copy.start()
            kz.append(copy)

    def y_copy(zz, i):
        to = (y + 1) % NY if i == 0 else (y + NY - 1) % NY
        ref = piece(zz, i, share)
        return remote(ref, ref, ky_send.at[2 * zz + i], ky_recv.at[2 * zz + i], ctx, 2 * to + c)

    def core_copy(zz, i, s, n):
        ref = piece(zz, i, s)
        return remote(ref, ref, kc_send.at[4 * zz + 2 * n + i], kc_recv.at[zz], ctx, partner)

    def forward_own(i):
        zz = (z + by_distance(i)) % NZ
        for kv in range(2):
            arrived(piece(zz, kv, share), kz_recv.at[2 * zz + kv])
            y_copy(zz, kv).start()
            core_copy(zz, kv, share, 0).start()

    def forward_other(i):
        zz = (z + by_distance(i)) % NZ
        for kv in range(2):
            arrived(piece(zz, kv, other), ky_recv.at[2 * zz + kv])
            core_copy(zz, kv, other, 1).start()

    forward_own(0)

    def q2_copy(d):
        g = (z + d) % NZ
        return remote(qs.at[:, g], q2.at[z % 4], q2_send.at[d], q2_recv, g * NX + x, t)

    @pl.when(zc == c)
    def _():
        arrived(qs, q1_recv)
        for d in range(1, NZ):
            q2_copy(d).start()
        pltpu.make_async_copy(qs.at[:, z], q2.at[z % 4], q2_recv).start()

    for copy in loads[1:]:
        copy.wait()
    fill_masks(
        kind_ref[head] == 1, count_ref[head], head, x, y, blocks, cols8, offs8, row_bias, tile_bias
    )
    top[...] = jnp.full((NX, 256, 128), MASKED, F32)
    total[...] = jnp.zeros((NX, 256, 128), F32)
    mixed[...] = jnp.zeros((NX, 256, HD), F32)

    forward_own(1)

    arrived(q2, q2_recv)
    for i in range(64):
        qf[4 * i : 4 * i + 4, :] = q2[i // 16, i % 16].astype(F32)
    qb[x] = qf[...].astype(BF16)
    qx = [
        remote(qb.at[x], qb.at[x], qx_send.at[d], qx_recv.at[d], z * NX + (x + d) % NX, t)
        for d in range(1, NX)
    ]
    for copy in qx:
        copy.start()

    def w_view(xx, cc):
        return wv.at[aligned(256 * xx, 256), aligned(512 * cc, 512)]

    wx = [
        remote(w_ref, w_view(x, c), w_send.at[d], w_recv.at[d], z * NX + (x + d) % NX, t)
        for d in range(1, NX)
    ]
    for copy in wx:
        copy.start()
    wc = [remote(w_ref, w_view(x, c), wc_send.at[0], wc_recv, ctx, partner)]
    wc[0].start()

    forward_other(0)
    for d in range(1, NX):
        arrived(qb.at[(x + NX - d) % NX], qx_recv.at[d])

    def chunk(zz, band):
        keys = kvb[zz, 0]
        values = kvb[zz, 1]

        def group(xx, carry):
            s = lax.dot_general(qb[xx], keys, (((1,), (1,)), ((), ())), preferred_element_type=F32)
            weights = []
            factors = []
            for zl in range(4):
                b = 16 * c + 4 * zl + xx
                old = top[xx, 64 * zl : 64 * zl + 64]
                tiles = []
                high = None
                for w in range(4):
                    bias = row_bias[4 * zz + w, pl.ds(b, 1), :]
                    if band:
                        which = 225 + b - 8 * (4 * zz + x) - 2 * w
                        bias = jnp.maximum(bias, tile_bias[jnp.clip(which, 0, 11)])
                    tile = s[64 * zl : 64 * zl + 64, 128 * w : 128 * w + 128] * SCALE + bias
                    high = tile if high is None else jnp.maximum(high, tile)
                    tiles.append(tile)
                new = jnp.maximum(old, jnp.max(high, axis=1, keepdims=True))
                top[xx, 64 * zl : 64 * zl + 64] = new
                factor = jnp.exp2(old - new)
                tiles = [jnp.exp2(tile - new) for tile in tiles]
                total[xx, 64 * zl : 64 * zl + 64] = total[xx, 64 * zl : 64 * zl + 64] * factor + (
                    (tiles[0] + tiles[1]) + (tiles[2] + tiles[3])
                )
                factors.append(factor)
                weights.append(jnp.concatenate([tile.astype(BF16) for tile in tiles], axis=1))
            added = jnp.dot(jnp.concatenate(weights, axis=0), values, preferred_element_type=F32)
            mixed[xx] = mixed[xx] * jnp.concatenate(factors, axis=0) + added
            return carry

        lax.fori_loop(0, NX, group, 0)

    def step(i, carry):
        zz = (z + by_distance(i)) % NZ

        @pl.when(i < NZ - 2)
        def _():
            forward_own(i + 2)

        @pl.when(i < NZ - 1)
        def _():
            forward_other(i + 1)

        arrived(kvb.at[zz, 0], kc_recv.at[zz])

        @pl.when(zz >= 6)
        def _():
            chunk(zz, True)

        @pl.when(zz < 6)
        def _():
            chunk(zz, False)

        return carry

    lax.fori_loop(0, NZ, step, 0)

    ox = []
    for d in (2, 1, 3, 0):
        xx = (x + d) % NX
        amount = jnp.sum(total[xx], axis=1, keepdims=True)
        o_out[xx] = (mixed[xx] / amount).astype(BF16)
        st_out[xx] = (top[xx] + jnp.log2(amount)).T[:8, :]
        if d:
            for i, (src, dst) in enumerate(((st_out, sb), (o_out, ob))):
                copy = remote(
                    src.at[xx], dst.at[d], ox_send.at[2 * d + i], ox_recv.at[2 * d + i], z * NX + xx, t
                )
                copy.start()
                ox.append(copy)
    for d in range(1, NX):
        ref = w_view((x + NX - d) % NX, c)
        arrived(ref, w_recv.at[d])
        copy = remote(ref, ref, wc_send.at[d], wc_recv, ctx, partner)
        copy.start()
        wc.append(copy)
    for d in range(1, NX):
        arrived(sb.at[d], ox_recv.at[2 * d])
    levels = [st_out[x]] + [sb[d] for d in range(1, NX)]
    best = jnp.maximum(jnp.maximum(levels[0], levels[1]), jnp.maximum(levels[2], levels[3]))
    parts = [jnp.exp2(level - best) for level in levels]
    amount = (parts[0] + parts[1]) + (parts[2] + parts[3])
    parts = [p / amount for p in parts]
    table = jnp.concatenate(parts + [jnp.zeros((96, 256), F32)], axis=0).T
    for d in range(1, NX):
        arrived(ob.at[d], ox_recv.at[2 * d + 1])
    joined = table[:, 0:1] * o_out[x].astype(F32)
    for d in range(1, NX):
        joined = joined + table[:, 8 * d : 8 * d + 1] * ob[d].astype(F32)
    joined = joined.astype(BF16)
    for i in range(4):
        ab[i, :, aligned(HD * y, HD)] = joined[64 * i : 64 * i + 64, :]

    def a_copy(i, d):
        ref = ab.at[i, :, aligned(HD * y, HD)]
        return remote(ref, ref, a_send.at[8 * i + d], a_recv.at[i], ctx, 2 * ((y + d) % NY) + c)

    for j in range(4):
        for d in (4, 3, 5, 2, 6, 1, 7):
            a_copy((z + j) % 4, d).start()

    arrived(wv.at[:, pl.ds(0, 512)], wc_recv)
    w_own.wait()

    def z_copy(i, cc):
        return remote(
            part.at[i, cc], rb.at[z], z_send.at[2 * i + cc], z_recv, (4 * c + i) * NX + x, 2 * y + cc
        )

    for j in range(4):
        i = (z + j) % 4
        arrived(ab.at[i, :, pl.ds(0, 896)], a_recv.at[i])
        projected = jnp.dot(ab[i], wv[...], preferred_element_type=F32).astype(BF16)
        for cc in range(2):
            part[i, cc] = projected[:, 512 * cc : 512 * cc + 512]
            mine = jnp.logical_and(4 * c + i == z, cc == c)

            @pl.when(jnp.logical_not(mine))
            def _():
                z_copy(i, cc).start()

            @pl.when(mine)
            def _():
                pltpu.make_async_copy(part.at[i, cc], rb.at[z], z_recv).start()

    arrived(rb, z_recv)
    summed = rb[0].astype(F32)
    for g in range(1, NZ):
        summed = summed + rb[g].astype(F32)
    for tt in range(NT):
        fb[tt] = summed[4 * tt : 4 * tt + 4, :].astype(BF16)
    last = [
        remote(fb.at[(t + d) % NT], fr.at[t], f_send.at[d], f_recv, ctx, (t + d) % NT)
        for d in range(1, NT)
    ]
    for copy in last:
        copy.start()
    pltpu.make_async_copy(fb.at[t], fr.at[t], f_recv).start()

    for copy in q1[1:] + kz + qx + wx + wc + ox:
        copy.wait_send()

    @pl.when(zc != c)
    def _():
        q1[0].wait_send()

    @pl.when(zc == c)
    def _():
        for d in range(1, NZ):
            q2_copy(d).wait_send()

    def sent(zz, carry):
        for kv in range(2):
            y_copy(zz, kv).wait_send()
            core_copy(zz, kv, share, 0).wait_send()
            core_copy(zz, kv, other, 1).wait_send()
        return carry

    lax.fori_loop(0, NZ, sent, 0)
    for i in range(4):
        for d in range(1, NY):
            a_copy(i, d).wait_send()
        for cc in range(2):
            mine = jnp.logical_and(4 * c + i == z, cc == c)

            @pl.when(jnp.logical_not(mine))
            def _():
                z_copy(i, cc).wait_send()

    arrived(fr, f_recv)
    for tt in range(NT):
        out_ref[:, 512 * tt : 512 * tt + 512] = fr[tt]
    for copy in last:
        copy.wait_send()


def layer(q, k, v, w, kinds, counts, blocks, cols, offs):
    dma = pltpu.SemaphoreType.DMA
    hbm = pl.BlockSpec(memory_space=pltpu.HBM)
    smem = pl.BlockSpec(memory_space=pltpu.SMEM)
    vmem = pltpu.VMEM
    return pl.pallas_call(
        layer_kernel,
        out_shape=jax.ShapeDtypeStruct((4, 8192), BF16),
        in_specs=[hbm, hbm, hbm, hbm, smem, smem, hbm, hbm, hbm],
        out_specs=pl.BlockSpec(memory_space=pltpu.VMEM),
        scratch_shapes=[
            vmem((4, 8192), BF16),
            vmem((NY, KVH, 4, HD), BF16),
            vmem((NT, KVH, 4, HD), BF16),
            vmem((4, NT, 4, HD), BF16),
            vmem((256, HD), F32),
            vmem((NX, 256, HD), BF16),
            vmem((NZ, 2, 512, HD), BF16),
            vmem((1024, 1024), BF16),
            vmem((32, 16, H), jnp.int32),
            vmem((8, 1024), jnp.int32),
            vmem((8, 128), jnp.int32),
            vmem((32, 32, 128), F32),
            vmem((12, 64, 128), F32),
            vmem((NX, 256, 128), F32),
            vmem((NX, 256, 128), F32),
            vmem((NX, 256, HD), F32),
            vmem((NX, 256, HD), BF16),
            vmem((NX, 8, 256), F32),
            vmem((NX, 256, HD), BF16),
            vmem((NX, 8, 256), F32),
            vmem((4, 64, 1024), BF16),
            vmem((4, 2, 64, 512), BF16),
            vmem((NZ, 64, 512), BF16),
            vmem((NT, 4, 512), BF16),
            vmem((NT, 4, 512), BF16),
            dma((5,)),
            dma((8,)), dma, dma((8,)), dma, dma((4,)), dma((4,)),
            dma((16,)), dma((16,)), dma((16,)), dma((16,)), dma((32,)), dma((8,)),
            dma((4,)), dma((4,)), dma((4,)), dma, dma((8,)), dma((8,)),
            dma((32,)), dma((4,)), dma((8,)), dma, dma((16,)), dma,
        ],
        compiler_params=pltpu.CompilerParams(
            collective_id=0, has_side_effects=True, vmem_limit_bytes=56 * 1024 * 1024
        ),
        name="layer",
    )(q, k, v, w, kinds, counts, blocks, cols, offs)


def shards(q, k, v, w, kinds, counts, blocks, cols, offs):
    return layer(q, k, v, w, kinds, counts, blocks.transpose(1, 2, 0), cols, offs)


def solution(mesh):
    return jax.shard_map(
        shards,
        mesh=mesh,
        in_specs=(
            P(("ctx", "tp"), None),
            P("ctx", None),
            P("ctx", None),
            P("ctx", "tp"),
            P(),
            P(),
            P(),
            P(),
            P(),
        ),
        out_specs=P(("ctx", "tp"), None),
        check_vma=False,
    )
```

```python
import math

import jax
import jax.numpy as jnp
from jax import lax
from jax.experimental import pallas as pl
from jax.experimental.pallas import tpu as pltpu
from jax.sharding import PartitionSpec as P

H = 64
KVH = 8
HD = 128
NX, NZ, NY = 4, 8, 8
NT = 2 * NY
MASKED = -1e30
MESH = pl.DeviceIdType.MESH
F32 = jnp.float32
BF16 = jnp.bfloat16
SCALE = math.log2(math.e) / math.sqrt(HD)


def remote(src, dst, send_sem, recv_sem, ctx, tp):
    return pltpu.make_async_remote_copy(
        src_ref=src,
        dst_ref=dst,
        send_sem=send_sem,
        recv_sem=recv_sem,
        device_id=(ctx, tp),
        device_id_type=MESH,
    )


def arrived(ref, sem):
    pltpu.make_async_copy(ref, ref, sem).wait()


def lanes(shape):
    return lax.broadcasted_iota(jnp.int32, shape, len(shape) - 1)


def subs(shape):
    return lax.broadcasted_iota(jnp.int32, shape, 0)


def aligned(start, size):
    return pl.ds(pl.multiple_of(start, size), size)


def by_distance(i):
    odd = i % 2
    return odd * ((i + 1) // 2) + (1 - odd) * ((8 - i // 2) % 8)


def member_rows(values, first_row):
    high = jnp.where(values // 128 == first_row, 1.0, 0.0).astype(BF16)
    low = jnp.where(values % 128 == subs((128, values.shape[1])), 1.0, 0.0).astype(BF16)
    found = lax.dot_general(high, low, (((1,), (1,)), ((), ())), preferred_element_type=F32)
    return jnp.where(found > 0.5, 0.0, MASKED)


def fill_masks(slash, count, head, x, y, blocks, cols8, offs8, row_bias, tile_bias):
    tile = subs((32, 1024))
    tile = 16 * (tile // 4) + 4 * x + tile % 4
    vertical = member_rows(cols8[pl.ds(y, 1), :], tile)
    ids = jnp.where(lanes((32, 16, H)) == head, blocks[...].astype(F32), 0.0)
    ids = jnp.sum(ids, axis=2, keepdims=True)
    at = lanes((1, 1, 128))
    block = (8 * (4 * (at // 8) + x) + at % 8).astype(F32)
    turn = lax.broadcasted_iota(jnp.int32, (32, 16, 128), 1)
    hit = jnp.where(ids == block, 0.0, MASKED)
    hit = jnp.where(turn >= 1, jnp.where(turn < count, hit, MASKED), MASKED)
    chosen = jnp.max(hit, axis=1)
    left = lanes((32, 128)) < 64
    for i in range(32):
        pair = jnp.where(left, chosen[:, 2 * i : 2 * i + 1], chosen[:, 2 * i + 1 : 2 * i + 2])
        row_bias[i] = jnp.where(slash, jnp.broadcast_to(vertical[i : i + 1, :], (32, 128)), pair)
    rev = 511 - offs8[pl.ds(y, 1), :]
    phases = [member_rows(rev + 128 + 64 * phase, subs((8, 128))) for phase in range(2)]
    back = subs((64, 128)) - lanes((64, 128))
    right = lanes((64, 128)) >= 64
    nothing = jnp.full((64, 128), MASKED, F32)
    tile_bias[0] = nothing
    tile_bias[11] = nothing
    for i in range(10):
        start = 576 - 64 * i
        phase = (start // 64) % 2
        first = (start + 64 * phase) // 128
        pair = jnp.concatenate(
            [phases[phase][first : first + 1, :], phases[phase][first + 1 : first + 2, :]], axis=1
        )
        rolled = pltpu.roll(jnp.broadcast_to(pair, (64, 256)), 256 - 63, 1, stride=1, stride_axis=0)
        own = nothing
        if i == 0:
            own = jnp.where(right, MASKED, jnp.where(back >= 0, 0.0, MASKED))
        if i == 1:
            own = jnp.where(right, jnp.where(back + 64 >= 0, 0.0, MASKED), MASKED)
        tile_bias[i + 1] = jnp.where(slash, rolled[:, :128], own)


def layer_kernel(
    q_ref, k_ref, v_ref, w_ref, kind_ref, count_ref, blocks_ref, cols_ref, offs_ref,
    out_ref,
    qv, qt, qs, qy, q4, qf, qb, kl, kvb, wv, blocks, cols8, offs8, row_bias, tile_bias,
    top, total, mixed, o_out, st_out, ob, sb, ab, part, rb, fb, fr,
    in_sem, q1_send, q1_recv, q2_send, q2_recv, qx_send, qx_recv,
    kz_send, kz_recv, ky_send, ky_recv, kc_send, kc_recv,
    w_send, w_recv, wc_send, wc_recv, ox_send, ox_recv,
    a_send, a_recv, z_send, z_recv, f_send, f_recv,
):
    ctx = lax.axis_index("ctx")
    t = lax.axis_index("tp")
    z, x, y, c = ctx // NX, ctx % NX, t // 2, t % 2
    partner = 2 * y + 1 - c
    head = 8 * z + y

    loads = [
        pltpu.make_async_copy(q_ref, qv, in_sem.at[0]),
        pltpu.make_async_copy(blocks_ref, blocks, in_sem.at[1]),
        pltpu.make_async_copy(cols_ref.at[aligned(8 * z, 8)], cols8, in_sem.at[2]),
        pltpu.make_async_copy(offs_ref.at[aligned(8 * z, 8)], offs8, in_sem.at[3]),
    ]
    for copy in loads:
        copy.start()

    barrier = pltpu.get_barrier_semaphore()

    def greet(to_ctx, to_tp):
        pl.semaphore_signal(barrier, inc=1, device_id=(to_ctx, to_tp), device_id_type=MESH)

    for d in range(1, NT):
        greet(ctx, (t + d) % NT)
    for d in range(1, NZ):
        for cc in range(2):
            greet(((z + d) % NZ) * NX + x, 2 * y + cc)
    for d in range(1, NX):
        greet(z * NX + (x + d) % NX, t)

    loads[0].wait()
    for yy in range(NY):
        for g in range(KVH):
            at = (8 * g + yy) * HD
            qt[g, yy] = qv[:, at : at + HD]
    share = 2 * (y % 2) + c
    other = 2 * (1 - y % 2) + c

    def piece(zz, i, s):
        return kvb.at[zz, i, aligned(128 * s, 128)]

    rows = aligned(128 * share, 128)
    dense = []
    for i, ref in enumerate((k_ref, v_ref)):
        pltpu.make_async_copy(
            ref.at[rows, aligned(HD * z, HD)], piece(z, i, share), kz_recv.at[2 * z + i]
        ).start()
        for d in range(1, NZ):
            cols = aligned(HD * ((z + d) % NZ), HD)
            dense.append(pltpu.make_async_copy(ref.at[rows, cols], kl.at[i, d], in_sem.at[5 + 8 * i + d]))
            dense[-1].start()
    w_own = pltpu.make_async_copy(w_ref, wv.at[c, x], in_sem.at[4])
    w_own.start()

    for copy in dense:
        copy.wait()
    pl.semaphore_wait(barrier, NT - 1 + 2 * (NZ - 1) + NX - 1)

    q1 = [
        remote(qt.at[(z + d) % NZ], qs.at[z], q1_send.at[d], q1_recv, ((z + d) % NZ) * NX + x, t)
        for d in range(1, NZ)
    ]
    for copy in q1:
        copy.start()
    pltpu.make_async_copy(qt.at[z], qs.at[z], q1_recv).start()

    kz = []
    for d in (1, 7, 2, 6, 3, 5, 4):
        g = (z + d) % NZ
        for i in range(2):
            copy = remote(
                kl.at[i, d], piece(z, i, share),
                kz_send.at[2 * d + i], kz_recv.at[2 * z + i], g * NX + x, t,
            )
            copy.start()
            kz.append(copy)

    def y_copy(zz, i):
        to = (y + 1) % NY if i == 0 else (y + NY - 1) % NY
        ref = piece(zz, i, share)
        return remote(ref, ref, ky_send.at[2 * zz + i], ky_recv.at[2 * zz + i], ctx, 2 * to + c)

    def core_copy(zz, i, s, n):
        ref = piece(zz, i, s)
        return remote(ref, ref, kc_send.at[4 * zz + 2 * n + i], kc_recv.at[zz], ctx, partner)

    def forward_own(i):
        zz = (z + by_distance(i)) % NZ
        for kv in range(2):
            arrived(piece(zz, kv, share), kz_recv.at[2 * zz + kv])
            y_copy(zz, kv).start()
            core_copy(zz, kv, share, 0).start()

    def forward_other(i):
        zz = (z + by_distance(i)) % NZ
        for kv in range(2):
            arrived(piece(zz, kv, other), ky_recv.at[2 * zz + kv])
            core_copy(zz, kv, other, 1).start()

    forward_own(0)

    for copy in loads[1:]:
        copy.wait()
    fill_masks(
        kind_ref[head] == 1, count_ref[head], head, x, y, blocks, cols8, offs8, row_bias, tile_bias
    )
    top[...] = jnp.full((NX, 256, 128), MASKED, F32)
    total[...] = jnp.zeros((NX, 256, 128), F32)
    mixed[...] = jnp.zeros((NX, 256, HD), F32)

    arrived(qs, q1_recv)
    for yy in range(NY):
        for zz in range(NZ):
            qy[yy, zz] = qs[zz, yy]
    q2 = []
    for d in range(1, NT):
        tt = (t + d) % NT
        src = qy.at[tt // 2, pl.ds(4 * (tt % 2), 4)]
        q2.append(remote(src, q4.at[t], q2_send.at[d], q2_recv, ctx, tt))
        q2[-1].start()
    pltpu.make_async_copy(qy.at[y, pl.ds(4 * c, 4)], q4.at[t], q2_recv).start()

    forward_own(1)
    forward_own(2)
    forward_other(0)

    arrived(q4, q2_recv)
    for zl in range(4):
        for tt in range(NT):
            qf[zl, 4 * tt : 4 * tt + 4, :] = q4[tt, zl].astype(F32)
    qb[x] = qf[...].astype(BF16)
    qx = [
        remote(qb.at[x], qb.at[x], qx_send.at[d], qx_recv.at[d], z * NX + (x + d) % NX, t)
        for d in range(1, NX)
    ]
    for copy in qx:
        copy.start()

    wx = [
        remote(w_ref, wv.at[c, x], w_send.at[d], w_recv.at[d], z * NX + (x + d) % NX, t)
        for d in range(1, NX)
    ]
    for copy in wx:
        copy.start()
    wc = [remote(w_ref, wv.at[c, x], wc_send.at[0], wc_recv, ctx, partner)]
    wc[0].start()

    for i in range(3, 7):
        forward_own(i)
        forward_other(i - 2)
    for d in range(1, NX):
        arrived(qb.at[(x + NX - d) % NX], qx_recv.at[d])
    forward_own(7)

    def chunk(zz, band):
        keys = kvb[zz, 0]
        values = kvb[zz, 1]

        queries = qb[...].reshape(1024, HD)
        s = lax.dot_general(queries, keys, (((1,), (1,)), ((), ())), preferred_element_type=F32)
        weights = []
        factors = []
        for n in range(16):
            xx, zl = n // 4, n % 4
            b = 16 * c + 4 * zl + xx
            old = top[xx, 64 * zl : 64 * zl + 64]
            tiles = []
            high = None
            for w in range(4):
                bias = row_bias[4 * zz + w, pl.ds(b, 1), :]
                if band:
                    which = 225 + b - 8 * (4 * zz + x) - 2 * w
                    bias = jnp.maximum(bias, tile_bias[jnp.clip(which, 0, 11)])
                tile = s[64 * n : 64 * n + 64, 128 * w : 128 * w + 128] * SCALE + bias
                high = tile if high is None else jnp.maximum(high, tile)
                tiles.append(tile)
            new = jnp.maximum(old, jnp.max(high, axis=1, keepdims=True))
            top[xx, 64 * zl : 64 * zl + 64] = new
            factor = jnp.exp2(old - new)
            tiles = [jnp.exp2(tile - new) for tile in tiles]
            total[xx, 64 * zl : 64 * zl + 64] = total[xx, 64 * zl : 64 * zl + 64] * factor + (
                (tiles[0] + tiles[1]) + (tiles[2] + tiles[3])
            )
            factors.append(factor)
            weights.append(jnp.concatenate([tile.astype(BF16) for tile in tiles], axis=1))
        added = jnp.dot(jnp.concatenate(weights, axis=0), values, preferred_element_type=F32)
        for n in range(16):
            at = (n // 4, pl.ds(64 * (n % 4), 64))
            mixed[at] = mixed[at] * factors[n] + added[64 * n : 64 * n + 64]

    def step(i, carry):
        zz = (z + by_distance(i)) % NZ

        @pl.when(i < NZ - 5)
        def _():
            forward_other(i + 5)

        arrived(kvb.at[zz, 0], kc_recv.at[zz])

        @pl.when(zz >= 6)
        def _():
            chunk(zz, True)

        @pl.when(zz < 6)
        def _():
            chunk(zz, False)

        return carry

    lax.fori_loop(0, NZ, step, 0)

    ox = []
    for d in (2, 1, 3, 0):
        xx = (x + d) % NX
        amount = jnp.sum(total[xx], axis=1, keepdims=True)
        o_out[xx] = (mixed[xx] / amount).astype(BF16)
        st_out[xx] = (top[xx] + jnp.log2(amount)).T[:8, :]
        if d:
            for i, (src, dst) in enumerate(((st_out, sb), (o_out, ob))):
                copy = remote(
                    src.at[xx], dst.at[d], ox_send.at[2 * d + i], ox_recv.at[2 * d + i], z * NX + xx, t
                )
                copy.start()
                ox.append(copy)
    for d in range(1, NX):
        ref = wv.at[c, (x + NX - d) % NX]
        arrived(ref, w_recv.at[d])
        copy = remote(ref, ref, wc_send.at[d], wc_recv, ctx, partner)
        copy.start()
        wc.append(copy)
    for d in range(1, NX):
        arrived(sb.at[d], ox_recv.at[2 * d])
    levels = [st_out[x]] + [sb[d] for d in range(1, NX)]
    best = jnp.maximum(jnp.maximum(levels[0], levels[1]), jnp.maximum(levels[2], levels[3]))
    parts = [jnp.exp2(level - best) for level in levels]
    amount = (parts[0] + parts[1]) + (parts[2] + parts[3])
    parts = [p / amount for p in parts]
    table = jnp.concatenate(parts + [jnp.zeros((96, 256), F32)], axis=0).T
    for d in range(1, NX):
        arrived(ob.at[d], ox_recv.at[2 * d + 1])
    joined = table[:, 0:1] * o_out[x].astype(F32)
    for d in range(1, NX):
        joined = joined + table[:, 8 * d : 8 * d + 1] * ob[d].astype(F32)
    joined = joined.astype(BF16)
    for i in range(4):
        ab[i, y] = joined[64 * i : 64 * i + 64, :]

    def a_copy(i, d):
        ref = ab.at[i, y]
        return remote(ref, ref, a_send.at[8 * i + d], a_recv.at[i], ctx, 2 * ((y + d) % NY) + c)

    for j in range(4):
        for d in (4, 3, 5, 2, 6, 1, 7):
            a_copy((z + j) % 4, d).start()

    arrived(wv.at[0], wc_recv)
    w_own.wait()

    def z_copy(i, cc):
        return remote(
            part.at[i, cc], rb.at[z], z_send.at[2 * i + cc], z_recv, (4 * c + i) * NX + x, 2 * y + cc
        )

    for j in range(4):
        i = (z + j) % 4
        arrived(ab.at[i, pl.ds(0, NY - 1)], a_recv.at[i])
        features = jnp.concatenate([ab[i, yy] for yy in range(NY)], axis=1)
        for cc in range(2):
            weight = wv[cc].reshape(1024, 512)
            part[i, cc] = jnp.dot(features, weight, preferred_element_type=F32).astype(BF16)
            mine = jnp.logical_and(4 * c + i == z, cc == c)

            @pl.when(jnp.logical_not(mine))
            def _():
                z_copy(i, cc).start()

            @pl.when(mine)
            def _():
                pltpu.make_async_copy(part.at[i, cc], rb.at[z], z_recv).start()

    arrived(rb, z_recv)
    summed = rb[0].astype(F32)
    for g in range(1, NZ):
        summed = summed + rb[g].astype(F32)
    for tt in range(NT):
        fb[tt] = summed[4 * tt : 4 * tt + 4, :].astype(BF16)
    last = [
        remote(fb.at[(t + d) % NT], fr.at[t], f_send.at[d], f_recv, ctx, (t + d) % NT)
        for d in range(1, NT)
    ]
    for copy in last:
        copy.start()
    pltpu.make_async_copy(fb.at[t], fr.at[t], f_recv).start()

    for copy in q1 + q2 + kz + qx + wx + wc + ox:
        copy.wait_send()

    def sent(zz, carry):
        for kv in range(2):
            y_copy(zz, kv).wait_send()
            core_copy(zz, kv, share, 0).wait_send()
            core_copy(zz, kv, other, 1).wait_send()
        return carry

    lax.fori_loop(0, NZ, sent, 0)
    for i in range(4):
        for d in range(1, NY):
            a_copy(i, d).wait_send()
        for cc in range(2):
            mine = jnp.logical_and(4 * c + i == z, cc == c)

            @pl.when(jnp.logical_not(mine))
            def _():
                z_copy(i, cc).wait_send()

    arrived(fr, f_recv)
    for tt in range(NT):
        out_ref[:, 512 * tt : 512 * tt + 512] = fr[tt]
    for copy in last:
        copy.wait_send()


def layer(q, k, v, w, kinds, counts, blocks, cols, offs):
    dma = pltpu.SemaphoreType.DMA
    hbm = pl.BlockSpec(memory_space=pltpu.HBM)
    smem = pl.BlockSpec(memory_space=pltpu.SMEM)
    vmem = pltpu.VMEM
    return pl.pallas_call(
        layer_kernel,
        out_shape=jax.ShapeDtypeStruct((4, 8192), BF16),
        in_specs=[hbm, hbm, hbm, hbm, smem, smem, hbm, hbm, hbm],
        out_specs=pl.BlockSpec(memory_space=pltpu.VMEM),
        scratch_shapes=[
            vmem((4, 8192), BF16),
            vmem((KVH, NY, 4, HD), BF16),
            vmem((NZ, NY, 4, HD), BF16),
            vmem((NY, NZ, 4, HD), BF16),
            vmem((NT, 4, 4, HD), BF16),
            vmem((4, 64, HD), F32),
            vmem((NX, 4, 64, HD), BF16),
            vmem((2, NZ, 128, HD), BF16),
            vmem((NZ, 2, 512, HD), BF16),
            vmem((2, NX, 256, 512), BF16),
            vmem((32, 16, H), jnp.int32),
            vmem((8, 1024), jnp.int32),
            vmem((8, 128), jnp.int32),
            vmem((32, 32, 128), F32),
            vmem((12, 64, 128), F32),
            vmem((NX, 256, 128), F32),
            vmem((NX, 256, 128), F32),
            vmem((NX, 256, HD), F32),
            vmem((NX, 256, HD), BF16),
            vmem((NX, 8, 256), F32),
            vmem((NX, 256, HD), BF16),
            vmem((NX, 8, 256), F32),
            vmem((4, NY, 64, HD), BF16),
            vmem((4, 2, 64, 512), BF16),
            vmem((NZ, 64, 512), BF16),
            vmem((NT, 4, 512), BF16),
            vmem((NT, 4, 512), BF16),
            dma((21,)),
            dma((8,)), dma, dma((16,)), dma, dma((4,)), dma((4,)),
            dma((16,)), dma((16,)), dma((16,)), dma((16,)), dma((32,)), dma((8,)),
            dma((4,)), dma((4,)), dma((4,)), dma, dma((8,)), dma((8,)),
            dma((32,)), dma((4,)), dma((8,)), dma, dma((16,)), dma,
        ],
        compiler_params=pltpu.CompilerParams(
            collective_id=0, has_side_effects=True, vmem_limit_bytes=56 * 1024 * 1024
        ),
        name="layer",
    )(q, k, v, w, kinds, counts, blocks, cols, offs)


def shards(q, k, v, w, kinds, counts, blocks, cols, offs):
    return layer(q, k, v, w, kinds, counts, blocks.transpose(1, 2, 0), cols, offs)


def solution(mesh):
    return jax.shard_map(
        shards,
        mesh=mesh,
        in_specs=(
            P(("ctx", "tp"), None),
            P("ctx", None),
            P("ctx", None),
            P("ctx", "tp"),
            P(),
            P(),
            P(),
            P(),
            P(),
        ),
        out_specs=P(("ctx", "tp"), None),
        check_vma=False,
    )
```

```python
import math

import jax
import jax.numpy as jnp
from jax import lax
from jax.experimental import pallas as pl
from jax.experimental.pallas import tpu as pltpu
from jax.sharding import PartitionSpec as P

H = 64
KVH = 8
HD = 128
NX, NZ, NY = 4, 8, 8
NT = 2 * NY
MASKED = -1e30
MESH = pl.DeviceIdType.MESH
F32 = jnp.float32
BF16 = jnp.bfloat16
SCALE = math.log2(math.e) / math.sqrt(HD)


def remote(src, dst, send_sem, recv_sem, ctx, tp):
    return pltpu.make_async_remote_copy(
        src_ref=src,
        dst_ref=dst,
        send_sem=send_sem,
        recv_sem=recv_sem,
        device_id=(ctx, tp),
        device_id_type=MESH,
    )


def arrived(ref, sem):
    pltpu.make_async_copy(ref, ref, sem).wait()


def lanes(shape):
    return lax.broadcasted_iota(jnp.int32, shape, len(shape) - 1)


def subs(shape):
    return lax.broadcasted_iota(jnp.int32, shape, 0)


def aligned(start, size):
    return pl.ds(pl.multiple_of(start, size), size)


def by_distance(i):
    odd = i % 2
    return odd * ((i + 1) // 2) + (1 - odd) * ((8 - i // 2) % 8)


def member_rows(values, first_row):
    high = jnp.where(values // 128 == first_row, 1.0, 0.0).astype(BF16)
    low = jnp.where(values % 128 == subs((128, values.shape[1])), 1.0, 0.0).astype(BF16)
    found = lax.dot_general(high, low, (((1,), (1,)), ((), ())), preferred_element_type=F32)
    return jnp.where(found > 0.5, 0.0, MASKED)


def fill_masks(slash, count, head, x, y, blocks, cols8, offs8, row_bias, tile_bias):
    tile = subs((32, 1024))
    tile = 16 * (tile // 4) + 4 * x + tile % 4
    vertical = member_rows(cols8[pl.ds(y, 1), :], tile)
    ids = jnp.where(lanes((32, 16, H)) == head, blocks[...].astype(F32), 0.0)
    ids = jnp.sum(ids, axis=2, keepdims=True)
    at = lanes((1, 1, 128))
    block = (8 * (4 * (at // 8) + x) + at % 8).astype(F32)
    turn = lax.broadcasted_iota(jnp.int32, (32, 16, 128), 1)
    hit = jnp.where(ids == block, 0.0, MASKED)
    hit = jnp.where(turn >= 1, jnp.where(turn < count, hit, MASKED), MASKED)
    chosen = jnp.max(hit, axis=1)
    left = lanes((32, 128)) < 64
    for i in range(32):
        pair = jnp.where(left, chosen[:, 2 * i : 2 * i + 1], chosen[:, 2 * i + 1 : 2 * i + 2])
        row_bias[i] = jnp.where(slash, jnp.broadcast_to(vertical[i : i + 1, :], (32, 128)), pair)
    rev = 511 - offs8[pl.ds(y, 1), :]
    phases = [member_rows(rev + 128 + 64 * phase, subs((8, 128))) for phase in range(2)]
    back = subs((64, 128)) - lanes((64, 128))
    right = lanes((64, 128)) >= 64
    nothing = jnp.full((64, 128), MASKED, F32)
    tile_bias[0] = nothing
    tile_bias[11] = nothing
    for i in range(10):
        start = 576 - 64 * i
        phase = (start // 64) % 2
        first = (start + 64 * phase) // 128
        pair = jnp.concatenate(
            [phases[phase][first : first + 1, :], phases[phase][first + 1 : first + 2, :]], axis=1
        )
        rolled = pltpu.roll(jnp.broadcast_to(pair, (64, 256)), 256 - 63, 1, stride=1, stride_axis=0)
        own = nothing
        if i == 0:
            own = jnp.where(right, MASKED, jnp.where(back >= 0, 0.0, MASKED))
        if i == 1:
            own = jnp.where(right, jnp.where(back + 64 >= 0, 0.0, MASKED), MASKED)
        tile_bias[i + 1] = jnp.where(slash, rolled[:, :128], own)


def layer_kernel(
    q_ref, k_ref, v_ref, w_ref, kind_ref, count_ref, blocks_ref, cols_ref, offs_ref,
    out_ref,
    qv, qt, qs, qy, q4, qf, qb, kl, kvb, wv, blocks, cols8, offs8, row_bias, tile_bias,
    top, total, mixed, o_out, st_out, ob, sb, ab, part, rb, fb, fr,
    in_sem, q1_send, q1_recv, q2_send, q2_recv, qx_send, qx_recv,
    kz_send, kz_recv, ky_send, ky_recv, kc_send, kc_recv,
    w_send, w_recv, wc_send, wc_recv, ox_send, ox_recv,
    a_send, a_recv, z_send, z_recv, f_send, f_recv,
):
    ctx = lax.axis_index("ctx")
    t = lax.axis_index("tp")
    z, x, y, c = ctx // NX, ctx % NX, t // 2, t % 2
    partner = 2 * y + 1 - c
    head = 8 * z + y

    loads = [
        pltpu.make_async_copy(q_ref, qv, in_sem.at[0]),
        pltpu.make_async_copy(blocks_ref, blocks, in_sem.at[1]),
        pltpu.make_async_copy(cols_ref.at[aligned(8 * z, 8)], cols8, in_sem.at[2]),
        pltpu.make_async_copy(offs_ref.at[aligned(8 * z, 8)], offs8, in_sem.at[3]),
    ]
    for copy in loads:
        copy.start()

    barrier = pltpu.get_barrier_semaphore()

    def greet(to_ctx, to_tp):
        pl.semaphore_signal(barrier, inc=1, device_id=(to_ctx, to_tp), device_id_type=MESH)

    for d in range(1, NT):
        greet(ctx, (t + d) % NT)
    for d in range(1, NZ):
        for cc in range(2):
            greet(((z + d) % NZ) * NX + x, 2 * y + cc)
    for d in range(1, NX):
        greet(z * NX + (x + d) % NX, t)

    loads[0].wait()
    for yy in range(NY):
        for g in range(KVH):
            at = (8 * g + yy) * HD
            qt[g, yy] = qv[:, at : at + HD]
    share = 2 * (y % 2) + c
    other = 2 * (1 - y % 2) + c

    def piece(zz, i, s):
        return kvb.at[zz, i, aligned(128 * s, 128)]

    rows = aligned(128 * share, 128)
    dense = []
    for i, ref in enumerate((k_ref, v_ref)):
        pltpu.make_async_copy(
            ref.at[rows, aligned(HD * z, HD)], piece(z, i, share), kz_recv.at[2 * z + i]
        ).start()
        for d in range(1, NZ):
            cols = aligned(HD * ((z + d) % NZ), HD)
            dense.append(pltpu.make_async_copy(ref.at[rows, cols], kl.at[i, d], in_sem.at[5 + 8 * i + d]))
            dense[-1].start()
    w_own = pltpu.make_async_copy(w_ref, wv.at[c, x], in_sem.at[4])
    w_own.start()

    for copy in dense:
        copy.wait()
    pl.semaphore_wait(barrier, NT - 1 + 2 * (NZ - 1) + NX - 1)

    q1 = [
        remote(qt.at[(z + d) % NZ], qs.at[z], q1_send.at[d], q1_recv, ((z + d) % NZ) * NX + x, t)
        for d in range(1, NZ)
    ]
    for copy in q1:
        copy.start()
    pltpu.make_async_copy(qt.at[z], qs.at[z], q1_recv).start()

    kz = []
    for d in (1, 7, 2, 6, 3, 5, 4):
        g = (z + d) % NZ
        for i in range(2):
            copy = remote(
                kl.at[i, d], piece(z, i, share),
                kz_send.at[2 * d + i], kz_recv.at[2 * z + i], g * NX + x, t,
            )
            copy.start()
            kz.append(copy)

    wx = [
        remote(w_ref, wv.at[c, x], w_send.at[d], w_recv.at[d], z * NX + (x + d) % NX, t)
        for d in range(1, NX)
    ]
    for copy in wx:
        copy.start()
    wc = [remote(w_ref, wv.at[c, x], wc_send.at[0], wc_recv, ctx, partner)]
    wc[0].start()

    def y_copy(zz, i):
        to = (y + 1) % NY if i == 0 else (y + NY - 1) % NY
        ref = piece(zz, i, share)
        return remote(ref, ref, ky_send.at[2 * zz + i], ky_recv.at[2 * zz + i], ctx, 2 * to + c)

    def core_copy(zz, i, s, n):
        ref = piece(zz, i, s)
        return remote(ref, ref, kc_send.at[4 * zz + 2 * n + i], kc_recv.at[zz], ctx, partner)

    def forward_own(i):
        zz = (z + by_distance(i)) % NZ
        for kv in range(2):
            arrived(piece(zz, kv, share), kz_recv.at[2 * zz + kv])
            y_copy(zz, kv).start()
            core_copy(zz, kv, share, 0).start()

    def forward_other(i):
        zz = (z + by_distance(i)) % NZ
        for kv in range(2):
            arrived(piece(zz, kv, other), ky_recv.at[2 * zz + kv])
            core_copy(zz, kv, other, 1).start()

    forward_own(0)

    for copy in loads[1:]:
        copy.wait()
    fill_masks(
        kind_ref[head] == 1, count_ref[head], head, x, y, blocks, cols8, offs8, row_bias, tile_bias
    )
    top[...] = jnp.full((NX, 256, 128), MASKED, F32)
    total[...] = jnp.zeros((NX, 256, 128), F32)
    mixed[...] = jnp.zeros((NX, 256, HD), F32)

    arrived(qs, q1_recv)
    for yy in range(NY):
        for zz in range(NZ):
            qy[yy, zz] = qs[zz, yy]
    q2 = []
    for d in range(1, NT):
        tt = (t + d) % NT
        src = qy.at[tt // 2, pl.ds(4 * (tt % 2), 4)]
        q2.append(remote(src, q4.at[t], q2_send.at[d], q2_recv, ctx, tt))
        q2[-1].start()
    pltpu.make_async_copy(qy.at[y, pl.ds(4 * c, 4)], q4.at[t], q2_recv).start()

    forward_own(1)
    forward_own(2)
    forward_other(0)

    arrived(q4, q2_recv)
    for zl in range(4):
        for tt in range(NT):
            qf[zl, 4 * tt : 4 * tt + 4, :] = q4[tt, zl].astype(F32)
    qb[x] = qf[...].astype(BF16)
    qx = [
        remote(qb.at[x], qb.at[x], qx_send.at[d], qx_recv.at[d], z * NX + (x + d) % NX, t)
        for d in range(1, NX)
    ]
    for copy in qx:
        copy.start()

    for i in range(3, 7):
        forward_own(i)
        forward_other(i - 2)
    for d in range(1, NX):
        arrived(qb.at[(x + NX - d) % NX], qx_recv.at[d])
    forward_own(7)

    def chunk(zz, band):
        keys = kvb[zz, 0]
        values = kvb[zz, 1]

        queries = qb[...].reshape(1024, HD)
        s = lax.dot_general(queries, keys, (((1,), (1,)), ((), ())), preferred_element_type=F32)
        weights = []
        factors = []
        for n in range(16):
            xx, zl = n // 4, n % 4
            b = 16 * c + 4 * zl + xx
            old = top[xx, 64 * zl : 64 * zl + 64]
            tiles = []
            high = None
            for w in range(4):
                bias = row_bias[4 * zz + w, pl.ds(b, 1), :]
                if band:
                    which = 225 + b - 8 * (4 * zz + x) - 2 * w
                    bias = jnp.maximum(bias, tile_bias[jnp.clip(which, 0, 11)])
                tile = s[64 * n : 64 * n + 64, 128 * w : 128 * w + 128] * SCALE + bias
                high = tile if high is None else jnp.maximum(high, tile)
                tiles.append(tile)
            new = jnp.maximum(old, jnp.max(high, axis=1, keepdims=True))
            top[xx, 64 * zl : 64 * zl + 64] = new
            factor = jnp.exp2(old - new)
            tiles = [jnp.exp2(tile - new) for tile in tiles]
            total[xx, 64 * zl : 64 * zl + 64] = total[xx, 64 * zl : 64 * zl + 64] * factor + (
                (tiles[0] + tiles[1]) + (tiles[2] + tiles[3])
            )
            factors.append(factor)
            weights.append(jnp.concatenate([tile.astype(BF16) for tile in tiles], axis=1))
        added = jnp.dot(jnp.concatenate(weights, axis=0), values, preferred_element_type=F32)
        for n in range(16):
            at = (n // 4, pl.ds(64 * (n % 4), 64))
            mixed[at] = mixed[at] * factors[n] + added[64 * n : 64 * n + 64]

    def step(i, carry):
        zz = (z + by_distance(i)) % NZ

        @pl.when(i < NZ - 5)
        def _():
            forward_other(i + 5)

        arrived(kvb.at[zz, 0], kc_recv.at[zz])

        @pl.when(zz >= 6)
        def _():
            chunk(zz, True)

        @pl.when(zz < 6)
        def _():
            chunk(zz, False)

        return carry

    lax.fori_loop(0, NZ, step, 0)

    ox = []
    for d in (2, 1, 3, 0):
        xx = (x + d) % NX
        amount = jnp.sum(total[xx], axis=1, keepdims=True)
        o_out[xx] = (mixed[xx] / amount).astype(BF16)
        st_out[xx] = (top[xx] + jnp.log2(amount)).T[:8, :]
        if d:
            for i, (src, dst) in enumerate(((st_out, sb), (o_out, ob))):
                copy = remote(
                    src.at[xx], dst.at[d], ox_send.at[2 * d + i], ox_recv.at[2 * d + i], z * NX + xx, t
                )
                copy.start()
                ox.append(copy)
    for d in range(1, NX):
        arrived(sb.at[d], ox_recv.at[2 * d])
    levels = [st_out[x]] + [sb[d] for d in range(1, NX)]
    best = jnp.maximum(jnp.maximum(levels[0], levels[1]), jnp.maximum(levels[2], levels[3]))
    parts = [jnp.exp2(level - best) for level in levels]
    amount = (parts[0] + parts[1]) + (parts[2] + parts[3])
    parts = [p / amount for p in parts]
    table = jnp.concatenate(parts + [jnp.zeros((96, 256), F32)], axis=0).T
    for d in range(1, NX):
        arrived(ob.at[d], ox_recv.at[2 * d + 1])
    joined = table[:, 0:1] * o_out[x].astype(F32)
    for d in range(1, NX):
        joined = joined + table[:, 8 * d : 8 * d + 1] * ob[d].astype(F32)
    joined = joined.astype(BF16)
    for i in range(4):
        ab[i, y] = joined[64 * i : 64 * i + 64, :]

    def a_copy(i, d):
        ref = ab.at[i, y]
        return remote(ref, ref, a_send.at[8 * i + d], a_recv.at[i], ctx, 2 * ((y + d) % NY) + c)

    for j in range(4):
        for d in (4, 3, 5, 2, 6, 1, 7):
            a_copy((z + j) % 4, d).start()

    for d in range(1, NX):
        ref = wv.at[c, (x + NX - d) % NX]
        arrived(ref, w_recv.at[d])
        copy = remote(ref, ref, wc_send.at[d], wc_recv, ctx, partner)
        copy.start()
        wc.append(copy)
    arrived(wv.at[0], wc_recv)
    w_own.wait()

    def z_copy(i, cc):
        return remote(
            part.at[i, cc], rb.at[z], z_send.at[2 * i + cc], z_recv, (4 * c + i) * NX + x, 2 * y + cc
        )

    for j in range(4):
        i = (z + j) % 4
        arrived(ab.at[i, pl.ds(0, NY - 1)], a_recv.at[i])
        features = jnp.concatenate([ab[i, yy] for yy in range(NY)], axis=1)
        for cc in range(2):
            weight = wv[cc].reshape(1024, 512)
            part[i, cc] = jnp.dot(features, weight, preferred_element_type=F32).astype(BF16)
            mine = jnp.logical_and(4 * c + i == z, cc == c)

            @pl.when(jnp.logical_not(mine))
            def _():
                z_copy(i, cc).start()

            @pl.when(mine)
            def _():
                pltpu.make_async_copy(part.at[i, cc], rb.at[z], z_recv).start()

    arrived(rb, z_recv)
    summed = rb[0].astype(F32)
    for g in range(1, NZ):
        summed = summed + rb[g].astype(F32)
    for tt in range(NT):
        fb[tt] = summed[4 * tt : 4 * tt + 4, :].astype(BF16)
    last = [
        remote(fb.at[(t + d) % NT], fr.at[t], f_send.at[d], f_recv, ctx, (t + d) % NT)
        for d in range(1, NT)
    ]
    for copy in last:
        copy.start()
    pltpu.make_async_copy(fb.at[t], fr.at[t], f_recv).start()

    for copy in q1 + q2 + kz + qx + wx + wc + ox:
        copy.wait_send()

    def sent(zz, carry):
        for kv in range(2):
            y_copy(zz, kv).wait_send()
            core_copy(zz, kv, share, 0).wait_send()
            core_copy(zz, kv, other, 1).wait_send()
        return carry

    lax.fori_loop(0, NZ, sent, 0)
    for i in range(4):
        for d in range(1, NY):
            a_copy(i, d).wait_send()
        for cc in range(2):
            mine = jnp.logical_and(4 * c + i == z, cc == c)

            @pl.when(jnp.logical_not(mine))
            def _():
                z_copy(i, cc).wait_send()

    arrived(fr, f_recv)
    for tt in range(NT):
        out_ref[:, 512 * tt : 512 * tt + 512] = fr[tt]
    for copy in last:
        copy.wait_send()


def layer(q, k, v, w, kinds, counts, blocks, cols, offs):
    dma = pltpu.SemaphoreType.DMA
    hbm = pl.BlockSpec(memory_space=pltpu.HBM)
    smem = pl.BlockSpec(memory_space=pltpu.SMEM)
    vmem = pltpu.VMEM
    return pl.pallas_call(
        layer_kernel,
        out_shape=jax.ShapeDtypeStruct((4, 8192), BF16),
        in_specs=[hbm, hbm, hbm, hbm, smem, smem, hbm, hbm, hbm],
        out_specs=pl.BlockSpec(memory_space=pltpu.VMEM),
        scratch_shapes=[
            vmem((4, 8192), BF16),
            vmem((KVH, NY, 4, HD), BF16),
            vmem((NZ, NY, 4, HD), BF16),
            vmem((NY, NZ, 4, HD), BF16),
            vmem((NT, 4, 4, HD), BF16),
            vmem((4, 64, HD), F32),
            vmem((NX, 4, 64, HD), BF16),
            vmem((2, NZ, 128, HD), BF16),
            vmem((NZ, 2, 512, HD), BF16),
            vmem((2, NX, 256, 512), BF16),
            vmem((32, 16, H), jnp.int32),
            vmem((8, 1024), jnp.int32),
            vmem((8, 128), jnp.int32),
            vmem((32, 32, 128), F32),
            vmem((12, 64, 128), F32),
            vmem((NX, 256, 128), F32),
            vmem((NX, 256, 128), F32),
            vmem((NX, 256, HD), F32),
            vmem((NX, 256, HD), BF16),
            vmem((NX, 8, 256), F32),
            vmem((NX, 256, HD), BF16),
            vmem((NX, 8, 256), F32),
            vmem((4, NY, 64, HD), BF16),
            vmem((4, 2, 64, 512), BF16),
            vmem((NZ, 64, 512), BF16),
            vmem((NT, 4, 512), BF16),
            vmem((NT, 4, 512), BF16),
            dma((21,)),
            dma((8,)), dma, dma((16,)), dma, dma((4,)), dma((4,)),
            dma((16,)), dma((16,)), dma((16,)), dma((16,)), dma((32,)), dma((8,)),
            dma((4,)), dma((4,)), dma((4,)), dma, dma((8,)), dma((8,)),
            dma((32,)), dma((4,)), dma((8,)), dma, dma((16,)), dma,
        ],
        compiler_params=pltpu.CompilerParams(
            collective_id=0, has_side_effects=True, vmem_limit_bytes=56 * 1024 * 1024
        ),
        name="layer",
    )(q, k, v, w, kinds, counts, blocks, cols, offs)


def shards(q, k, v, w, kinds, counts, blocks, cols, offs):
    return layer(q, k, v, w, kinds, counts, blocks.transpose(1, 2, 0), cols, offs)


def solution(mesh):
    return jax.shard_map(
        shards,
        mesh=mesh,
        in_specs=(
            P(("ctx", "tp"), None),
            P("ctx", None),
            P("ctx", None),
            P("ctx", "tp"),
            P(),
            P(),
            P(),
            P(),
            P(),
        ),
        out_specs=P(("ctx", "tp"), None),
        check_vma=False,
    )
```

```python
import math

import jax
import jax.numpy as jnp
from jax import lax
from jax.experimental import pallas as pl
from jax.experimental.pallas import tpu as pltpu
from jax.sharding import PartitionSpec as P

H = 64
KVH = 8
HD = 128
NX, NZ, NY = 4, 8, 8
NT = 2 * NY
MASKED = -1e30
MESH = pl.DeviceIdType.MESH
F32 = jnp.float32
BF16 = jnp.bfloat16
SCALE = math.log2(math.e) / math.sqrt(HD)


def remote(src, dst, send_sem, recv_sem, ctx, tp):
    return pltpu.make_async_remote_copy(
        src_ref=src,
        dst_ref=dst,
        send_sem=send_sem,
        recv_sem=recv_sem,
        device_id=(ctx, tp),
        device_id_type=MESH,
    )


def arrived(ref, sem):
    pltpu.make_async_copy(ref, ref, sem).wait()


def lanes(shape):
    return lax.broadcasted_iota(jnp.int32, shape, len(shape) - 1)


def subs(shape):
    return lax.broadcasted_iota(jnp.int32, shape, 0)


def aligned(start, size):
    return pl.ds(pl.multiple_of(start, size), size)


def by_distance(i):
    odd = i % 2
    return odd * ((i + 1) // 2) + (1 - odd) * ((8 - i // 2) % 8)


def member_rows(values, first_row):
    high = jnp.where(values // 128 == first_row, 1.0, 0.0).astype(BF16)
    low = jnp.where(values % 128 == subs((128, values.shape[1])), 1.0, 0.0).astype(BF16)
    found = lax.dot_general(high, low, (((1,), (1,)), ((), ())), preferred_element_type=F32)
    return jnp.where(found > 0.5, 0.0, MASKED)


def fill_masks(slash, count, head, x, y, blocks, cols8, offs8, row_bias, tile_bias):
    tile = subs((32, 1024))
    tile = 16 * (tile // 4) + 4 * x + tile % 4
    vertical = member_rows(cols8[pl.ds(y, 1), :], tile)
    ids = jnp.where(lanes((32, 16, H)) == head, blocks[...].astype(F32), 0.0)
    ids = jnp.sum(ids, axis=2, keepdims=True)
    at = lanes((1, 1, 128))
    block = (8 * (4 * (at // 8) + x) + at % 8).astype(F32)
    turn = lax.broadcasted_iota(jnp.int32, (32, 16, 128), 1)
    hit = jnp.where(ids == block, 0.0, MASKED)
    hit = jnp.where(turn >= 1, jnp.where(turn < count, hit, MASKED), MASKED)
    chosen = jnp.max(hit, axis=1)
    left = lanes((32, 128)) < 64
    for i in range(32):
        pair = jnp.where(left, chosen[:, 2 * i : 2 * i + 1], chosen[:, 2 * i + 1 : 2 * i + 2])
        row_bias[i] = jnp.where(slash, jnp.broadcast_to(vertical[i : i + 1, :], (32, 128)), pair)
    rev = 511 - offs8[pl.ds(y, 1), :]
    phases = [member_rows(rev + 128 + 64 * phase, subs((8, 128))) for phase in range(2)]
    back = subs((64, 128)) - lanes((64, 128))
    right = lanes((64, 128)) >= 64
    nothing = jnp.full((64, 128), MASKED, F32)
    tile_bias[0] = nothing
    tile_bias[11] = nothing
    for i in range(10):
        start = 576 - 64 * i
        phase = (start // 64) % 2
        first = (start + 64 * phase) // 128
        pair = jnp.concatenate(
            [phases[phase][first : first + 1, :], phases[phase][first + 1 : first + 2, :]], axis=1
        )
        rolled = pltpu.roll(jnp.broadcast_to(pair, (64, 256)), 256 - 63, 1, stride=1, stride_axis=0)
        own = nothing
        if i == 0:
            own = jnp.where(right, MASKED, jnp.where(back >= 0, 0.0, MASKED))
        if i == 1:
            own = jnp.where(right, jnp.where(back + 64 >= 0, 0.0, MASKED), MASKED)
        tile_bias[i + 1] = jnp.where(slash, rolled[:, :128], own)


def layer_kernel(
    q_ref, k_ref, v_ref, w_ref, kind_ref, count_ref, blocks_ref, cols_ref, offs_ref,
    out_ref,
    qv, qt, qs, qy, q4, qf, qb, kl, kvb, wv, blocks, cols8, offs8, row_bias, tile_bias,
    top, total, mixed, o_out, st_out, ob, sb, share_of, ab, part, rb, fb, fr,
    in_sem, q1_send, q1_recv, q2_send, q2_recv, qx_send, qx_recv,
    kz_send, kz_recv, ky_send, ky_recv, kc_send, kc_recv,
    w_send, w_recv, wc_send, wc_recv, st_send, st_recv, ox_send, ox_recv,
    a_send, a_recv, z_send, z_recv, f_send, f_recv,
):
    ctx = lax.axis_index("ctx")
    t = lax.axis_index("tp")
    z, x, y, c = ctx // NX, ctx % NX, t // 2, t % 2
    partner = 2 * y + 1 - c
    head = 8 * z + y

    loads = [
        pltpu.make_async_copy(q_ref, qv, in_sem.at[0]),
        pltpu.make_async_copy(blocks_ref, blocks, in_sem.at[1]),
        pltpu.make_async_copy(cols_ref.at[aligned(8 * z, 8)], cols8, in_sem.at[2]),
        pltpu.make_async_copy(offs_ref.at[aligned(8 * z, 8)], offs8, in_sem.at[3]),
    ]
    for copy in loads:
        copy.start()

    barrier = pltpu.get_barrier_semaphore()

    def greet(to_ctx, to_tp):
        pl.semaphore_signal(barrier, inc=1, device_id=(to_ctx, to_tp), device_id_type=MESH)

    for d in range(1, NT):
        greet(ctx, (t + d) % NT)
    for d in range(1, NZ):
        for cc in range(2):
            greet(((z + d) % NZ) * NX + x, 2 * y + cc)
    for d in range(1, NX):
        greet(z * NX + (x + d) % NX, t)

    loads[0].wait()
    for yy in range(NY):
        for g in range(KVH):
            at = (8 * g + yy) * HD
            qt[g, yy] = qv[:, at : at + HD]
    share = 2 * (y % 2) + c
    other = 2 * (1 - y % 2) + c

    def piece(zz, i, s):
        return kvb.at[zz, i, aligned(128 * s, 128)]

    rows = aligned(128 * share, 128)
    dense = []
    for i, ref in enumerate((k_ref, v_ref)):
        pltpu.make_async_copy(
            ref.at[rows, aligned(HD * z, HD)], piece(z, i, share), kz_recv.at[2 * z + i]
        ).start()
        for d in range(1, NZ):
            cols = aligned(HD * ((z + d) % NZ), HD)
            dense.append(pltpu.make_async_copy(ref.at[rows, cols], kl.at[i, d], in_sem.at[5 + 8 * i + d]))
            dense[-1].start()
    w_own = pltpu.make_async_copy(w_ref, wv.at[c, x], in_sem.at[4])
    w_own.start()

    for copy in dense:
        copy.wait()
    pl.semaphore_wait(barrier, NT - 1 + 2 * (NZ - 1) + NX - 1)

    q1 = [
        remote(qt.at[(z + d) % NZ], qs.at[z], q1_send.at[d], q1_recv, ((z + d) % NZ) * NX + x, t)
        for d in range(1, NZ)
    ]
    for copy in q1:
        copy.start()
    pltpu.make_async_copy(qt.at[z], qs.at[z], q1_recv).start()

    kz = []
    for d in (1, 7, 2, 6, 3, 5, 4):
        g = (z + d) % NZ
        for i in range(2):
            copy = remote(
                kl.at[i, d], piece(z, i, share),
                kz_send.at[2 * d + i], kz_recv.at[2 * z + i], g * NX + x, t,
            )
            copy.start()
            kz.append(copy)

    def y_copy(zz, i):
        to = (y + 1) % NY if i == 0 else (y + NY - 1) % NY
        ref = piece(zz, i, share)
        return remote(ref, ref, ky_send.at[2 * zz + i], ky_recv.at[2 * zz + i], ctx, 2 * to + c)

    def core_copy(zz, i, s, n):
        ref = piece(zz, i, s)
        return remote(ref, ref, kc_send.at[4 * zz + 2 * n + i], kc_recv.at[zz], ctx, partner)

    def forward_own(i):
        zz = (z + by_distance(i)) % NZ
        for kv in range(2):
            arrived(piece(zz, kv, share), kz_recv.at[2 * zz + kv])
            y_copy(zz, kv).start()
            core_copy(zz, kv, share, 0).start()

    def forward_other(i):
        zz = (z + by_distance(i)) % NZ
        for kv in range(2):
            arrived(piece(zz, kv, other), ky_recv.at[2 * zz + kv])
            core_copy(zz, kv, other, 1).start()

    forward_own(0)

    for copy in loads[1:]:
        copy.wait()
    fill_masks(
        kind_ref[head] == 1, count_ref[head], head, x, y, blocks, cols8, offs8, row_bias, tile_bias
    )
    top[...] = jnp.full((NX, 256, 128), MASKED, F32)
    total[...] = jnp.zeros((NX, 256, 128), F32)
    mixed[...] = jnp.zeros((NX, 256, HD), F32)

    arrived(qs, q1_recv)
    for yy in range(NY):
        for zz in range(NZ):
            qy[yy, zz] = qs[zz, yy]
    q2 = []
    for d in range(1, NT):
        tt = (t + d) % NT
        src = qy.at[tt // 2, pl.ds(4 * (tt % 2), 4)]
        q2.append(remote(src, q4.at[t], q2_send.at[d], q2_recv, ctx, tt))
        q2[-1].start()
    pltpu.make_async_copy(qy.at[y, pl.ds(4 * c, 4)], q4.at[t], q2_recv).start()

    forward_own(1)
    forward_own(2)
    forward_other(0)

    arrived(q4, q2_recv)
    for zl in range(4):
        for tt in range(NT):
            qf[zl, 4 * tt : 4 * tt + 4, :] = q4[tt, zl].astype(F32)
    qb[x] = qf[...].astype(BF16)
    qx = [
        remote(qb.at[x], qb.at[x], qx_send.at[d], qx_recv.at[d], z * NX + (x + d) % NX, t)
        for d in range(1, NX)
    ]
    for copy in qx:
        copy.start()

    wx = [
        remote(w_ref, wv.at[c, x], w_send.at[d], w_recv.at[d], z * NX + (x + d) % NX, t)
        for d in (1, 3)
    ]
    wc = [remote(w_ref, wv.at[c, x], wc_send.at[0], wc_recv, ctx, partner)]
    for copy in wx + wc:
        copy.start()

    def w_relay(d):
        ref = wv.at[c, (x + NX - d) % NX, pl.ds(64 * (d - 1), 128)]
        return remote(ref, ref, w_send.at[d - 1], w_recv.at[d - 1], z * NX + (x + d) % NX, t)

    def w_core(d):
        ref = wv.at[c, (x + NX - d) % NX]
        return remote(ref, ref, wc_send.at[d], wc_recv, ctx, partner)

    for i in range(3, 7):
        forward_own(i)
        forward_other(i - 2)
    for d in range(1, NX):
        arrived(qb.at[(x + NX - d) % NX], qx_recv.at[d])
    forward_own(7)

    def chunk(zz, band):
        keys = kvb[zz, 0]
        values = kvb[zz, 1]

        queries = qb[...].reshape(1024, HD)
        s = lax.dot_general(queries, keys, (((1,), (1,)), ((), ())), preferred_element_type=F32)
        weights = []
        factors = []
        for n in range(16):
            xx, zl = n // 4, n % 4
            b = 16 * c + 4 * zl + xx
            old = top[xx, 64 * zl : 64 * zl + 64]
            tiles = []
            high = None
            for w in range(4):
                bias = row_bias[4 * zz + w, pl.ds(b, 1), :]
                if band:
                    which = 225 + b - 8 * (4 * zz + x) - 2 * w
                    bias = jnp.maximum(bias, tile_bias[jnp.clip(which, 0, 11)])
                tile = s[64 * n : 64 * n + 64, 128 * w : 128 * w + 128] * SCALE + bias
                high = tile if high is None else jnp.maximum(high, tile)
                tiles.append(tile)
            new = jnp.maximum(old, jnp.max(high, axis=1, keepdims=True))
            top[xx, 64 * zl : 64 * zl + 64] = new
            factor = jnp.exp2(old - new)
            tiles = [jnp.exp2(tile - new) for tile in tiles]
            total[xx, 64 * zl : 64 * zl + 64] = total[xx, 64 * zl : 64 * zl + 64] * factor + (
                (tiles[0] + tiles[1]) + (tiles[2] + tiles[3])
            )
            factors.append(factor)
            weights.append(jnp.concatenate([tile.astype(BF16) for tile in tiles], axis=1))
        added = jnp.dot(jnp.concatenate(weights, axis=0), values, preferred_element_type=F32)
        for n in range(16):
            at = (n // 4, pl.ds(64 * (n % 4), 64))
            mixed[at] = mixed[at] * factors[n] + added[64 * n : 64 * n + 64]

    def step(i, carry):
        zz = (z + by_distance(i)) % NZ

        @pl.when(i < NZ - 5)
        def _():
            forward_other(i + 5)

        @pl.when(i == 5)
        def _():
            for d in (1, 3):
                arrived(wv.at[c, (x + NX - d) % NX], w_recv.at[d])
                w_relay(d).start()
                w_core(d).start()

        arrived(kvb.at[zz, 0], kc_recv.at[zz])

        @pl.when(zz >= 6)
        def _():
            chunk(zz, True)

        @pl.when(zz < 6)
        def _():
            chunk(zz, False)

        return carry

    lax.fori_loop(0, NZ, step, 0)

    def st_copy(d):
        xx = (x + d) % NX
        return remote(st_out.at[xx], sb.at[d], st_send.at[d], st_recv.at[d], z * NX + xx, t)

    def o_copy(i, d):
        xx = (x + d) % NX
        return remote(
            o_out.at[xx, i], ob.at[d, i], ox_send.at[4 * i + d], ox_recv.at[4 * i + d], z * NX + xx, t
        )

    for d in (2, 1, 3, 0):
        xx = (x + d) % NX
        amount = jnp.sum(total[xx], axis=1, keepdims=True)
        o_out[xx] = (mixed[xx] / amount).astype(BF16).reshape(4, 64, HD)
        st_out[xx] = (top[xx] + jnp.log2(amount)).T[:8, :]
        if d:
            st_copy(d).start()
            o_copy(z % 4, d).start()
    for j in range(1, 4):
        for d in (2, 1, 3):
            o_copy((z + j) % 4, d).start()
    for d in range(1, NX):
        arrived(sb.at[d], st_recv.at[d])
    levels = [st_out[x]] + [sb[d] for d in range(1, NX)]
    best = jnp.maximum(jnp.maximum(levels[0], levels[1]), jnp.maximum(levels[2], levels[3]))
    parts = [jnp.exp2(level - best) for level in levels]
    amount = (parts[0] + parts[1]) + (parts[2] + parts[3])
    parts = [p / amount for p in parts]
    share_of[...] = jnp.concatenate(parts + [jnp.zeros((96, 256), F32)], axis=0).T

    def a_copy(i, d):
        ref = ab.at[i, y]
        return remote(ref, ref, a_send.at[8 * i + d], a_recv.at[i], ctx, 2 * ((y + d) % NY) + c)

    for j in range(4):
        i = (z + j) % 4
        part_share = share_of[aligned(64 * i, 64), :]
        joined = part_share[:, 0:1] * o_out[x, i].astype(F32)
        for d in range(1, NX):
            arrived(ob.at[d, i], ox_recv.at[4 * i + d])
            joined = joined + part_share[:, 8 * d : 8 * d + 1] * ob[d, i].astype(F32)
        ab[i, y] = joined.astype(BF16)
        for d in (4, 3, 5, 2, 6, 1, 7):
            a_copy(i, d).start()

    for h in range(2):
        arrived(wv.at[c, (x + 2) % NX, pl.ds(128 * h, 128)], w_recv.at[2 * h])
    w_core(2).start()
    arrived(wv.at[0], wc_recv)
    w_own.wait()

    def z_copy(i, cc):
        return remote(
            part.at[i, cc], rb.at[z], z_send.at[2 * i + cc], z_recv, (4 * c + i) * NX + x, 2 * y + cc
        )

    for j in range(4):
        i = (z + j) % 4
        arrived(ab.at[i, pl.ds(0, NY - 1)], a_recv.at[i])
        features = jnp.concatenate([ab[i, yy] for yy in range(NY)], axis=1)
        for cc in range(2):
            weight = wv[cc].reshape(1024, 512)
            part[i, cc] = jnp.dot(features, weight, preferred_element_type=F32).astype(BF16)
            mine = jnp.logical_and(4 * c + i == z, cc == c)

            @pl.when(jnp.logical_not(mine))
            def _():
                z_copy(i, cc).start()

            @pl.when(mine)
            def _():
                pltpu.make_async_copy(part.at[i, cc], rb.at[z], z_recv).start()

    arrived(rb, z_recv)
    summed = rb[0].astype(F32)
    for g in range(1, NZ):
        summed = summed + rb[g].astype(F32)
    for tt in range(NT):
        fb[tt] = summed[4 * tt : 4 * tt + 4, :].astype(BF16)
    last = [
        remote(fb.at[(t + d) % NT], fr.at[t], f_send.at[d], f_recv, ctx, (t + d) % NT)
        for d in range(1, NT)
    ]
    for copy in last:
        copy.start()
    pltpu.make_async_copy(fb.at[t], fr.at[t], f_recv).start()

    for copy in q1 + q2 + kz + qx + wx + wc:
        copy.wait_send()
    for d in range(1, NX):
        w_core(d).wait_send()
        st_copy(d).wait_send()
        for i in range(4):
            o_copy(i, d).wait_send()
    for d in (1, 3):
        w_relay(d).wait_send()

    def sent(zz, carry):
        for kv in range(2):
            y_copy(zz, kv).wait_send()
            core_copy(zz, kv, share, 0).wait_send()
            core_copy(zz, kv, other, 1).wait_send()
        return carry

    lax.fori_loop(0, NZ, sent, 0)
    for i in range(4):
        for d in range(1, NY):
            a_copy(i, d).wait_send()
        for cc in range(2):
            mine = jnp.logical_and(4 * c + i == z, cc == c)

            @pl.when(jnp.logical_not(mine))
            def _():
                z_copy(i, cc).wait_send()

    arrived(fr, f_recv)
    for tt in range(NT):
        out_ref[:, 512 * tt : 512 * tt + 512] = fr[tt]
    for copy in last:
        copy.wait_send()


def layer(q, k, v, w, kinds, counts, blocks, cols, offs):
    dma = pltpu.SemaphoreType.DMA
    hbm = pl.BlockSpec(memory_space=pltpu.HBM)
    smem = pl.BlockSpec(memory_space=pltpu.SMEM)
    vmem = pltpu.VMEM
    return pl.pallas_call(
        layer_kernel,
        out_shape=jax.ShapeDtypeStruct((4, 8192), BF16),
        in_specs=[hbm, hbm, hbm, hbm, smem, smem, hbm, hbm, hbm],
        out_specs=pl.BlockSpec(memory_space=pltpu.VMEM),
        scratch_shapes=[
            vmem((4, 8192), BF16),
            vmem((KVH, NY, 4, HD), BF16),
            vmem((NZ, NY, 4, HD), BF16),
            vmem((NY, NZ, 4, HD), BF16),
            vmem((NT, 4, 4, HD), BF16),
            vmem((4, 64, HD), F32),
            vmem((NX, 4, 64, HD), BF16),
            vmem((2, NZ, 128, HD), BF16),
            vmem((NZ, 2, 512, HD), BF16),
            vmem((2, NX, 256, 512), BF16),
            vmem((32, 16, H), jnp.int32),
            vmem((8, 1024), jnp.int32),
            vmem((8, 128), jnp.int32),
            vmem((32, 32, 128), F32),
            vmem((12, 64, 128), F32),
            vmem((NX, 256, 128), F32),
            vmem((NX, 256, 128), F32),
            vmem((NX, 256, HD), F32),
            vmem((NX, 4, 64, HD), BF16),
            vmem((NX, 8, 256), F32),
            vmem((NX, 4, 64, HD), BF16),
            vmem((NX, 8, 256), F32),
            vmem((256, 128), F32),
            vmem((4, NY, 64, HD), BF16),
            vmem((4, 2, 64, 512), BF16),
            vmem((NZ, 64, 512), BF16),
            vmem((NT, 4, 512), BF16),
            vmem((NT, 4, 512), BF16),
            dma((21,)),
            dma((8,)), dma, dma((16,)), dma, dma((4,)), dma((4,)),
            dma((16,)), dma((16,)), dma((16,)), dma((16,)), dma((32,)), dma((8,)),
            dma((4,)), dma((4,)), dma((4,)), dma, dma((4,)), dma((4,)), dma((16,)), dma((16,)),
            dma((32,)), dma((4,)), dma((8,)), dma, dma((16,)), dma,
        ],
        compiler_params=pltpu.CompilerParams(
            collective_id=0, has_side_effects=True, vmem_limit_bytes=56 * 1024 * 1024
        ),
        name="layer",
    )(q, k, v, w, kinds, counts, blocks, cols, offs)


def shards(q, k, v, w, kinds, counts, blocks, cols, offs):
    return layer(q, k, v, w, kinds, counts, blocks.transpose(1, 2, 0), cols, offs)


def solution(mesh):
    return jax.shard_map(
        shards,
        mesh=mesh,
        in_specs=(
            P(("ctx", "tp"), None),
            P("ctx", None),
            P("ctx", None),
            P("ctx", "tp"),
            P(),
            P(),
            P(),
            P(),
            P(),
        ),
        out_specs=P(("ctx", "tp"), None),
        check_vma=False,
    )
```

```python
import math

import jax
import jax.numpy as jnp
from jax import lax
from jax.experimental import pallas as pl
from jax.experimental.pallas import tpu as pltpu
from jax.sharding import PartitionSpec as P

H = 64
KVH = 8
HD = 128
NX, NZ, NY = 4, 8, 8
NT = 2 * NY
MASKED = -1e30
MESH = pl.DeviceIdType.MESH
F32 = jnp.float32
BF16 = jnp.bfloat16
SCALE = math.log2(math.e) / math.sqrt(HD)


def remote(src, dst, send_sem, recv_sem, ctx, tp):
    return pltpu.make_async_remote_copy(
        src_ref=src,
        dst_ref=dst,
        send_sem=send_sem,
        recv_sem=recv_sem,
        device_id=(ctx, tp),
        device_id_type=MESH,
    )


def arrived(ref, sem):
    pltpu.make_async_copy(ref, ref, sem).wait()


def lanes(shape):
    return lax.broadcasted_iota(jnp.int32, shape, len(shape) - 1)


def subs(shape):
    return lax.broadcasted_iota(jnp.int32, shape, 0)


def aligned(start, size):
    return pl.ds(pl.multiple_of(start, size), size)


def by_distance(i):
    odd = i % 2
    return odd * ((i + 1) // 2) + (1 - odd) * ((8 - i // 2) % 8)


def member_rows(values, first_row):
    high = jnp.where(values // 128 == first_row, 1.0, 0.0).astype(BF16)
    low = jnp.where(values % 128 == subs((128, values.shape[1])), 1.0, 0.0).astype(BF16)
    found = lax.dot_general(high, low, (((1,), (1,)), ((), ())), preferred_element_type=F32)
    return jnp.where(found > 0.5, 0.0, MASKED)


def fill_masks(slash, count, head, x, y, blocks, cols8, offs8, row_bias, tile_bias):
    tile = subs((32, 1024))
    tile = 16 * (tile // 4) + 4 * x + tile % 4
    vertical = member_rows(cols8[pl.ds(y, 1), :], tile)
    ids = jnp.where(lanes((32, 16, H)) == head, blocks[...].astype(F32), 0.0)
    ids = jnp.sum(ids, axis=2, keepdims=True)
    at = lanes((1, 1, 128))
    block = (8 * (4 * (at // 8) + x) + at % 8).astype(F32)
    turn = lax.broadcasted_iota(jnp.int32, (32, 16, 128), 1)
    hit = jnp.where(ids == block, 0.0, MASKED)
    hit = jnp.where(turn >= 1, jnp.where(turn < count, hit, MASKED), MASKED)
    chosen = jnp.max(hit, axis=1)
    left = lanes((32, 128)) < 64
    for i in range(32):
        pair = jnp.where(left, chosen[:, 2 * i : 2 * i + 1], chosen[:, 2 * i + 1 : 2 * i + 2])
        row_bias[i] = jnp.where(slash, jnp.broadcast_to(vertical[i : i + 1, :], (32, 128)), pair)
    rev = 511 - offs8[pl.ds(y, 1), :]
    phases = [member_rows(rev + 128 + 64 * phase, subs((8, 128))) for phase in range(2)]
    back = subs((64, 128)) - lanes((64, 128))
    right = lanes((64, 128)) >= 64
    nothing = jnp.full((64, 128), MASKED, F32)
    tile_bias[0] = nothing
    tile_bias[11] = nothing
    for i in range(10):
        start = 576 - 64 * i
        phase = (start // 64) % 2
        first = (start + 64 * phase) // 128
        pair = jnp.concatenate(
            [phases[phase][first : first + 1, :], phases[phase][first + 1 : first + 2, :]], axis=1
        )
        rolled = pltpu.roll(jnp.broadcast_to(pair, (64, 256)), 256 - 63, 1, stride=1, stride_axis=0)
        own = nothing
        if i == 0:
            own = jnp.where(right, MASKED, jnp.where(back >= 0, 0.0, MASKED))
        if i == 1:
            own = jnp.where(right, jnp.where(back + 64 >= 0, 0.0, MASKED), MASKED)
        tile_bias[i + 1] = jnp.where(slash, rolled[:, :128], own)


def layer_kernel(
    q_ref, k_ref, v_ref, w_ref, kind_ref, count_ref, blocks_ref, cols_ref, offs_ref,
    out_ref,
    qv, qt, qs, qy, q4, qf, qb, kl, kvb, wv, blocks, cols8, offs8, row_bias, tile_bias,
    top, total, mixed, o_out, st_out, ob, sb, share_of, ab, part, rb,
    in_sem, q1_send, q1_recv, q2_send, q2_recv, qx_send, qx_recv,
    kz_send, kz_recv, ky_send, ky_recv, kc_send, kc_recv,
    w_send, w_recv, wc_send, wc_recv, st_send, st_recv, ox_send, ox_recv,
    a_send, a_recv, z_send, z_recv,
):
    ctx = lax.axis_index("ctx")
    t = lax.axis_index("tp")
    z, x, y, c = ctx // NX, ctx % NX, t // 2, t % 2
    partner = 2 * y + 1 - c
    head = 8 * z + y

    loads = [
        pltpu.make_async_copy(q_ref, qv, in_sem.at[0]),
        pltpu.make_async_copy(blocks_ref, blocks, in_sem.at[1]),
        pltpu.make_async_copy(cols_ref.at[aligned(8 * z, 8)], cols8, in_sem.at[2]),
        pltpu.make_async_copy(offs_ref.at[aligned(8 * z, 8)], offs8, in_sem.at[3]),
    ]
    for copy in loads:
        copy.start()

    barrier = pltpu.get_barrier_semaphore()

    def greet(to_ctx, to_tp):
        pl.semaphore_signal(barrier, inc=1, device_id=(to_ctx, to_tp), device_id_type=MESH)

    for d in range(1, NT):
        greet(ctx, (t + d) % NT)
    for d in range(1, NZ):
        for cc in range(2):
            greet(((z + d) % NZ) * NX + x, 2 * y + cc)
    for d in range(1, NX):
        greet(z * NX + (x + d) % NX, t)

    loads[0].wait()
    for yy in range(NY):
        for g in range(KVH):
            at = (8 * g + yy) * HD
            qt[g, yy] = qv[:, at : at + HD]
    share = 2 * (y % 2) + c
    other = 2 * (1 - y % 2) + c

    def piece(zz, i, s):
        return kvb.at[zz, i, aligned(128 * s, 128)]

    rows = aligned(128 * share, 128)
    dense = []
    for i, ref in enumerate((k_ref, v_ref)):
        pltpu.make_async_copy(
            ref.at[rows, aligned(HD * z, HD)], piece(z, i, share), kz_recv.at[2 * z + i]
        ).start()
        for d in range(1, NZ):
            cols = aligned(HD * ((z + d) % NZ), HD)
            dense.append(pltpu.make_async_copy(ref.at[rows, cols], kl.at[i, d], in_sem.at[5 + 8 * i + d]))
            dense[-1].start()
    w_own = pltpu.make_async_copy(w_ref, wv.at[c, x], in_sem.at[4])
    w_own.start()

    for copy in dense:
        copy.wait()
    pl.semaphore_wait(barrier, NT - 1 + 2 * (NZ - 1) + NX - 1)

    q1 = [
        remote(qt.at[(z + d) % NZ], qs.at[z], q1_send.at[d], q1_recv, ((z + d) % NZ) * NX + x, t)
        for d in range(1, NZ)
    ]
    for copy in q1:
        copy.start()
    pltpu.make_async_copy(qt.at[z], qs.at[z], q1_recv).start()

    kz = []
    for d in (1, 7, 2, 6, 3, 5, 4):
        g = (z + d) % NZ
        for i in range(2):
            copy = remote(
                kl.at[i, d], piece(z, i, share),
                kz_send.at[2 * d + i], kz_recv.at[2 * z + i], g * NX + x, t,
            )
            copy.start()
            kz.append(copy)

    def y_copy(zz, i):
        to = (y + 1) % NY if i == 0 else (y + NY - 1) % NY
        ref = piece(zz, i, share)
        return remote(ref, ref, ky_send.at[2 * zz + i], ky_recv.at[2 * zz + i], ctx, 2 * to + c)

    def core_copy(zz, i, s, n):
        ref = piece(zz, i, s)
        return remote(ref, ref, kc_send.at[4 * zz + 2 * n + i], kc_recv.at[zz], ctx, partner)

    def forward_own(i):
        zz = (z + by_distance(i)) % NZ
        for kv in range(2):
            arrived(piece(zz, kv, share), kz_recv.at[2 * zz + kv])
            y_copy(zz, kv).start()
            core_copy(zz, kv, share, 0).start()

    def forward_other(i):
        zz = (z + by_distance(i)) % NZ
        for kv in range(2):
            arrived(piece(zz, kv, other), ky_recv.at[2 * zz + kv])
            core_copy(zz, kv, other, 1).start()

    forward_own(0)

    for copy in loads[1:]:
        copy.wait()
    fill_masks(
        kind_ref[head] == 1, count_ref[head], head, x, y, blocks, cols8, offs8, row_bias, tile_bias
    )
    top[...] = jnp.full((NX, 256, 128), MASKED, F32)
    total[...] = jnp.zeros((NX, 256, 128), F32)
    mixed[...] = jnp.zeros((NX, 256, HD), F32)

    arrived(qs, q1_recv)
    for yy in range(NY):
        for zz in range(NZ):
            qy[yy, zz] = qs[zz, yy]
    q2 = []
    for d in range(1, NT):
        tt = (t + d) % NT
        src = qy.at[tt // 2, pl.ds(4 * (tt % 2), 4)]
        q2.append(remote(src, q4.at[t], q2_send.at[d], q2_recv, ctx, tt))
        q2[-1].start()
    pltpu.make_async_copy(qy.at[y, pl.ds(4 * c, 4)], q4.at[t], q2_recv).start()

    forward_own(1)
    forward_own(2)
    forward_other(0)

    arrived(q4, q2_recv)
    for zl in range(4):
        for tt in range(NT):
            qf[zl, 4 * tt : 4 * tt + 4, :] = q4[tt, zl].astype(F32)
    qb[x] = qf[...].astype(BF16)
    qx = [
        remote(qb.at[x], qb.at[x], qx_send.at[d], qx_recv.at[d], z * NX + (x + d) % NX, t)
        for d in range(1, NX)
    ]
    for copy in qx:
        copy.start()

    wx = [
        remote(w_ref, wv.at[c, x], w_send.at[d], w_recv.at[d], z * NX + (x + d) % NX, t)
        for d in (1, 3)
    ]
    wc = [remote(w_ref, wv.at[c, x], wc_send.at[0], wc_recv, ctx, partner)]
    for copy in wx + wc:
        copy.start()

    def w_relay(d):
        ref = wv.at[c, (x + NX - d) % NX, pl.ds(64 * (d - 1), 128)]
        return remote(ref, ref, w_send.at[d - 1], w_recv.at[d - 1], z * NX + (x + d) % NX, t)

    def w_core(d):
        ref = wv.at[c, (x + NX - d) % NX]
        return remote(ref, ref, wc_send.at[d], wc_recv, ctx, partner)

    for i in range(3, 7):
        forward_own(i)
        forward_other(i - 2)
    for d in range(1, NX):
        arrived(qb.at[(x + NX - d) % NX], qx_recv.at[d])
    forward_own(7)

    def chunk(zz, band):
        keys = kvb[zz, 0]
        values = kvb[zz, 1]

        queries = qb[...].reshape(1024, HD)
        s = lax.dot_general(queries, keys, (((1,), (1,)), ((), ())), preferred_element_type=F32)
        weights = []
        factors = []
        for n in range(16):
            xx, zl = n // 4, n % 4
            b = 16 * c + 4 * zl + xx
            old = top[xx, 64 * zl : 64 * zl + 64]
            tiles = []
            high = None
            for w in range(4):
                bias = row_bias[4 * zz + w, pl.ds(b, 1), :]
                if band:
                    which = 225 + b - 8 * (4 * zz + x) - 2 * w
                    bias = jnp.maximum(bias, tile_bias[jnp.clip(which, 0, 11)])
                tile = s[64 * n : 64 * n + 64, 128 * w : 128 * w + 128] * SCALE + bias
                high = tile if high is None else jnp.maximum(high, tile)
                tiles.append(tile)
            new = jnp.maximum(old, jnp.max(high, axis=1, keepdims=True))
            top[xx, 64 * zl : 64 * zl + 64] = new
            factor = jnp.exp2(old - new)
            tiles = [jnp.exp2(tile - new) for tile in tiles]
            total[xx, 64 * zl : 64 * zl + 64] = total[xx, 64 * zl : 64 * zl + 64] * factor + (
                (tiles[0] + tiles[1]) + (tiles[2] + tiles[3])
            )
            factors.append(factor)
            weights.append(jnp.concatenate([tile.astype(BF16) for tile in tiles], axis=1))
        added = jnp.dot(jnp.concatenate(weights, axis=0), values, preferred_element_type=F32)
        for n in range(16):
            at = (n // 4, pl.ds(64 * (n % 4), 64))
            mixed[at] = mixed[at] * factors[n] + added[64 * n : 64 * n + 64]

    def step(i, carry):
        zz = (z + by_distance(i)) % NZ

        @pl.when(i < NZ - 5)
        def _():
            forward_other(i + 5)

        @pl.when(i == 5)
        def _():
            for d in (1, 3):
                arrived(wv.at[c, (x + NX - d) % NX], w_recv.at[d])
                w_relay(d).start()
                w_core(d).start()

        arrived(kvb.at[zz, 0], kc_recv.at[zz])

        @pl.when(zz >= 6)
        def _():
            chunk(zz, True)

        @pl.when(zz < 6)
        def _():
            chunk(zz, False)

        return carry

    lax.fori_loop(0, NZ, step, 0)

    def st_copy(d):
        xx = (x + d) % NX
        return remote(st_out.at[xx], sb.at[d], st_send.at[d], st_recv.at[d], z * NX + xx, t)

    def o_copy(i, d):
        xx = (x + d) % NX
        return remote(
            o_out.at[xx, i], ob.at[d, i], ox_send.at[4 * i + d], ox_recv.at[4 * i + d], z * NX + xx, t
        )

    for d in (2, 1, 3, 0):
        xx = (x + d) % NX
        amount = jnp.sum(total[xx], axis=1, keepdims=True)
        o_out[xx] = (mixed[xx] / amount).astype(BF16).reshape(4, 64, HD)
        st_out[xx] = (top[xx] + jnp.log2(amount)).T[:8, :]
        if d:
            st_copy(d).start()
            o_copy(z % 4, d).start()
    for j in range(1, 4):
        for d in (2, 1, 3):
            o_copy((z + j) % 4, d).start()
    for d in range(1, NX):
        arrived(sb.at[d], st_recv.at[d])
    levels = [st_out[x]] + [sb[d] for d in range(1, NX)]
    best = jnp.maximum(jnp.maximum(levels[0], levels[1]), jnp.maximum(levels[2], levels[3]))
    parts = [jnp.exp2(level - best) for level in levels]
    amount = (parts[0] + parts[1]) + (parts[2] + parts[3])
    parts = [p / amount for p in parts]
    share_of[...] = jnp.concatenate(parts + [jnp.zeros((96, 256), F32)], axis=0).T

    def a_copy(i, d):
        ref = ab.at[i, y]
        return remote(ref, ref, a_send.at[8 * i + d], a_recv.at[i], ctx, 2 * ((y + d) % NY) + c)

    for j in range(4):
        i = (z + j) % 4
        part_share = share_of[aligned(64 * i, 64), :]
        joined = part_share[:, 0:1] * o_out[x, i].astype(F32)
        for d in range(1, NX):
            arrived(ob.at[d, i], ox_recv.at[4 * i + d])
            joined = joined + part_share[:, 8 * d : 8 * d + 1] * ob[d, i].astype(F32)
        ab[i, y] = joined.astype(BF16)
        for d in (4, 3, 5, 2, 6, 1, 7):
            a_copy(i, d).start()

    for h in range(2):
        arrived(wv.at[c, (x + 2) % NX, pl.ds(128 * h, 128)], w_recv.at[2 * h])
    w_core(2).start()
    arrived(wv.at[0], wc_recv)
    w_own.wait()

    def z_copy(i, d):
        tt = (t + d) % NT
        return remote(
            part.at[i, tt], rb.at[z, y], z_send.at[NT * i + d], z_recv, (4 * c + i) * NX + x, tt
        )

    for j in range(4):
        i = (z + j) % 4
        arrived(ab.at[i, pl.ds(0, NY - 1)], a_recv.at[i])
        features = jnp.concatenate([ab[i, yy] for yy in range(NY)], axis=1)
        for cc in range(2):
            weight = wv[cc].reshape(1024, 512)
            rows = jnp.dot(features, weight, preferred_element_type=F32)
            for tt in range(NT):
                part[i, tt, :, 512 * cc : 512 * cc + 512] = rows[4 * tt : 4 * tt + 4, :].astype(BF16)
        for d in range(1, NT):
            z_copy(i, d).start()

        @pl.when(4 * c + i == z)
        def _():
            pltpu.make_async_copy(part.at[i, t], rb.at[z, y], z_recv).start()

        @pl.when(4 * c + i != z)
        def _():
            z_copy(i, 0).start()

    for copy in q1 + q2 + kz + qx + wx + wc:
        copy.wait_send()
    for d in range(1, NX):
        w_core(d).wait_send()
        st_copy(d).wait_send()
        for i in range(4):
            o_copy(i, d).wait_send()
    for d in (1, 3):
        w_relay(d).wait_send()

    def sent(zz, carry):
        for kv in range(2):
            y_copy(zz, kv).wait_send()
            core_copy(zz, kv, share, 0).wait_send()
            core_copy(zz, kv, other, 1).wait_send()
        return carry

    lax.fori_loop(0, NZ, sent, 0)
    for i in range(4):
        for d in range(1, NY):
            a_copy(i, d).wait_send()
        for d in range(1, NT):
            z_copy(i, d).wait_send()

        @pl.when(4 * c + i != z)
        def _():
            z_copy(i, 0).wait_send()

    arrived(rb, z_recv)
    for yy in range(NY):
        summed = rb[0, yy].astype(F32)
        for g in range(1, NZ):
            summed = summed + rb[g, yy].astype(F32)
        out_ref[:, 1024 * yy : 1024 * yy + 1024] = summed.astype(BF16)


def layer(q, k, v, w, kinds, counts, blocks, cols, offs):
    dma = pltpu.SemaphoreType.DMA
    hbm = pl.BlockSpec(memory_space=pltpu.HBM)
    smem = pl.BlockSpec(memory_space=pltpu.SMEM)
    vmem = pltpu.VMEM
    return pl.pallas_call(
        layer_kernel,
        out_shape=jax.ShapeDtypeStruct((4, 8192), BF16),
        in_specs=[hbm, hbm, hbm, hbm, smem, smem, hbm, hbm, hbm],
        out_specs=pl.BlockSpec(memory_space=pltpu.VMEM),
        scratch_shapes=[
            vmem((4, 8192), BF16),
            vmem((KVH, NY, 4, HD), BF16),
            vmem((NZ, NY, 4, HD), BF16),
            vmem((NY, NZ, 4, HD), BF16),
            vmem((NT, 4, 4, HD), BF16),
            vmem((4, 64, HD), F32),
            vmem((NX, 4, 64, HD), BF16),
            vmem((2, NZ, 128, HD), BF16),
            vmem((NZ, 2, 512, HD), BF16),
            vmem((2, NX, 256, 512), BF16),
            vmem((32, 16, H), jnp.int32),
            vmem((8, 1024), jnp.int32),
            vmem((8, 128), jnp.int32),
            vmem((32, 32, 128), F32),
            vmem((12, 64, 128), F32),
            vmem((NX, 256, 128), F32),
            vmem((NX, 256, 128), F32),
            vmem((NX, 256, HD), F32),
            vmem((NX, 4, 64, HD), BF16),
            vmem((NX, 8, 256), F32),
            vmem((NX, 4, 64, HD), BF16),
            vmem((NX, 8, 256), F32),
            vmem((256, 128), F32),
            vmem((4, NY, 64, HD), BF16),
            vmem((4, NT, 4, 1024), BF16),
            vmem((NZ, NY, 4, 1024), BF16),
            dma((21,)),
            dma((8,)), dma, dma((16,)), dma, dma((4,)), dma((4,)),
            dma((16,)), dma((16,)), dma((16,)), dma((16,)), dma((32,)), dma((8,)),
            dma((4,)), dma((4,)), dma((4,)), dma, dma((4,)), dma((4,)), dma((16,)), dma((16,)),
            dma((32,)), dma((4,)), dma((64,)), dma,
        ],
        compiler_params=pltpu.CompilerParams(
            collective_id=0, has_side_effects=True, vmem_limit_bytes=56 * 1024 * 1024
        ),
        name="layer",
    )(q, k, v, w, kinds, counts, blocks, cols, offs)


def shards(q, k, v, w, kinds, counts, blocks, cols, offs):
    return layer(q, k, v, w, kinds, counts, blocks.transpose(1, 2, 0), cols, offs)


def solution(mesh):
    return jax.shard_map(
        shards,
        mesh=mesh,
        in_specs=(
            P(("ctx", "tp"), None),
            P("ctx", None),
            P("ctx", None),
            P("ctx", "tp"),
            P(),
            P(),
            P(),
            P(),
            P(),
        ),
        out_specs=P(("ctx", "tp"), None),
        check_vma=False,
    )
```

```python
import math

import jax
import jax.numpy as jnp
from jax import lax
from jax.experimental import pallas as pl
from jax.experimental.pallas import tpu as pltpu
from jax.sharding import PartitionSpec as P

H = 64
KVH = 8
HD = 128
NX, NZ, NY = 4, 8, 8
NT = 2 * NY
MASKED = -1e30
MESH = pl.DeviceIdType.MESH
F32 = jnp.float32
BF16 = jnp.bfloat16
SCALE = math.log2(math.e) / math.sqrt(HD)


def remote(src, dst, send_sem, recv_sem, ctx, tp):
    return pltpu.make_async_remote_copy(
        src_ref=src,
        dst_ref=dst,
        send_sem=send_sem,
        recv_sem=recv_sem,
        device_id=(ctx, tp),
        device_id_type=MESH,
    )


def arrived(ref, sem):
    pltpu.make_async_copy(ref, ref, sem).wait()


def lanes(shape):
    return lax.broadcasted_iota(jnp.int32, shape, len(shape) - 1)


def subs(shape):
    return lax.broadcasted_iota(jnp.int32, shape, 0)


def aligned(start, size):
    return pl.ds(pl.multiple_of(start, size), size)


def by_distance(i):
    odd = i % 2
    return odd * ((i + 1) // 2) + (1 - odd) * ((8 - i // 2) % 8)


def member_rows(values, first_row):
    high = jnp.where(values // 128 == first_row, 1.0, 0.0).astype(BF16)
    low = jnp.where(values % 128 == subs((128, values.shape[1])), 1.0, 0.0).astype(BF16)
    found = lax.dot_general(high, low, (((1,), (1,)), ((), ())), preferred_element_type=F32)
    return jnp.where(found > 0.5, 0.0, MASKED)


def fill_masks(slash, count, head, x, y, blocks, cols8, offs8, row_bias, tile_bias):
    tile = subs((32, 1024))
    tile = 16 * (tile // 4) + 4 * x + tile % 4
    vertical = member_rows(cols8[pl.ds(y, 1), :], tile)
    ids = jnp.where(lanes((32, 16, H)) == head, blocks[...].astype(F32), 0.0)
    ids = jnp.sum(ids, axis=2, keepdims=True)
    at = lanes((1, 1, 128))
    block = (8 * (4 * (at // 8) + x) + at % 8).astype(F32)
    turn = lax.broadcasted_iota(jnp.int32, (32, 16, 128), 1)
    hit = jnp.where(ids == block, 0.0, MASKED)
    hit = jnp.where(turn >= 1, jnp.where(turn < count, hit, MASKED), MASKED)
    chosen = jnp.max(hit, axis=1)
    left = lanes((32, 128)) < 64
    for i in range(32):
        pair = jnp.where(left, chosen[:, 2 * i : 2 * i + 1], chosen[:, 2 * i + 1 : 2 * i + 2])
        row_bias[i] = jnp.where(slash, jnp.broadcast_to(vertical[i : i + 1, :], (32, 128)), pair)
    rev = 511 - offs8[pl.ds(y, 1), :]
    phases = [member_rows(rev + 128 + 64 * phase, subs((8, 128))) for phase in range(2)]
    back = subs((64, 128)) - lanes((64, 128))
    right = lanes((64, 128)) >= 64
    nothing = jnp.full((64, 128), MASKED, F32)
    tile_bias[0] = nothing
    tile_bias[11] = nothing
    for i in range(10):
        start = 576 - 64 * i
        phase = (start // 64) % 2
        first = (start + 64 * phase) // 128
        pair = jnp.concatenate(
            [phases[phase][first : first + 1, :], phases[phase][first + 1 : first + 2, :]], axis=1
        )
        rolled = pltpu.roll(jnp.broadcast_to(pair, (64, 256)), 256 - 63, 1, stride=1, stride_axis=0)
        own = nothing
        if i == 0:
            own = jnp.where(right, MASKED, jnp.where(back >= 0, 0.0, MASKED))
        if i == 1:
            own = jnp.where(right, jnp.where(back + 64 >= 0, 0.0, MASKED), MASKED)
        tile_bias[i + 1] = jnp.where(slash, rolled[:, :128], own)


def layer_kernel(
    q_ref, k_ref, v_ref, w_ref, kind_ref, count_ref, blocks_ref, cols_ref, offs_ref,
    out_ref,
    qv, qt, qs, qy, q4, qf, qb, kl, kvb, wv, blocks, cols8, offs8, row_bias, tile_bias,
    top, total, mixed, o_out, st_out, ob, sb, share_of, ab, part, early, pieces, late, fb, fr,
    in_sem, q1_send, q1_recv, q2_send, q2_recv, qx_send, qx_recv,
    kz_send, kz_recv, ky_send, ky_recv, kc_send, kc_recv,
    w_send, w_recv, wc_send, wc_recv, st_send, st_recv, ox_send, ox_recv,
    a_send, a_recv, z_send, z_recv, r_send, r_recv, f_send, f_recv,
):
    ctx = lax.axis_index("ctx")
    t = lax.axis_index("tp")
    z, x, y, c = ctx // NX, ctx % NX, t // 2, t % 2
    partner = 2 * y + 1 - c
    head = 8 * z + y

    loads = [
        pltpu.make_async_copy(q_ref, qv, in_sem.at[0]),
        pltpu.make_async_copy(blocks_ref, blocks, in_sem.at[1]),
        pltpu.make_async_copy(cols_ref.at[aligned(8 * z, 8)], cols8, in_sem.at[2]),
        pltpu.make_async_copy(offs_ref.at[aligned(8 * z, 8)], offs8, in_sem.at[3]),
    ]
    for copy in loads:
        copy.start()

    barrier = pltpu.get_barrier_semaphore()

    def greet(to_ctx, to_tp):
        pl.semaphore_signal(barrier, inc=1, device_id=(to_ctx, to_tp), device_id_type=MESH)

    for d in range(1, NT):
        greet(ctx, (t + d) % NT)
    for d in range(1, NZ):
        for cc in range(2):
            greet(((z + d) % NZ) * NX + x, 2 * y + cc)
    for d in range(1, NX):
        greet(z * NX + (x + d) % NX, t)

    loads[0].wait()
    for yy in range(NY):
        for g in range(KVH):
            at = (8 * g + yy) * HD
            qt[g, yy] = qv[:, at : at + HD]
    share = 2 * (y % 2) + c
    other = 2 * (1 - y % 2) + c

    def piece(zz, i, s):
        return kvb.at[zz, i, aligned(128 * s, 128)]

    rows = aligned(128 * share, 128)
    dense = []
    for i, ref in enumerate((k_ref, v_ref)):
        pltpu.make_async_copy(
            ref.at[rows, aligned(HD * z, HD)], piece(z, i, share), kz_recv.at[2 * z + i]
        ).start()
        for d in range(1, NZ):
            cols = aligned(HD * ((z + d) % NZ), HD)
            dense.append(pltpu.make_async_copy(ref.at[rows, cols], kl.at[i, d], in_sem.at[5 + 8 * i + d]))
            dense[-1].start()
    w_own = pltpu.make_async_copy(w_ref, wv.at[c, x], in_sem.at[4])
    w_own.start()

    for copy in dense:
        copy.wait()
    pl.semaphore_wait(barrier, NT - 1 + 2 * (NZ - 1) + NX - 1)

    q1 = [
        remote(qt.at[(z + d) % NZ], qs.at[z], q1_send.at[d], q1_recv, ((z + d) % NZ) * NX + x, t)
        for d in range(1, NZ)
    ]
    for copy in q1:
        copy.start()
    pltpu.make_async_copy(qt.at[z], qs.at[z], q1_recv).start()

    kz = []
    for d in (1, 7, 2, 6, 3, 5, 4):
        g = (z + d) % NZ
        for i in range(2):
            copy = remote(
                kl.at[i, d], piece(z, i, share),
                kz_send.at[2 * d + i], kz_recv.at[2 * z + i], g * NX + x, t,
            )
            copy.start()
            kz.append(copy)

    def y_copy(zz, i):
        to = (y + 1) % NY if i == 0 else (y + NY - 1) % NY
        ref = piece(zz, i, share)
        return remote(ref, ref, ky_send.at[2 * zz + i], ky_recv.at[2 * zz + i], ctx, 2 * to + c)

    def core_copy(zz, i, s, n):
        ref = piece(zz, i, s)
        return remote(ref, ref, kc_send.at[4 * zz + 2 * n + i], kc_recv.at[zz], ctx, partner)

    def forward_own(i):
        zz = (z + by_distance(i)) % NZ
        for kv in range(2):
            arrived(piece(zz, kv, share), kz_recv.at[2 * zz + kv])
            y_copy(zz, kv).start()
            core_copy(zz, kv, share, 0).start()

    def forward_other(i):
        zz = (z + by_distance(i)) % NZ
        for kv in range(2):
            arrived(piece(zz, kv, other), ky_recv.at[2 * zz + kv])
            core_copy(zz, kv, other, 1).start()

    forward_own(0)

    for copy in loads[1:]:
        copy.wait()
    fill_masks(
        kind_ref[head] == 1, count_ref[head], head, x, y, blocks, cols8, offs8, row_bias, tile_bias
    )
    top[...] = jnp.full((NX, 256, 128), MASKED, F32)
    total[...] = jnp.zeros((NX, 256, 128), F32)
    mixed[...] = jnp.zeros((NX, 256, HD), F32)

    arrived(qs, q1_recv)
    for yy in range(NY):
        for zz in range(NZ):
            qy[yy, zz] = qs[zz, yy]
    q2 = []
    for d in range(1, NT):
        tt = (t + d) % NT
        src = qy.at[tt // 2, pl.ds(4 * (tt % 2), 4)]
        q2.append(remote(src, q4.at[t], q2_send.at[d], q2_recv, ctx, tt))
        q2[-1].start()
    pltpu.make_async_copy(qy.at[y, pl.ds(4 * c, 4)], q4.at[t], q2_recv).start()

    forward_own(1)
    forward_own(2)
    forward_other(0)

    arrived(q4, q2_recv)
    for zl in range(4):
        for tt in range(NT):
            qf[zl, 4 * tt : 4 * tt + 4, :] = q4[tt, zl].astype(F32)
    qb[x] = qf[...].astype(BF16)
    qx = [
        remote(qb.at[x], qb.at[x], qx_send.at[d], qx_recv.at[d], z * NX + (x + d) % NX, t)
        for d in range(1, NX)
    ]
    for copy in qx:
        copy.start()

    wx = [
        remote(w_ref, wv.at[c, x], w_send.at[d], w_recv.at[d], z * NX + (x + d) % NX, t)
        for d in (1, 3)
    ]
    wc = [remote(w_ref, wv.at[c, x], wc_send.at[0], wc_recv, ctx, partner)]
    for copy in wx + wc:
        copy.start()

    def w_relay(d):
        ref = wv.at[c, (x + NX - d) % NX, pl.ds(64 * (d - 1), 128)]
        return remote(ref, ref, w_send.at[d - 1], w_recv.at[d - 1], z * NX + (x + d) % NX, t)

    def w_core(d):
        ref = wv.at[c, (x + NX - d) % NX]
        return remote(ref, ref, wc_send.at[d], wc_recv, ctx, partner)

    for i in range(3, 7):
        forward_own(i)
        forward_other(i - 2)
    for d in range(1, NX):
        arrived(qb.at[(x + NX - d) % NX], qx_recv.at[d])
    forward_own(7)

    def chunk(zz, band):
        keys = kvb[zz, 0]
        values = kvb[zz, 1]

        queries = qb[...].reshape(1024, HD)
        s = lax.dot_general(queries, keys, (((1,), (1,)), ((), ())), preferred_element_type=F32)
        weights = []
        factors = []
        for n in range(16):
            xx, zl = n // 4, n % 4
            b = 16 * c + 4 * zl + xx
            old = top[xx, 64 * zl : 64 * zl + 64]
            tiles = []
            high = None
            for w in range(4):
                bias = row_bias[4 * zz + w, pl.ds(b, 1), :]
                if band:
                    which = 225 + b - 8 * (4 * zz + x) - 2 * w
                    bias = jnp.maximum(bias, tile_bias[jnp.clip(which, 0, 11)])
                tile = s[64 * n : 64 * n + 64, 128 * w : 128 * w + 128] * SCALE + bias
                high = tile if high is None else jnp.maximum(high, tile)
                tiles.append(tile)
            new = jnp.maximum(old, jnp.max(high, axis=1, keepdims=True))
            top[xx, 64 * zl : 64 * zl + 64] = new
            factor = jnp.exp2(old - new)
            tiles = [jnp.exp2(tile - new) for tile in tiles]
            total[xx, 64 * zl : 64 * zl + 64] = total[xx, 64 * zl : 64 * zl + 64] * factor + (
                (tiles[0] + tiles[1]) + (tiles[2] + tiles[3])
            )
            factors.append(factor)
            weights.append(jnp.concatenate([tile.astype(BF16) for tile in tiles], axis=1))
        added = jnp.dot(jnp.concatenate(weights, axis=0), values, preferred_element_type=F32)
        for n in range(16):
            at = (n // 4, pl.ds(64 * (n % 4), 64))
            mixed[at] = mixed[at] * factors[n] + added[64 * n : 64 * n + 64]

    def step(i, carry):
        zz = (z + by_distance(i)) % NZ

        @pl.when(i < NZ - 5)
        def _():
            forward_other(i + 5)

        @pl.when(i == 5)
        def _():
            for d in (1, 3):
                arrived(wv.at[c, (x + NX - d) % NX], w_recv.at[d])
                w_relay(d).start()
                w_core(d).start()

        arrived(kvb.at[zz, 0], kc_recv.at[zz])

        @pl.when(zz >= 6)
        def _():
            chunk(zz, True)

        @pl.when(zz < 6)
        def _():
            chunk(zz, False)

        return carry

    lax.fori_loop(0, NZ, step, 0)

    def st_copy(d):
        xx = (x + d) % NX
        return remote(st_out.at[xx], sb.at[d], st_send.at[d], st_recv.at[d], z * NX + xx, t)

    def o_copy(i, d):
        xx = (x + d) % NX
        return remote(
            o_out.at[xx, i], ob.at[d, i], ox_send.at[4 * i + d], ox_recv.at[4 * i + d], z * NX + xx, t
        )

    for d in (2, 1, 3, 0):
        xx = (x + d) % NX
        amount = jnp.sum(total[xx], axis=1, keepdims=True)
        o_out[xx] = (mixed[xx] / amount).astype(BF16).reshape(4, 64, HD)
        st_out[xx] = (top[xx] + jnp.log2(amount)).T[:8, :]
        if d:
            st_copy(d).start()
            o_copy(z % 4, d).start()
    for j in range(1, 4):
        for d in (2, 1, 3):
            o_copy((z + j) % 4, d).start()
    for d in range(1, NX):
        arrived(sb.at[d], st_recv.at[d])
    levels = [st_out[x]] + [sb[d] for d in range(1, NX)]
    best = jnp.maximum(jnp.maximum(levels[0], levels[1]), jnp.maximum(levels[2], levels[3]))
    parts = [jnp.exp2(level - best) for level in levels]
    amount = (parts[0] + parts[1]) + (parts[2] + parts[3])
    parts = [p / amount for p in parts]
    share_of[...] = jnp.concatenate(parts + [jnp.zeros((96, 256), F32)], axis=0).T

    def a_copy(i, d):
        ref = ab.at[i, y]
        return remote(ref, ref, a_send.at[8 * i + d], a_recv.at[i], ctx, 2 * ((y + d) % NY) + c)

    for j in range(4):
        i = (z + j) % 4
        part_share = share_of[aligned(64 * i, 64), :]
        joined = part_share[:, 0:1] * o_out[x, i].astype(F32)
        for d in range(1, NX):
            arrived(ob.at[d, i], ox_recv.at[4 * i + d])
            joined = joined + part_share[:, 8 * d : 8 * d + 1] * ob[d, i].astype(F32)
        ab[i, y] = joined.astype(BF16)
        for d in (4, 3, 5, 2, 6, 1, 7):
            a_copy(i, d).start()

    for h in range(2):
        arrived(wv.at[c, (x + 2) % NX, pl.ds(128 * h, 128)], w_recv.at[2 * h])
    w_core(2).start()
    arrived(wv.at[0], wc_recv)
    w_own.wait()

    def z_copy(j, cc):
        to = (4 * c + (z + j) % 4) * NX + x
        return remote(
            part.at[j, cc], early.at[2 * j + z // 4], z_send.at[2 * j + cc], z_recv, to, 2 * y + cc
        )

    def row_copy(j, d):
        to = (4 * c + (z + j) % 4) * NX + x
        tt = (t + d) % NT
        return remote(
            pieces.at[j - 2, tt], late.at[2 * (j - 2) + z // 4, y],
            r_send.at[NT * (j - 2) + d], r_recv, to, tt,
        )

    for j in range(4):
        i = (z + j) % 4
        arrived(ab.at[i, pl.ds(0, NY - 1)], a_recv.at[i])
        features = jnp.concatenate([ab[i, yy] for yy in range(NY)], axis=1)
        for cc in range(2):
            weight = wv[cc].reshape(1024, 512)
            rows = jnp.dot(features, weight, preferred_element_type=F32)
            if j >= 2:
                for tt in range(NT):
                    pieces[j - 2, tt, :, 512 * cc : 512 * cc + 512] = rows[4 * tt : 4 * tt + 4, :].astype(BF16)
                continue
            part[j, cc] = rows.astype(BF16)
            if j:
                z_copy(j, cc).start()
                continue
            mine = jnp.logical_and(4 * c + i == z, cc == c)

            @pl.when(jnp.logical_not(mine))
            def _():
                z_copy(0, cc).start()

            @pl.when(mine)
            def _():
                pltpu.make_async_copy(part.at[0, cc], early.at[z // 4], z_recv).start()

        if j >= 2:
            for d in range(NT):
                row_copy(j, d).start()

    arrived(early, z_recv)
    summed = (early[0].astype(F32) + early[1].astype(F32)) + (early[2].astype(F32) + early[3].astype(F32))
    for tt in range(NT):
        fb[tt] = summed[4 * tt : 4 * tt + 4, :].astype(BF16)
    last = [
        remote(fb.at[(t + d) % NT], fr.at[t], f_send.at[d], f_recv, ctx, (t + d) % NT)
        for d in range(1, NT)
    ]
    for copy in last:
        copy.start()
    pltpu.make_async_copy(fb.at[t], fr.at[t], f_recv).start()

    for copy in q1 + q2 + kz + qx + wx + wc:
        copy.wait_send()
    for d in range(1, NX):
        w_core(d).wait_send()
        st_copy(d).wait_send()
        for i in range(4):
            o_copy(i, d).wait_send()
    for d in (1, 3):
        w_relay(d).wait_send()

    def sent(zz, carry):
        for kv in range(2):
            y_copy(zz, kv).wait_send()
            core_copy(zz, kv, share, 0).wait_send()
            core_copy(zz, kv, other, 1).wait_send()
        return carry

    lax.fori_loop(0, NZ, sent, 0)
    for i in range(4):
        for d in range(1, NY):
            a_copy(i, d).wait_send()
    for cc in range(2):
        mine = jnp.logical_and(4 * c + z % 4 == z, cc == c)

        @pl.when(jnp.logical_not(mine))
        def _():
            z_copy(0, cc).wait_send()

        z_copy(1, cc).wait_send()
    for j in (2, 3):
        for d in range(NT):
            row_copy(j, d).wait_send()
    for copy in last:
        copy.wait_send()

    arrived(late, r_recv)
    arrived(fr, f_recv)
    for tt in range(NT):
        summed = fr[tt].astype(F32)
        for e in range(4):
            summed = summed + late[e, tt // 2, :, 512 * (tt % 2) : 512 * (tt % 2) + 512].astype(F32)
        out_ref[:, 512 * tt : 512 * tt + 512] = summed.astype(BF16)


def layer(q, k, v, w, kinds, counts, blocks, cols, offs):
    dma = pltpu.SemaphoreType.DMA
    hbm = pl.BlockSpec(memory_space=pltpu.HBM)
    smem = pl.BlockSpec(memory_space=pltpu.SMEM)
    vmem = pltpu.VMEM
    return pl.pallas_call(
        layer_kernel,
        out_shape=jax.ShapeDtypeStruct((4, 8192), BF16),
        in_specs=[hbm, hbm, hbm, hbm, smem, smem, hbm, hbm, hbm],
        out_specs=pl.BlockSpec(memory_space=pltpu.VMEM),
        scratch_shapes=[
            vmem((4, 8192), BF16),
            vmem((KVH, NY, 4, HD), BF16),
            vmem((NZ, NY, 4, HD), BF16),
            vmem((NY, NZ, 4, HD), BF16),
            vmem((NT, 4, 4, HD), BF16),
            vmem((4, 64, HD), F32),
            vmem((NX, 4, 64, HD), BF16),
            vmem((2, NZ, 128, HD), BF16),
            vmem((NZ, 2, 512, HD), BF16),
            vmem((2, NX, 256, 512), BF16),
            vmem((32, 16, H), jnp.int32),
            vmem((8, 1024), jnp.int32),
            vmem((8, 128), jnp.int32),
            vmem((32, 32, 128), F32),
            vmem((12, 64, 128), F32),
            vmem((NX, 256, 128), F32),
            vmem((NX, 256, 128), F32),
            vmem((NX, 256, HD), F32),
            vmem((NX, 4, 64, HD), BF16),
            vmem((NX, 8, 256), F32),
            vmem((NX, 4, 64, HD), BF16),
            vmem((NX, 8, 256), F32),
            vmem((256, 128), F32),
            vmem((4, NY, 64, HD), BF16),
            vmem((2, 2, 64, 512), BF16),
            vmem((4, 64, 512), BF16),
            vmem((2, NT, 4, 1024), BF16),
            vmem((4, NY, 4, 1024), BF16),
            vmem((NT, 4, 512), BF16),
            vmem((NT, 4, 512), BF16),
            dma((21,)),
            dma((8,)), dma, dma((16,)), dma, dma((4,)), dma((4,)),
            dma((16,)), dma((16,)), dma((16,)), dma((16,)), dma((32,)), dma((8,)),
            dma((4,)), dma((4,)), dma((4,)), dma, dma((4,)), dma((4,)), dma((16,)), dma((16,)),
            dma((32,)), dma((4,)), dma((4,)), dma, dma((32,)), dma, dma((16,)), dma,
        ],
        compiler_params=pltpu.CompilerParams(
            collective_id=0, has_side_effects=True, vmem_limit_bytes=56_450_000
        ),
        name="layer",
    )(q, k, v, w, kinds, counts, blocks, cols, offs)


def shards(q, k, v, w, kinds, counts, blocks, cols, offs):
    return layer(q, k, v, w, kinds, counts, blocks.transpose(1, 2, 0), cols, offs)


def solution(mesh):
    return jax.shard_map(
        shards,
        mesh=mesh,
        in_specs=(
            P(("ctx", "tp"), None),
            P("ctx", None),
            P("ctx", None),
            P("ctx", "tp"),
            P(),
            P(),
            P(),
            P(),
            P(),
        ),
        out_specs=P(("ctx", "tp"), None),
        check_vma=False,
    )
```

```python
import math

import jax
import jax.numpy as jnp
from jax import lax
from jax.experimental import pallas as pl
from jax.experimental.pallas import tpu as pltpu
from jax.sharding import PartitionSpec as P

H = 64
KVH = 8
HD = 128
NX, NZ, NY = 4, 8, 8
NT = 2 * NY
MASKED = -1e30
MESH = pl.DeviceIdType.MESH
F32 = jnp.float32
BF16 = jnp.bfloat16
SCALE = math.log2(math.e) / math.sqrt(HD)


def remote(src, dst, send_sem, recv_sem, ctx, tp):
    return pltpu.make_async_remote_copy(
        src_ref=src,
        dst_ref=dst,
        send_sem=send_sem,
        recv_sem=recv_sem,
        device_id=(ctx, tp),
        device_id_type=MESH,
    )


def arrived(ref, sem):
    pltpu.make_async_copy(ref, ref, sem).wait()


def lanes(shape):
    return lax.broadcasted_iota(jnp.int32, shape, len(shape) - 1)


def subs(shape):
    return lax.broadcasted_iota(jnp.int32, shape, 0)


def aligned(start, size):
    return pl.ds(pl.multiple_of(start, size), size)


def by_distance(i):
    odd = i % 2
    return odd * ((i + 1) // 2) + (1 - odd) * ((8 - i // 2) % 8)


def member_rows(values, first_row):
    high = jnp.where(values // 128 == first_row, 1.0, 0.0).astype(BF16)
    low = jnp.where(values % 128 == subs((128, values.shape[1])), 1.0, 0.0).astype(BF16)
    found = lax.dot_general(high, low, (((1,), (1,)), ((), ())), preferred_element_type=F32)
    return jnp.where(found > 0.5, 0.0, MASKED)


def fill_masks(slash, count, head, x, y, blocks, cols8, offs8, row_bias, tile_bias):
    tile = subs((32, 1024))
    tile = 16 * (tile // 4) + 4 * x + tile % 4
    vertical = member_rows(cols8[pl.ds(y, 1), :], tile)
    ids = jnp.where(lanes((32, 16, H)) == head, blocks[...].astype(F32), 0.0)
    ids = jnp.sum(ids, axis=2, keepdims=True)
    at = lanes((1, 1, 128))
    block = (8 * (4 * (at // 8) + x) + at % 8).astype(F32)
    turn = lax.broadcasted_iota(jnp.int32, (32, 16, 128), 1)
    hit = jnp.where(ids == block, 0.0, MASKED)
    hit = jnp.where(turn >= 1, jnp.where(turn < count, hit, MASKED), MASKED)
    chosen = jnp.max(hit, axis=1)
    left = lanes((32, 128)) < 64
    for i in range(32):
        pair = jnp.where(left, chosen[:, 2 * i : 2 * i + 1], chosen[:, 2 * i + 1 : 2 * i + 2])
        row_bias[i] = jnp.where(slash, jnp.broadcast_to(vertical[i : i + 1, :], (32, 128)), pair)
    rev = 511 - offs8[pl.ds(y, 1), :]
    phases = [member_rows(rev + 128 + 64 * phase, subs((8, 128))) for phase in range(2)]
    back = subs((64, 128)) - lanes((64, 128))
    right = lanes((64, 128)) >= 64
    nothing = jnp.full((64, 128), MASKED, F32)
    tile_bias[0] = nothing
    tile_bias[11] = nothing
    for i in range(10):
        start = 576 - 64 * i
        phase = (start // 64) % 2
        first = (start + 64 * phase) // 128
        pair = jnp.concatenate(
            [phases[phase][first : first + 1, :], phases[phase][first + 1 : first + 2, :]], axis=1
        )
        rolled = pltpu.roll(jnp.broadcast_to(pair, (64, 256)), 256 - 63, 1, stride=1, stride_axis=0)
        own = nothing
        if i == 0:
            own = jnp.where(right, MASKED, jnp.where(back >= 0, 0.0, MASKED))
        if i == 1:
            own = jnp.where(right, jnp.where(back + 64 >= 0, 0.0, MASKED), MASKED)
        tile_bias[i + 1] = jnp.where(slash, rolled[:, :128], own)


def layer_kernel(
    q_ref, k_ref, v_ref, w_ref, kind_ref, count_ref, blocks_ref, cols_ref, offs_ref,
    out_ref,
    qv, qt, qs, qy, q4, qf, qb, kl, kvb, wv, blocks, cols8, offs8, row_bias, tile_bias,
    top, total, mixed, o_out, st_out, ob, sb, share_of, ab, part, early, pieces, late, fb, fr,
    in_sem, q1_send, q1_recv, q2_send, q2_recv, qx_send, qx_recv,
    kz_send, kz_recv, ky_send, ky_recv, kc_send, kc_recv,
    w_send, w_recv, wc_send, wc_recv, st_send, st_recv, ox_send, ox_recv,
    a_send, a_recv, z_send, z_recv, r_send, r_recv, f_send, f_recv,
):
    ctx = lax.axis_index("ctx")
    t = lax.axis_index("tp")
    z, x, y, c = ctx // NX, ctx % NX, t // 2, t % 2
    partner = 2 * y + 1 - c
    head = 8 * z + y

    loads = [
        pltpu.make_async_copy(q_ref, qv, in_sem.at[0]),
        pltpu.make_async_copy(blocks_ref, blocks, in_sem.at[1]),
        pltpu.make_async_copy(cols_ref.at[aligned(8 * z, 8)], cols8, in_sem.at[2]),
        pltpu.make_async_copy(offs_ref.at[aligned(8 * z, 8)], offs8, in_sem.at[3]),
    ]
    for copy in loads:
        copy.start()

    barrier = pltpu.get_barrier_semaphore()

    def greet(to_ctx, to_tp):
        pl.semaphore_signal(barrier, inc=1, device_id=(to_ctx, to_tp), device_id_type=MESH)

    for d in range(1, NT):
        greet(ctx, (t + d) % NT)
    for d in range(1, NZ):
        for cc in range(2):
            greet(((z + d) % NZ) * NX + x, 2 * y + cc)
    for d in range(1, NX):
        greet(z * NX + (x + d) % NX, t)

    loads[0].wait()
    for yy in range(NY):
        for g in range(KVH):
            at = (8 * g + yy) * HD
            qt[g, yy] = qv[:, at : at + HD]
    share = 2 * (y % 2) + c
    other = 2 * (1 - y % 2) + c

    def piece(zz, i, s):
        return kvb.at[zz, i, aligned(128 * s, 128)]

    rows = aligned(128 * share, 128)
    dense = []
    for i, ref in enumerate((k_ref, v_ref)):
        pltpu.make_async_copy(
            ref.at[rows, aligned(HD * z, HD)], piece(z, i, share), kz_recv.at[2 * z + i]
        ).start()
        for d in range(1, NZ):
            cols = aligned(HD * ((z + d) % NZ), HD)
            dense.append(pltpu.make_async_copy(ref.at[rows, cols], kl.at[i, d], in_sem.at[5 + 8 * i + d]))
            dense[-1].start()
    w_own = pltpu.make_async_copy(w_ref, wv.at[c, x], in_sem.at[4])
    w_own.start()

    for copy in dense:
        copy.wait()
    pl.semaphore_wait(barrier, NT - 1 + 2 * (NZ - 1) + NX - 1)

    q1 = [
        remote(qt.at[(z + d) % NZ], qs.at[z], q1_send.at[d], q1_recv, ((z + d) % NZ) * NX + x, t)
        for d in range(1, NZ)
    ]
    for copy in q1:
        copy.start()
    pltpu.make_async_copy(qt.at[z], qs.at[z], q1_recv).start()

    kz = []
    for d in (1, 7, 2, 6, 3, 5, 4):
        g = (z + d) % NZ
        for i in range(2):
            copy = remote(
                kl.at[i, d], piece(z, i, share),
                kz_send.at[2 * d + i], kz_recv.at[2 * z + i], g * NX + x, t,
            )
            copy.start()
            kz.append(copy)

    def y_copy(zz, i):
        to = (y + 1) % NY if i == 0 else (y + NY - 1) % NY
        ref = piece(zz, i, share)
        return remote(ref, ref, ky_send.at[2 * zz + i], ky_recv.at[2 * zz + i], ctx, 2 * to + c)

    def core_copy(zz, i, s, n):
        ref = piece(zz, i, s)
        return remote(ref, ref, kc_send.at[4 * zz + 2 * n + i], kc_recv.at[zz], ctx, partner)

    def forward_own(i):
        zz = (z + by_distance(i)) % NZ
        for kv in range(2):
            arrived(piece(zz, kv, share), kz_recv.at[2 * zz + kv])
            y_copy(zz, kv).start()
            core_copy(zz, kv, share, 0).start()

    def forward_other(i):
        zz = (z + by_distance(i)) % NZ
        for kv in range(2):
            arrived(piece(zz, kv, other), ky_recv.at[2 * zz + kv])
            core_copy(zz, kv, other, 1).start()

    forward_own(0)

    for copy in loads[1:]:
        copy.wait()
    fill_masks(
        kind_ref[head] == 1, count_ref[head], head, x, y, blocks, cols8, offs8, row_bias, tile_bias
    )
    top[...] = jnp.full((NX, 256, 128), MASKED, F32)
    total[...] = jnp.zeros((NX, 256, 128), F32)
    mixed[...] = jnp.zeros((NX, 256, HD), F32)

    arrived(qs, q1_recv)
    for yy in range(NY):
        for zz in range(NZ):
            qy[yy, zz] = qs[zz, yy]
    q2 = []
    for d in range(1, NT):
        tt = (t + d) % NT
        src = qy.at[tt // 2, pl.ds(4 * (tt % 2), 4)]
        q2.append(remote(src, q4.at[t], q2_send.at[d], q2_recv, ctx, tt))
        q2[-1].start()
    pltpu.make_async_copy(qy.at[y, pl.ds(4 * c, 4)], q4.at[t], q2_recv).start()

    forward_own(1)
    forward_own(2)
    forward_other(0)

    arrived(q4, q2_recv)
    for zl in range(4):
        for tt in range(NT):
            qf[zl, 4 * tt : 4 * tt + 4, :] = q4[tt, zl].astype(F32)
    qb[x] = qf[...].astype(BF16)
    qx = [
        remote(qb.at[x], qb.at[x], qx_send.at[d], qx_recv.at[d], z * NX + (x + d) % NX, t)
        for d in range(1, NX)
    ]
    for copy in qx:
        copy.start()

    wx = [
        remote(w_ref, wv.at[c, x], w_send.at[d], w_recv.at[d], z * NX + (x + d) % NX, t)
        for d in (1, 3)
    ]
    wc = [remote(w_ref, wv.at[c, x], wc_send.at[0], wc_recv, ctx, partner)]
    for copy in wx + wc:
        copy.start()

    def w_relay(d):
        ref = wv.at[c, (x + NX - d) % NX, pl.ds(64 * (d - 1), 128)]
        return remote(ref, ref, w_send.at[d - 1], w_recv.at[d - 1], z * NX + (x + d) % NX, t)

    def w_core(d):
        ref = wv.at[c, (x + NX - d) % NX]
        return remote(ref, ref, wc_send.at[d], wc_recv, ctx, partner)

    def chunk(zz, band, groups):
        keys = kvb[zz, 0]
        values = kvb[zz, 1]

        queries = [qb[(x + k) % NX].reshape(256, HD) for k in groups]
        queries = queries[0] if len(queries) == 1 else jnp.concatenate(queries, axis=0)
        s = lax.dot_general(queries, keys, (((1,), (1,)), ((), ())), preferred_element_type=F32)
        weights = []
        factors = []
        for n in range(4 * len(groups)):
            xx, zl = (x + groups[n // 4]) % NX, n % 4
            b = 16 * c + 4 * zl + xx
            old = top[xx, 64 * zl : 64 * zl + 64]
            tiles = []
            high = None
            for w in range(4):
                bias = row_bias[4 * zz + w, pl.ds(b, 1), :]
                if band:
                    which = 225 + b - 8 * (4 * zz + x) - 2 * w
                    bias = jnp.maximum(bias, tile_bias[jnp.clip(which, 0, 11)])
                tile = s[64 * n : 64 * n + 64, 128 * w : 128 * w + 128] * SCALE + bias
                high = tile if high is None else jnp.maximum(high, tile)
                tiles.append(tile)
            new = jnp.maximum(old, jnp.max(high, axis=1, keepdims=True))
            top[xx, 64 * zl : 64 * zl + 64] = new
            factor = jnp.exp2(old - new)
            tiles = [jnp.exp2(tile - new) for tile in tiles]
            total[xx, 64 * zl : 64 * zl + 64] = total[xx, 64 * zl : 64 * zl + 64] * factor + (
                (tiles[0] + tiles[1]) + (tiles[2] + tiles[3])
            )
            factors.append(factor)
            weights.append(jnp.concatenate([tile.astype(BF16) for tile in tiles], axis=1))
        added = jnp.dot(jnp.concatenate(weights, axis=0), values, preferred_element_type=F32)
        for n in range(4 * len(groups)):
            at = ((x + groups[n // 4]) % NX, pl.ds(64 * (n % 4), 64))
            mixed[at] = mixed[at] * factors[n] + added[64 * n : 64 * n + 64]

    def attend(zz, groups):
        @pl.when(zz >= 6)
        def _():
            chunk(zz, True, groups)

        @pl.when(zz < 6)
        def _():
            chunk(zz, False, groups)

    def own_step(i, carry):
        zz = (z + by_distance(i)) % NZ

        @pl.when(i < NZ - 3)
        def _():
            forward_own(i + 3)

        forward_other(i + 1)
        arrived(kvb.at[zz, 0], kc_recv.at[zz])
        attend(zz, (0,))
        return carry

    lax.fori_loop(0, 6, own_step, 0)
    forward_other(7)
    for d in range(1, NX):
        arrived(qb.at[(x + NX - d) % NX], qx_recv.at[d])

    def rest_step(i, carry):
        @pl.when(i == 3)
        def _():
            for d in (1, 3):
                arrived(wv.at[c, (x + NX - d) % NX], w_recv.at[d])
                w_relay(d).start()
                w_core(d).start()

        attend((z + by_distance(i)) % NZ, (1, 2, 3))
        return carry

    lax.fori_loop(0, 6, rest_step, 0)

    def late_step(i, carry):
        zz = (z + by_distance(i)) % NZ
        arrived(kvb.at[zz, 0], kc_recv.at[zz])
        attend(zz, (0, 1, 2, 3))
        return carry

    lax.fori_loop(6, NZ, late_step, 0)

    def st_copy(d):
        xx = (x + d) % NX
        return remote(st_out.at[xx], sb.at[d], st_send.at[d], st_recv.at[d], z * NX + xx, t)

    def o_copy(i, d):
        xx = (x + d) % NX
        return remote(
            o_out.at[xx, i], ob.at[d, i], ox_send.at[4 * i + d], ox_recv.at[4 * i + d], z * NX + xx, t
        )

    for d in (2, 1, 3, 0):
        xx = (x + d) % NX
        amount = jnp.sum(total[xx], axis=1, keepdims=True)
        o_out[xx] = (mixed[xx] / amount).astype(BF16).reshape(4, 64, HD)
        st_out[xx] = (top[xx] + jnp.log2(amount)).T[:8, :]
        if d:
            st_copy(d).start()
            o_copy(z % 4, d).start()
    for j in range(1, 4):
        for d in (2, 1, 3):
            o_copy((z + j) % 4, d).start()
    for d in range(1, NX):
        arrived(sb.at[d], st_recv.at[d])
    levels = [st_out[x]] + [sb[d] for d in range(1, NX)]
    best = jnp.maximum(jnp.maximum(levels[0], levels[1]), jnp.maximum(levels[2], levels[3]))
    parts = [jnp.exp2(level - best) for level in levels]
    amount = (parts[0] + parts[1]) + (parts[2] + parts[3])
    parts = [p / amount for p in parts]
    share_of[...] = jnp.concatenate(parts + [jnp.zeros((96, 256), F32)], axis=0).T

    def a_copy(i, d):
        ref = ab.at[i, y]
        return remote(ref, ref, a_send.at[8 * i + d], a_recv.at[i], ctx, 2 * ((y + d) % NY) + c)

    for j in range(4):
        i = (z + j) % 4
        part_share = share_of[aligned(64 * i, 64), :]
        joined = part_share[:, 0:1] * o_out[x, i].astype(F32)
        for d in range(1, NX):
            arrived(ob.at[d, i], ox_recv.at[4 * i + d])
            joined = joined + part_share[:, 8 * d : 8 * d + 1] * ob[d, i].astype(F32)
        ab[i, y] = joined.astype(BF16)
        for d in (4, 3, 5, 2, 6, 1, 7):
            a_copy(i, d).start()

    for h in range(2):
        arrived(wv.at[c, (x + 2) % NX, pl.ds(128 * h, 128)], w_recv.at[2 * h])
    w_core(2).start()
    arrived(wv.at[0], wc_recv)
    w_own.wait()

    def z_copy(j, cc):
        to = (4 * c + (z + j) % 4) * NX + x
        return remote(
            part.at[j, cc], early.at[2 * j + z // 4], z_send.at[2 * j + cc], z_recv, to, 2 * y + cc
        )

    def row_copy(j, d):
        to = (4 * c + (z + j) % 4) * NX + x
        tt = (t + d) % NT
        return remote(
            pieces.at[j - 2, tt], late.at[2 * (j - 2) + z // 4, y],
            r_send.at[NT * (j - 2) + d], r_recv, to, tt,
        )

    for j in range(4):
        i = (z + j) % 4
        arrived(ab.at[i, pl.ds(0, NY - 1)], a_recv.at[i])
        features = jnp.concatenate([ab[i, yy] for yy in range(NY)], axis=1)
        for cc in range(2):
            weight = wv[cc].reshape(1024, 512)
            rows = jnp.dot(features, weight, preferred_element_type=F32)
            if j >= 2:
                for tt in range(NT):
                    pieces[j - 2, tt, :, 512 * cc : 512 * cc + 512] = rows[4 * tt : 4 * tt + 4, :].astype(BF16)
                continue
            part[j, cc] = rows.astype(BF16)
            if j:
                z_copy(j, cc).start()
                continue
            mine = jnp.logical_and(4 * c + i == z, cc == c)

            @pl.when(jnp.logical_not(mine))
            def _():
                z_copy(0, cc).start()

            @pl.when(mine)
            def _():
                pltpu.make_async_copy(part.at[0, cc], early.at[z // 4], z_recv).start()

        if j >= 2:
            for d in range(NT):
                row_copy(j, d).start()

    arrived(early, z_recv)
    summed = (early[0].astype(F32) + early[1].astype(F32)) + (early[2].astype(F32) + early[3].astype(F32))
    for tt in range(NT):
        fb[tt] = summed[4 * tt : 4 * tt + 4, :].astype(BF16)
    last = [
        remote(fb.at[(t + d) % NT], fr.at[t], f_send.at[d], f_recv, ctx, (t + d) % NT)
        for d in range(1, NT)
    ]
    for copy in last:
        copy.start()
    pltpu.make_async_copy(fb.at[t], fr.at[t], f_recv).start()

    for copy in q1 + q2 + kz + qx + wx + wc:
        copy.wait_send()
    for d in range(1, NX):
        w_core(d).wait_send()
        st_copy(d).wait_send()
        for i in range(4):
            o_copy(i, d).wait_send()
    for d in (1, 3):
        w_relay(d).wait_send()

    def sent(zz, carry):
        for kv in range(2):
            y_copy(zz, kv).wait_send()
            core_copy(zz, kv, share, 0).wait_send()
            core_copy(zz, kv, other, 1).wait_send()
        return carry

    lax.fori_loop(0, NZ, sent, 0)
    for i in range(4):
        for d in range(1, NY):
            a_copy(i, d).wait_send()
    for cc in range(2):
        mine = jnp.logical_and(4 * c + z % 4 == z, cc == c)

        @pl.when(jnp.logical_not(mine))
        def _():
            z_copy(0, cc).wait_send()

        z_copy(1, cc).wait_send()
    for j in (2, 3):
        for d in range(NT):
            row_copy(j, d).wait_send()
    for copy in last:
        copy.wait_send()

    arrived(late, r_recv)
    arrived(fr, f_recv)
    for tt in range(NT):
        summed = fr[tt].astype(F32)
        for e in range(4):
            summed = summed + late[e, tt // 2, :, 512 * (tt % 2) : 512 * (tt % 2) + 512].astype(F32)
        out_ref[:, 512 * tt : 512 * tt + 512] = summed.astype(BF16)


def layer(q, k, v, w, kinds, counts, blocks, cols, offs):
    dma = pltpu.SemaphoreType.DMA
    hbm = pl.BlockSpec(memory_space=pltpu.HBM)
    smem = pl.BlockSpec(memory_space=pltpu.SMEM)
    vmem = pltpu.VMEM
    return pl.pallas_call(
        layer_kernel,
        out_shape=jax.ShapeDtypeStruct((4, 8192), BF16),
        in_specs=[hbm, hbm, hbm, hbm, smem, smem, hbm, hbm, hbm],
        out_specs=pl.BlockSpec(memory_space=pltpu.VMEM),
        scratch_shapes=[
            vmem((4, 8192), BF16),
            vmem((KVH, NY, 4, HD), BF16),
            vmem((NZ, NY, 4, HD), BF16),
            vmem((NY, NZ, 4, HD), BF16),
            vmem((NT, 4, 4, HD), BF16),
            vmem((4, 64, HD), F32),
            vmem((NX, 4, 64, HD), BF16),
            vmem((2, NZ, 128, HD), BF16),
            vmem((NZ, 2, 512, HD), BF16),
            vmem((2, NX, 256, 512), BF16),
            vmem((32, 16, H), jnp.int32),
            vmem((8, 1024), jnp.int32),
            vmem((8, 128), jnp.int32),
            vmem((32, 32, 128), F32),
            vmem((12, 64, 128), F32),
            vmem((NX, 256, 128), F32),
            vmem((NX, 256, 128), F32),
            vmem((NX, 256, HD), F32),
            vmem((NX, 4, 64, HD), BF16),
            vmem((NX, 8, 256), F32),
            vmem((NX, 4, 64, HD), BF16),
            vmem((NX, 8, 256), F32),
            vmem((256, 128), F32),
            vmem((4, NY, 64, HD), BF16),
            vmem((2, 2, 64, 512), BF16),
            vmem((4, 64, 512), BF16),
            vmem((2, NT, 4, 1024), BF16),
            vmem((4, NY, 4, 1024), BF16),
            vmem((NT, 4, 512), BF16),
            vmem((NT, 4, 512), BF16),
            dma((21,)),
            dma((8,)), dma, dma((16,)), dma, dma((4,)), dma((4,)),
            dma((16,)), dma((16,)), dma((16,)), dma((16,)), dma((32,)), dma((8,)),
            dma((4,)), dma((4,)), dma((4,)), dma, dma((4,)), dma((4,)), dma((16,)), dma((16,)),
            dma((32,)), dma((4,)), dma((4,)), dma, dma((32,)), dma, dma((16,)), dma,
        ],
        compiler_params=pltpu.CompilerParams(
            collective_id=0, has_side_effects=True, vmem_limit_bytes=56 * 1024 * 1024
        ),
        name="layer",
    )(q, k, v, w, kinds, counts, blocks, cols, offs)


def shards(q, k, v, w, kinds, counts, blocks, cols, offs):
    return layer(q, k, v, w, kinds, counts, blocks.transpose(1, 2, 0), cols, offs)


def solution(mesh):
    return jax.shard_map(
        shards,
        mesh=mesh,
        in_specs=(
            P(("ctx", "tp"), None),
            P("ctx", None),
            P("ctx", None),
            P("ctx", "tp"),
            P(),
            P(),
            P(),
            P(),
            P(),
        ),
        out_specs=P(("ctx", "tp"), None),
        check_vma=False,
    )
```

```python
import math

import jax
import jax.numpy as jnp
from jax import lax
from jax.experimental import pallas as pl
from jax.experimental.pallas import tpu as pltpu
from jax.sharding import PartitionSpec as P

H = 64
KVH = 8
HD = 128
NX, NZ, NY = 4, 8, 8
NT = 2 * NY
MASKED = -1e30
MESH = pl.DeviceIdType.MESH
F32 = jnp.float32
BF16 = jnp.bfloat16
SCALE = math.log2(math.e) / math.sqrt(HD)


def remote(src, dst, send_sem, recv_sem, ctx, tp):
    return pltpu.make_async_remote_copy(
        src_ref=src,
        dst_ref=dst,
        send_sem=send_sem,
        recv_sem=recv_sem,
        device_id=(ctx, tp),
        device_id_type=MESH,
    )


def arrived(ref, sem):
    pltpu.make_async_copy(ref, ref, sem).wait()


def lanes(shape):
    return lax.broadcasted_iota(jnp.int32, shape, len(shape) - 1)


def subs(shape):
    return lax.broadcasted_iota(jnp.int32, shape, 0)


def aligned(start, size):
    return pl.ds(pl.multiple_of(start, size), size)


def by_distance(i):
    odd = i % 2
    return odd * ((i + 1) // 2) + (1 - odd) * ((8 - i // 2) % 8)


def member_rows(values, first_row):
    high = jnp.where(values // 128 == first_row, 1.0, 0.0).astype(BF16)
    low = jnp.where(values % 128 == subs((128, values.shape[1])), 1.0, 0.0).astype(BF16)
    found = lax.dot_general(high, low, (((1,), (1,)), ((), ())), preferred_element_type=F32)
    return jnp.where(found > 0.5, 0.0, MASKED)


def fill_masks(slash, count, head, x, y, blocks, cols8, offs8, row_bias, tile_bias):
    tile = subs((32, 1024))
    tile = 16 * (tile // 4) + 4 * x + tile % 4
    vertical = member_rows(cols8[pl.ds(y, 1), :], tile)
    ids = jnp.where(lanes((32, 16, H)) == head, blocks[...].astype(F32), 0.0)
    ids = jnp.sum(ids, axis=2, keepdims=True)
    at = lanes((1, 1, 128))
    block = (8 * (4 * (at // 8) + x) + at % 8).astype(F32)
    turn = lax.broadcasted_iota(jnp.int32, (32, 16, 128), 1)
    hit = jnp.where(ids == block, 0.0, MASKED)
    hit = jnp.where(turn >= 1, jnp.where(turn < count, hit, MASKED), MASKED)
    chosen = jnp.max(hit, axis=1)
    left = lanes((32, 128)) < 64
    for i in range(32):
        pair = jnp.where(left, chosen[:, 2 * i : 2 * i + 1], chosen[:, 2 * i + 1 : 2 * i + 2])
        row_bias[i] = jnp.where(slash, jnp.broadcast_to(vertical[i : i + 1, :], (32, 128)), pair)
    rev = 511 - offs8[pl.ds(y, 1), :]
    phases = [member_rows(rev + 128 + 64 * phase, subs((8, 128))) for phase in range(2)]
    back = subs((64, 128)) - lanes((64, 128))
    right = lanes((64, 128)) >= 64
    nothing = jnp.full((64, 128), MASKED, F32)
    tile_bias[0] = nothing
    tile_bias[11] = nothing
    for i in range(10):
        start = 576 - 64 * i
        phase = (start // 64) % 2
        first = (start + 64 * phase) // 128
        pair = jnp.concatenate(
            [phases[phase][first : first + 1, :], phases[phase][first + 1 : first + 2, :]], axis=1
        )
        rolled = pltpu.roll(jnp.broadcast_to(pair, (64, 256)), 256 - 63, 1, stride=1, stride_axis=0)
        own = nothing
        if i == 0:
            own = jnp.where(right, MASKED, jnp.where(back >= 0, 0.0, MASKED))
        if i == 1:
            own = jnp.where(right, jnp.where(back + 64 >= 0, 0.0, MASKED), MASKED)
        tile_bias[i + 1] = jnp.where(slash, rolled[:, :128], own)


def layer_kernel(
    q_ref, k_ref, v_ref, w_ref, kind_ref, count_ref, blocks_ref, cols_ref, offs_ref,
    out_ref,
    qv, qt, qs, qy, q4, qf, qb, kl, kvb, wv, blocks, cols8, offs8, row_bias, tile_bias,
    top, total, mixed, o_out, st_out, ob, sb, share_of, ab, part, early, pieces, late, fb, fr,
    in_sem, q1_send, q1_recv, q2_send, q2_recv, qx_send, qx_recv,
    kz_send, kz_recv, ky_send, ky_recv, kc_send, kc_recv,
    w_send, w_recv, wc_send, wc_recv, st_send, st_recv, ox_send, ox_recv,
    a_send, a_recv, z_send, z_recv, r_send, r_recv, f_send, f_recv,
):
    ctx = lax.axis_index("ctx")
    t = lax.axis_index("tp")
    z, x, y, c = ctx // NX, ctx % NX, t // 2, t % 2
    partner = 2 * y + 1 - c
    head = 8 * z + y

    loads = [
        pltpu.make_async_copy(q_ref, qv, in_sem.at[0]),
        pltpu.make_async_copy(blocks_ref, blocks, in_sem.at[1]),
        pltpu.make_async_copy(cols_ref.at[aligned(8 * z, 8)], cols8, in_sem.at[2]),
        pltpu.make_async_copy(offs_ref.at[aligned(8 * z, 8)], offs8, in_sem.at[3]),
    ]
    barrier = pltpu.get_barrier_semaphore()

    def greet(to_ctx, to_tp):
        pl.semaphore_signal(barrier, inc=1, device_id=(to_ctx, to_tp), device_id_type=MESH)

    for d in (4, 3, 5, 2, 6, 1, 7):
        greet(((z + d) % NZ) * NX + x, t)
        for core in (c, 1 - c):
            greet(ctx, 2 * ((y + d) % NY) + core)
    for d in (2, 1, 3):
        greet(z * NX + (x + d) % NX, t)
    greet(ctx, partner)

    for copy in loads:
        copy.start()
    share = 2 * (y % 2) + c
    other = 2 * (1 - y % 2) + c

    def piece(zz, i, s):
        return kvb.at[zz, i, aligned(128 * s, 128)]

    rows = aligned(128 * share, 128)
    dense = []
    for i, ref in enumerate((k_ref, v_ref)):
        pltpu.make_async_copy(
            ref.at[rows, aligned(HD * z, HD)], piece(z, i, share), kz_recv.at[2 * z + i]
        ).start()
        for d in range(1, NZ):
            cols = aligned(HD * ((z + d) % NZ), HD)
            dense.append(pltpu.make_async_copy(ref.at[rows, cols], kl.at[i, d], in_sem.at[5 + 8 * i + d]))
            dense[-1].start()
    w_own = pltpu.make_async_copy(w_ref, wv.at[c, x], in_sem.at[4])
    w_own.start()

    loads[0].wait()
    for yy in range(NY):
        for g in range(KVH):
            at = (8 * g + yy) * HD
            qt[g, yy] = qv[:, at : at + HD]
    for copy in dense:
        copy.wait()
    pl.semaphore_wait(barrier, NT - 1 + NZ - 1 + NX - 1)

    q1 = [
        remote(qt.at[(z + d) % NZ], qs.at[z], q1_send.at[d], q1_recv, ((z + d) % NZ) * NX + x, t)
        for d in range(1, NZ)
    ]
    for copy in q1:
        copy.start()
    pltpu.make_async_copy(qt.at[z], qs.at[z], q1_recv).start()

    kz = []
    for d in (1, 7, 2, 6, 3, 5, 4):
        g = (z + d) % NZ
        for i in range(2):
            copy = remote(
                kl.at[i, d], piece(z, i, share),
                kz_send.at[2 * d + i], kz_recv.at[2 * z + i], g * NX + x, t,
            )
            copy.start()
            kz.append(copy)

    def y_copy(zz, i):
        to = (y + 1) % NY if i == 0 else (y + NY - 1) % NY
        ref = piece(zz, i, share)
        return remote(ref, ref, ky_send.at[2 * zz + i], ky_recv.at[2 * zz + i], ctx, 2 * to + c)

    def core_copy(zz, i, s, n):
        ref = piece(zz, i, s)
        return remote(ref, ref, kc_send.at[4 * zz + 2 * n + i], kc_recv.at[zz], ctx, partner)

    def forward_own(i):
        zz = (z + by_distance(i)) % NZ
        for kv in range(2):
            arrived(piece(zz, kv, share), kz_recv.at[2 * zz + kv])
            y_copy(zz, kv).start()
            core_copy(zz, kv, share, 0).start()

    def forward_other(i):
        zz = (z + by_distance(i)) % NZ
        for kv in range(2):
            arrived(piece(zz, kv, other), ky_recv.at[2 * zz + kv])
            core_copy(zz, kv, other, 1).start()

    forward_own(0)

    for copy in loads[1:]:
        copy.wait()
    fill_masks(
        kind_ref[head] == 1, count_ref[head], head, x, y, blocks, cols8, offs8, row_bias, tile_bias
    )
    top[...] = jnp.full((NX, 256, 128), MASKED, F32)
    total[...] = jnp.zeros((NX, 256, 128), F32)
    mixed[...] = jnp.zeros((NX, 256, HD), F32)

    arrived(qs, q1_recv)
    for yy in range(NY):
        for zz in range(NZ):
            qy[yy, zz] = qs[zz, yy]
    q2 = []
    for d in range(1, NT):
        tt = (t + d) % NT
        src = qy.at[tt // 2, pl.ds(4 * (tt % 2), 4)]
        q2.append(remote(src, q4.at[t], q2_send.at[d], q2_recv, ctx, tt))
        q2[-1].start()
    pltpu.make_async_copy(qy.at[y, pl.ds(4 * c, 4)], q4.at[t], q2_recv).start()

    arrived(q4, q2_recv)
    for zl in range(4):
        for tt in range(NT):
            qf[zl, 4 * tt : 4 * tt + 4, :] = q4[tt, zl].astype(F32)
    qb[x] = qf[...].astype(BF16)
    qx = [
        remote(qb.at[x], qb.at[x], qx_send.at[d], qx_recv.at[d], z * NX + (x + d) % NX, t)
        for d in range(1, NX)
    ]
    for copy in qx:
        copy.start()

    wx = [
        remote(w_ref, wv.at[c, x], w_send.at[d], w_recv.at[d], z * NX + (x + d) % NX, t)
        for d in (1, 3)
    ]
    wc = [remote(w_ref, wv.at[c, x], wc_send.at[0], wc_recv, ctx, partner)]
    for copy in wx + wc:
        copy.start()

    def w_relay(d):
        ref = wv.at[c, (x + NX - d) % NX, pl.ds(64 * (d - 1), 128)]
        return remote(ref, ref, w_send.at[d - 1], w_recv.at[d - 1], z * NX + (x + d) % NX, t)

    def w_core(d):
        ref = wv.at[c, (x + NX - d) % NX]
        return remote(ref, ref, wc_send.at[d], wc_recv, ctx, partner)

    forward_other(0)
    for i in range(1, 6):
        forward_own(i)
    for d in range(1, NX):
        arrived(qb.at[(x + NX - d) % NX], qx_recv.at[d])
    forward_own(6)
    forward_other(1)
    forward_own(7)
    forward_other(2)

    def chunk(zz, band):
        keys = kvb[zz, 0]
        values = kvb[zz, 1]

        queries = qb[...].reshape(1024, HD)
        s = lax.dot_general(queries, keys, (((1,), (1,)), ((), ())), preferred_element_type=F32)
        weights = []
        factors = []
        for n in range(16):
            xx, zl = n // 4, n % 4
            b = 16 * c + 4 * zl + xx
            old = top[xx, 64 * zl : 64 * zl + 64]
            tiles = []
            high = None
            for w in range(4):
                bias = row_bias[4 * zz + w, pl.ds(b, 1), :]
                if band:
                    which = 225 + b - 8 * (4 * zz + x) - 2 * w
                    bias = jnp.maximum(bias, tile_bias[jnp.clip(which, 0, 11)])
                tile = s[64 * n : 64 * n + 64, 128 * w : 128 * w + 128] * SCALE + bias
                high = tile if high is None else jnp.maximum(high, tile)
                tiles.append(tile)
            new = jnp.maximum(old, jnp.max(high, axis=1, keepdims=True))
            top[xx, 64 * zl : 64 * zl + 64] = new
            factor = jnp.exp2(old - new)
            tiles = [jnp.exp2(tile - new) for tile in tiles]
            total[xx, 64 * zl : 64 * zl + 64] = total[xx, 64 * zl : 64 * zl + 64] * factor + (
                (tiles[0] + tiles[1]) + (tiles[2] + tiles[3])
            )
            factors.append(factor)
            weights.append(jnp.concatenate([tile.astype(BF16) for tile in tiles], axis=1))
        added = jnp.dot(jnp.concatenate(weights, axis=0), values, preferred_element_type=F32)
        for n in range(16):
            at = (n // 4, pl.ds(64 * (n % 4), 64))
            mixed[at] = mixed[at] * factors[n] + added[64 * n : 64 * n + 64]

    def step(i, carry):
        zz = (z + by_distance(i)) % NZ

        @pl.when(i < NZ - 3)
        def _():
            forward_other(i + 3)

        @pl.when(i == 5)
        def _():
            for d in (1, 3):
                arrived(wv.at[c, (x + NX - d) % NX], w_recv.at[d])
                w_relay(d).start()
                w_core(d).start()

        arrived(kvb.at[zz, 0], kc_recv.at[zz])

        @pl.when(zz >= 6)
        def _():
            chunk(zz, True)

        @pl.when(zz < 6)
        def _():
            chunk(zz, False)

        return carry

    lax.fori_loop(0, NZ, step, 0)

    def st_copy(d):
        xx = (x + d) % NX
        return remote(st_out.at[xx], sb.at[d], st_send.at[d], st_recv.at[d], z * NX + xx, t)

    def o_copy(i, d):
        xx = (x + d) % NX
        return remote(
            o_out.at[xx, i], ob.at[d, i], ox_send.at[4 * i + d], ox_recv.at[4 * i + d], z * NX + xx, t
        )

    for d in (2, 1, 3, 0):
        xx = (x + d) % NX
        amount = jnp.sum(total[xx], axis=1, keepdims=True)
        o_out[xx] = (mixed[xx] / amount).astype(BF16).reshape(4, 64, HD)
        st_out[xx] = (top[xx] + jnp.log2(amount)).T[:8, :]
        if d:
            st_copy(d).start()
            o_copy(z % 4, d).start()
    for j in range(1, 4):
        for d in (2, 1, 3):
            o_copy((z + j) % 4, d).start()
    for d in range(1, NX):
        arrived(sb.at[d], st_recv.at[d])
    levels = [st_out[x]] + [sb[d] for d in range(1, NX)]
    best = jnp.maximum(jnp.maximum(levels[0], levels[1]), jnp.maximum(levels[2], levels[3]))
    parts = [jnp.exp2(level - best) for level in levels]
    amount = (parts[0] + parts[1]) + (parts[2] + parts[3])
    parts = [p / amount for p in parts]
    share_of[...] = jnp.concatenate(parts + [jnp.zeros((96, 256), F32)], axis=0).T

    def a_copy(i, d):
        ref = ab.at[i, y]
        return remote(ref, ref, a_send.at[8 * i + d], a_recv.at[i], ctx, 2 * ((y + d) % NY) + c)

    for j in range(4):
        i = (z + j) % 4
        part_share = share_of[aligned(64 * i, 64), :]
        joined = part_share[:, 0:1] * o_out[x, i].astype(F32)
        for d in range(1, NX):
            arrived(ob.at[d, i], ox_recv.at[4 * i + d])
            joined = joined + part_share[:, 8 * d : 8 * d + 1] * ob[d, i].astype(F32)
        ab[i, y] = joined.astype(BF16)
        for d in (4, 3, 5, 2, 6, 1, 7):
            a_copy(i, d).start()

    for h in range(2):
        arrived(wv.at[c, (x + 2) % NX, pl.ds(128 * h, 128)], w_recv.at[2 * h])
    w_core(2).start()
    arrived(wv.at[0], wc_recv)
    w_own.wait()

    def z_copy(j, cc):
        to = (4 * c + (z + j) % 4) * NX + x
        return remote(
            part.at[j, cc], early.at[2 * j + z // 4], z_send.at[2 * j + cc], z_recv, to, 2 * y + cc
        )

    def row_copy(j, d):
        to = (4 * c + (z + j) % 4) * NX + x
        tt = (t + d) % NT
        return remote(
            pieces.at[j - 2, tt], late.at[2 * (j - 2) + z // 4, y],
            r_send.at[NT * (j - 2) + d], r_recv, to, tt,
        )

    for j in range(4):
        i = (z + j) % 4
        arrived(ab.at[i, pl.ds(0, NY - 1)], a_recv.at[i])
        features = jnp.concatenate([ab[i, yy] for yy in range(NY)], axis=1)
        for cc in range(2):
            weight = wv[cc].reshape(1024, 512)
            rows = jnp.dot(features, weight, preferred_element_type=F32)
            if j >= 2:
                for tt in range(NT):
                    pieces[j - 2, tt, :, 512 * cc : 512 * cc + 512] = rows[4 * tt : 4 * tt + 4, :].astype(BF16)
                continue
            part[j, cc] = rows.astype(BF16)
            if j:
                z_copy(j, cc).start()
                continue
            mine = jnp.logical_and(4 * c + i == z, cc == c)

            @pl.when(jnp.logical_not(mine))
            def _():
                z_copy(0, cc).start()

            @pl.when(mine)
            def _():
                pltpu.make_async_copy(part.at[0, cc], early.at[z // 4], z_recv).start()

        if j >= 2:
            for d in range(NT):
                row_copy(j, d).start()

    arrived(early, z_recv)
    summed = (early[0].astype(F32) + early[1].astype(F32)) + (early[2].astype(F32) + early[3].astype(F32))
    for tt in range(NT):
        fb[tt] = summed[4 * tt : 4 * tt + 4, :].astype(BF16)
    last = [
        remote(fb.at[(t + d) % NT], fr.at[t], f_send.at[d], f_recv, ctx, (t + d) % NT)
        for d in range(1, NT)
    ]
    for copy in last:
        copy.start()
    pltpu.make_async_copy(fb.at[t], fr.at[t], f_recv).start()

    for copy in q1 + q2 + kz + qx + wx + wc:
        copy.wait_send()
    for d in range(1, NX):
        w_core(d).wait_send()
        st_copy(d).wait_send()
        for i in range(4):
            o_copy(i, d).wait_send()
    for d in (1, 3):
        w_relay(d).wait_send()

    def sent(zz, carry):
        for kv in range(2):
            y_copy(zz, kv).wait_send()
            core_copy(zz, kv, share, 0).wait_send()
            core_copy(zz, kv, other, 1).wait_send()
        return carry

    lax.fori_loop(0, NZ, sent, 0)
    for i in range(4):
        for d in range(1, NY):
            a_copy(i, d).wait_send()
    for cc in range(2):
        mine = jnp.logical_and(4 * c + z % 4 == z, cc == c)

        @pl.when(jnp.logical_not(mine))
        def _():
            z_copy(0, cc).wait_send()

        z_copy(1, cc).wait_send()
    for j in (2, 3):
        for d in range(NT):
            row_copy(j, d).wait_send()
    for copy in last:
        copy.wait_send()

    arrived(late, r_recv)
    arrived(fr, f_recv)
    for tt in range(NT):
        summed = fr[tt].astype(F32)
        for e in range(4):
            summed = summed + late[e, tt // 2, :, 512 * (tt % 2) : 512 * (tt % 2) + 512].astype(F32)
        out_ref[:, 512 * tt : 512 * tt + 512] = summed.astype(BF16)


def layer(q, k, v, w, kinds, counts, blocks, cols, offs):
    dma = pltpu.SemaphoreType.DMA
    hbm = pl.BlockSpec(memory_space=pltpu.HBM)
    smem = pl.BlockSpec(memory_space=pltpu.SMEM)
    vmem = pltpu.VMEM
    return pl.pallas_call(
        layer_kernel,
        out_shape=jax.ShapeDtypeStruct((4, 8192), BF16),
        in_specs=[hbm, hbm, hbm, hbm, smem, smem, hbm, hbm, hbm],
        out_specs=pl.BlockSpec(memory_space=pltpu.VMEM),
        scratch_shapes=[
            vmem((4, 8192), BF16),
            vmem((KVH, NY, 4, HD), BF16),
            vmem((NZ, NY, 4, HD), BF16),
            vmem((NY, NZ, 4, HD), BF16),
            vmem((NT, 4, 4, HD), BF16),
            vmem((4, 64, HD), F32),
            vmem((NX, 4, 64, HD), BF16),
            vmem((2, NZ, 128, HD), BF16),
            vmem((NZ, 2, 512, HD), BF16),
            vmem((2, NX, 256, 512), BF16),
            vmem((32, 16, H), jnp.int32),
            vmem((8, 1024), jnp.int32),
            vmem((8, 128), jnp.int32),
            vmem((32, 32, 128), F32),
            vmem((12, 64, 128), F32),
            vmem((NX, 256, 128), F32),
            vmem((NX, 256, 128), F32),
            vmem((NX, 256, HD), F32),
            vmem((NX, 4, 64, HD), BF16),
            vmem((NX, 8, 256), F32),
            vmem((NX, 4, 64, HD), BF16),
            vmem((NX, 8, 256), F32),
            vmem((256, 128), F32),
            vmem((4, NY, 64, HD), BF16),
            vmem((2, 2, 64, 512), BF16),
            vmem((4, 64, 512), BF16),
            vmem((2, NT, 4, 1024), BF16),
            vmem((4, NY, 4, 1024), BF16),
            vmem((NT, 4, 512), BF16),
            vmem((NT, 4, 512), BF16),
            dma((21,)),
            dma((8,)), dma, dma((16,)), dma, dma((4,)), dma((4,)),
            dma((16,)), dma((16,)), dma((16,)), dma((16,)), dma((32,)), dma((8,)),
            dma((4,)), dma((4,)), dma((4,)), dma, dma((4,)), dma((4,)), dma((16,)), dma((16,)),
            dma((32,)), dma((4,)), dma((4,)), dma, dma((32,)), dma, dma((16,)), dma,
        ],
        compiler_params=pltpu.CompilerParams(
            collective_id=0, has_side_effects=True, vmem_limit_bytes=56 * 1024 * 1024
        ),
        name="layer",
    )(q, k, v, w, kinds, counts, blocks, cols, offs)


def shards(q, k, v, w, kinds, counts, blocks, cols, offs):
    return layer(q, k, v, w, kinds, counts, blocks.transpose(1, 2, 0), cols, offs)


def solution(mesh):
    return jax.shard_map(
        shards,
        mesh=mesh,
        in_specs=(
            P(("ctx", "tp"), None),
            P("ctx", None),
            P("ctx", None),
            P("ctx", "tp"),
            P(),
            P(),
            P(),
            P(),
            P(),
        ),
        out_specs=P(("ctx", "tp"), None),
        check_vma=False,
    )
```

```python
import math

import jax
import jax.numpy as jnp
from jax import lax
from jax.experimental import pallas as pl
from jax.experimental.pallas import tpu as pltpu
from jax.sharding import PartitionSpec as P

H = 64
KVH = 8
HD = 128
NX, NZ, NY = 4, 8, 8
NT = 2 * NY
MASKED = -1e30
MESH = pl.DeviceIdType.MESH
F32 = jnp.float32
BF16 = jnp.bfloat16
SCALE = math.log2(math.e) / math.sqrt(HD)


def remote(src, dst, send_sem, recv_sem, ctx, tp):
    return pltpu.make_async_remote_copy(
        src_ref=src,
        dst_ref=dst,
        send_sem=send_sem,
        recv_sem=recv_sem,
        device_id=(ctx, tp),
        device_id_type=MESH,
    )


def arrived(ref, sem):
    pltpu.make_async_copy(ref, ref, sem).wait()


def lanes(shape):
    return lax.broadcasted_iota(jnp.int32, shape, len(shape) - 1)


def subs(shape):
    return lax.broadcasted_iota(jnp.int32, shape, 0)


def aligned(start, size):
    return pl.ds(pl.multiple_of(start, size), size)


def by_distance(i):
    odd = i % 2
    return odd * ((i + 1) // 2) + (1 - odd) * ((8 - i // 2) % 8)


def member_rows(values, first_row):
    high = jnp.where(values // 128 == first_row, 1.0, 0.0).astype(BF16)
    low = jnp.where(values % 128 == subs((128, values.shape[1])), 1.0, 0.0).astype(BF16)
    found = lax.dot_general(high, low, (((1,), (1,)), ((), ())), preferred_element_type=F32)
    return jnp.where(found > 0.5, 0.0, MASKED)


def fill_masks(slash, count, head, x, y, blocks, cols8, offs8, row_bias, tile_bias):
    tile = subs((32, 1024))
    tile = 16 * (tile // 4) + 4 * x + tile % 4
    vertical = member_rows(cols8[pl.ds(y, 1), :], tile)
    ids = jnp.where(lanes((32, 16, H)) == head, blocks[...].astype(F32), 0.0)
    ids = jnp.sum(ids, axis=2, keepdims=True)
    at = lanes((1, 1, 128))
    block = (8 * (4 * (at // 8) + x) + at % 8).astype(F32)
    turn = lax.broadcasted_iota(jnp.int32, (32, 16, 128), 1)
    hit = jnp.where(ids == block, 0.0, MASKED)
    hit = jnp.where(turn >= 1, jnp.where(turn < count, hit, MASKED), MASKED)
    chosen = jnp.max(hit, axis=1)
    left = lanes((32, 128)) < 64
    for i in range(32):
        pair = jnp.where(left, chosen[:, 2 * i : 2 * i + 1], chosen[:, 2 * i + 1 : 2 * i + 2])
        row_bias[i] = jnp.where(slash, jnp.broadcast_to(vertical[i : i + 1, :], (32, 128)), pair)
    rev = 511 - offs8[pl.ds(y, 1), :]
    phases = [member_rows(rev + 128 + 64 * phase, subs((8, 128))) for phase in range(2)]
    back = subs((64, 128)) - lanes((64, 128))
    right = lanes((64, 128)) >= 64
    nothing = jnp.full((64, 128), MASKED, F32)
    tile_bias[0] = nothing
    tile_bias[11] = nothing
    for i in range(10):
        start = 576 - 64 * i
        phase = (start // 64) % 2
        first = (start + 64 * phase) // 128
        pair = jnp.concatenate(
            [phases[phase][first : first + 1, :], phases[phase][first + 1 : first + 2, :]], axis=1
        )
        rolled = pltpu.roll(jnp.broadcast_to(pair, (64, 256)), 256 - 63, 1, stride=1, stride_axis=0)
        own = nothing
        if i == 0:
            own = jnp.where(right, MASKED, jnp.where(back >= 0, 0.0, MASKED))
        if i == 1:
            own = jnp.where(right, jnp.where(back + 64 >= 0, 0.0, MASKED), MASKED)
        tile_bias[i + 1] = jnp.where(slash, rolled[:, :128], own)


def layer_kernel(
    q_ref, k_ref, v_ref, w_ref, kind_ref, count_ref, blocks_ref, cols_ref, offs_ref,
    out_ref,
    qv, qt, qs, qy, q4, qf, qb, kl, kvb, wv, blocks, cols8, offs8, row_bias, tile_bias,
    top, total, mixed, o_out, st_out, ob, sb, share_of, ab, part, early, pieces, late, fb, fr,
    in_sem, q1_send, q1_recv, q2_send, q2_recv, qx_send, qx_recv,
    kz_send, kz_recv, ky_send, ky_recv, kc_send, kc_recv,
    w_send, w_recv, wc_send, wc_recv, st_send, st_recv, ox_send, ox_recv,
    a_send, a_recv, z_send, z_recv, r_send, r_recv, f_send, f_recv,
):
    ctx = lax.axis_index("ctx")
    t = lax.axis_index("tp")
    z, x, y, c = ctx // NX, ctx % NX, t // 2, t % 2
    partner = 2 * y + 1 - c
    head = 8 * z + y

    loads = [
        pltpu.make_async_copy(q_ref, qv, in_sem.at[0]),
        pltpu.make_async_copy(blocks_ref, blocks, in_sem.at[1]),
        pltpu.make_async_copy(cols_ref.at[aligned(8 * z, 8)], cols8, in_sem.at[2]),
        pltpu.make_async_copy(offs_ref.at[aligned(8 * z, 8)], offs8, in_sem.at[3]),
    ]
    barrier = pltpu.get_barrier_semaphore()

    def greet(to_ctx, to_tp):
        pl.semaphore_signal(barrier, inc=1, device_id=(to_ctx, to_tp), device_id_type=MESH)

    for d in (4, 3, 5, 2, 6, 1, 7):
        greet(((z + d) % NZ) * NX + x, t)
        for core in (c, 1 - c):
            greet(ctx, 2 * ((y + d) % NY) + core)
    for d in (2, 1, 3):
        greet(z * NX + (x + d) % NX, t)
    greet(ctx, partner)

    for copy in loads:
        copy.start()
    share = 2 * (y % 2) + c
    other = 2 * (1 - y % 2) + c

    def piece(zz, i, s):
        return kvb.at[zz, i, aligned(128 * s, 128)]

    rows = aligned(128 * share, 128)
    dense = []
    for i, ref in enumerate((k_ref, v_ref)):
        pltpu.make_async_copy(
            ref.at[rows, aligned(HD * z, HD)], piece(z, i, share), kz_recv.at[2 * z + i]
        ).start()
        for d in range(1, NZ):
            cols = aligned(HD * ((z + d) % NZ), HD)
            dense.append(pltpu.make_async_copy(ref.at[rows, cols], kl.at[i, d], in_sem.at[5 + 8 * i + d]))
            dense[-1].start()
    w_own = pltpu.make_async_copy(w_ref, wv.at[c, x], in_sem.at[4])
    w_own.start()

    loads[0].wait()
    for yy in range(NY):
        for g in range(KVH):
            at = (8 * g + yy) * HD
            qt[g, yy] = qv[:, at : at + HD]
    for copy in dense:
        copy.wait()
    pl.semaphore_wait(barrier, NT - 1 + NZ - 1 + NX - 1)

    q1 = [
        remote(qt.at[(z + d) % NZ], qs.at[z], q1_send.at[d], q1_recv, ((z + d) % NZ) * NX + x, t)
        for d in range(1, NZ)
    ]
    for copy in q1:
        copy.start()
    pltpu.make_async_copy(qt.at[z], qs.at[z], q1_recv).start()

    kz = []
    for d in (1, 7, 2, 6, 3, 5, 4):
        g = (z + d) % NZ
        for i in range(2):
            copy = remote(
                kl.at[i, d], piece(z, i, share),
                kz_send.at[2 * d + i], kz_recv.at[2 * z + i], g * NX + x, t,
            )
            copy.start()
            kz.append(copy)

    def y_copy(zz, i):
        to = (y + 1) % NY if i == 0 else (y + NY - 1) % NY
        ref = piece(zz, i, share)
        return remote(ref, ref, ky_send.at[2 * zz + i], ky_recv.at[2 * zz + i], ctx, 2 * to + c)

    def core_copy(zz, i, s, n):
        ref = piece(zz, i, s)
        return remote(ref, ref, kc_send.at[4 * zz + 2 * n + i], kc_recv.at[zz], ctx, partner)

    def forward_own(i):
        zz = (z + by_distance(i)) % NZ
        for kv in range(2):
            arrived(piece(zz, kv, share), kz_recv.at[2 * zz + kv])
            y_copy(zz, kv).start()
            core_copy(zz, kv, share, 0).start()

    def forward_other(i):
        zz = (z + by_distance(i)) % NZ
        for kv in range(2):
            arrived(piece(zz, kv, other), ky_recv.at[2 * zz + kv])
            core_copy(zz, kv, other, 1).start()

    forward_own(0)

    for copy in loads[1:]:
        copy.wait()
    fill_masks(
        kind_ref[head] == 1, count_ref[head], head, x, y, blocks, cols8, offs8, row_bias, tile_bias
    )
    top[...] = jnp.full((NX, 256, 128), MASKED, F32)
    total[...] = jnp.zeros((NX, 256, 128), F32)
    mixed[...] = jnp.zeros((NX, 256, HD), F32)

    arrived(qs, q1_recv)
    for yy in range(NY):
        for zz in range(NZ):
            qy[yy, zz] = qs[zz, yy]
    q2 = []
    for d in range(1, NT):
        tt = (t + d) % NT
        src = qy.at[tt // 2, pl.ds(4 * (tt % 2), 4)]
        q2.append(remote(src, q4.at[t], q2_send.at[d], q2_recv, ctx, tt))
        q2[-1].start()
    pltpu.make_async_copy(qy.at[y, pl.ds(4 * c, 4)], q4.at[t], q2_recv).start()

    arrived(q4, q2_recv)
    for zl in range(4):
        for tt in range(NT):
            qf[zl, 4 * tt : 4 * tt + 4, :] = q4[tt, zl].astype(F32)
    qb[x] = qf[...].astype(BF16)
    qx = [
        remote(qb.at[x], qb.at[x], qx_send.at[d], qx_recv.at[d], z * NX + (x + d) % NX, t)
        for d in range(1, NX)
    ]
    for copy in qx:
        copy.start()

    wx = [
        remote(w_ref, wv.at[c, x], w_send.at[d], w_recv.at[d], z * NX + (x + d) % NX, t)
        for d in (1, 3)
    ]
    wc = [remote(w_ref, wv.at[c, x], wc_send.at[0], wc_recv, ctx, partner)]
    for copy in wx + wc:
        copy.start()

    def w_relay(d):
        ref = wv.at[c, (x + NX - d) % NX, pl.ds(64 * (d - 1), 128)]
        return remote(ref, ref, w_send.at[d - 1], w_recv.at[d - 1], z * NX + (x + d) % NX, t)

    def w_core(d):
        ref = wv.at[c, (x + NX - d) % NX]
        return remote(ref, ref, wc_send.at[d], wc_recv, ctx, partner)

    forward_other(0)
    for i in range(1, 6):
        forward_own(i)
    for d in range(1, NX):
        arrived(qb.at[(x + NX - d) % NX], qx_recv.at[d])
    forward_own(6)
    forward_other(1)
    forward_own(7)
    forward_other(2)

    def chunk(zz, band):
        keys = kvb[zz, 0]
        values = kvb[zz, 1]

        queries = qb[...].reshape(1024, HD)
        s = lax.dot_general(queries, keys, (((1,), (1,)), ((), ())), preferred_element_type=F32)
        weights = []
        factors = []
        for n in range(16):
            xx, zl = n // 4, n % 4
            b = 16 * c + 4 * zl + xx
            old = top[xx, 64 * zl : 64 * zl + 64]
            tiles = []
            high = None
            for w in range(4):
                bias = row_bias[4 * zz + w, pl.ds(b, 1), :]
                if band:
                    which = 225 + b - 8 * (4 * zz + x) - 2 * w
                    bias = jnp.maximum(bias, tile_bias[jnp.clip(which, 0, 11)])
                tile = s[64 * n : 64 * n + 64, 128 * w : 128 * w + 128] * SCALE + bias
                high = tile if high is None else jnp.maximum(high, tile)
                tiles.append(tile)
            new = jnp.maximum(old, jnp.max(high, axis=1, keepdims=True))
            top[xx, 64 * zl : 64 * zl + 64] = new
            factor = jnp.exp2(old - new)
            tiles = [jnp.exp2(tile - new) for tile in tiles]
            total[xx, 64 * zl : 64 * zl + 64] = total[xx, 64 * zl : 64 * zl + 64] * factor + (
                (tiles[0] + tiles[1]) + (tiles[2] + tiles[3])
            )
            factors.append(factor)
            weights.append(jnp.concatenate([tile.astype(BF16) for tile in tiles], axis=1))
        added = jnp.dot(jnp.concatenate(weights, axis=0), values, preferred_element_type=F32)
        for n in range(16):
            at = (n // 4, pl.ds(64 * (n % 4), 64))
            mixed[at] = mixed[at] * factors[n] + added[64 * n : 64 * n + 64]

    def step(i, carry):
        zz = (z + by_distance(i)) % NZ

        @pl.when(i < NZ - 3)
        def _():
            forward_other(i + 3)

        @pl.when(i == 5)
        def _():
            for d in (1, 3):
                arrived(wv.at[c, (x + NX - d) % NX], w_recv.at[d])
                w_relay(d).start()
                w_core(d).start()

        arrived(kvb.at[zz, 0], kc_recv.at[zz])

        @pl.when(zz >= 6)
        def _():
            chunk(zz, True)

        @pl.when(zz < 6)
        def _():
            chunk(zz, False)

        return carry

    lax.fori_loop(0, NZ, step, 0)

    def st_copy(d):
        xx = (x + d) % NX
        return remote(st_out.at[xx], sb.at[d], st_send.at[d], st_recv.at[d], z * NX + xx, t)

    def o_copy(i, d):
        xx = (x + d) % NX
        return remote(
            o_out.at[xx, i], ob.at[d, i], ox_send.at[4 * i + d], ox_recv.at[4 * i + d], z * NX + xx, t
        )

    def divide(d, i):
        xx = (x + d) % NX
        at = (xx, aligned(64 * i, 64))
        o_out[xx, i] = (mixed[at] * total[at]).astype(BF16)

    for d in (2, 1, 3, 0):
        xx = (x + d) % NX
        amount = jnp.sum(total[xx], axis=1, keepdims=True)
        total[xx] = jnp.broadcast_to(1.0 / amount, (256, 128))
        st_out[xx] = (top[xx] + jnp.log2(amount)).T[:8, :]
        if d:
            st_copy(d).start()
            divide(d, z % 4)
            o_copy(z % 4, d).start()
    for j in range(1, 4):
        for d in (2, 1, 3):
            divide(d, (z + j) % 4)
            o_copy((z + j) % 4, d).start()
    for i in range(4):
        divide(0, i)
    for d in range(1, NX):
        arrived(sb.at[d], st_recv.at[d])
    levels = [st_out[x]] + [sb[d] for d in range(1, NX)]
    best = jnp.maximum(jnp.maximum(levels[0], levels[1]), jnp.maximum(levels[2], levels[3]))
    parts = [jnp.exp2(level - best) for level in levels]
    amount = (parts[0] + parts[1]) + (parts[2] + parts[3])
    parts = [p / amount for p in parts]
    share_of[...] = jnp.concatenate(parts + [jnp.zeros((96, 256), F32)], axis=0).T

    def a_copy(i, d):
        ref = ab.at[i, y]
        return remote(ref, ref, a_send.at[8 * i + d], a_recv.at[i], ctx, 2 * ((y + d) % NY) + c)

    for j in range(4):
        i = (z + j) % 4
        part_share = share_of[aligned(64 * i, 64), :]
        joined = part_share[:, 0:1] * o_out[x, i].astype(F32)
        for d in range(1, NX):
            arrived(ob.at[d, i], ox_recv.at[4 * i + d])
            joined = joined + part_share[:, 8 * d : 8 * d + 1] * ob[d, i].astype(F32)
        ab[i, y] = joined.astype(BF16)
        for d in (4, 3, 5, 2, 6, 1, 7):
            a_copy(i, d).start()

    for h in range(2):
        arrived(wv.at[c, (x + 2) % NX, pl.ds(128 * h, 128)], w_recv.at[2 * h])
    w_core(2).start()
    arrived(wv.at[0], wc_recv)
    w_own.wait()

    def z_copy(j, cc):
        to = (4 * c + (z + j) % 4) * NX + x
        return remote(
            part.at[j, cc], early.at[2 * j + z // 4], z_send.at[2 * j + cc], z_recv, to, 2 * y + cc
        )

    def row_copy(j, d):
        to = (4 * c + (z + j) % 4) * NX + x
        tt = (t + d) % NT
        return remote(
            pieces.at[j - 2, tt], late.at[2 * (j - 2) + z // 4, y],
            r_send.at[NT * (j - 2) + d], r_recv, to, tt,
        )

    for j in range(4):
        i = (z + j) % 4
        arrived(ab.at[i, pl.ds(0, NY - 1)], a_recv.at[i])
        features = jnp.concatenate([ab[i, yy] for yy in range(NY)], axis=1)
        for cc in range(2):
            weight = wv[cc].reshape(1024, 512)
            rows = jnp.dot(features, weight, preferred_element_type=F32)
            if j >= 2:
                for tt in range(NT):
                    pieces[j - 2, tt, :, 512 * cc : 512 * cc + 512] = rows[4 * tt : 4 * tt + 4, :].astype(BF16)
                continue
            part[j, cc] = rows.astype(BF16)
            if j:
                z_copy(j, cc).start()
                continue
            mine = jnp.logical_and(4 * c + i == z, cc == c)

            @pl.when(jnp.logical_not(mine))
            def _():
                z_copy(0, cc).start()

            @pl.when(mine)
            def _():
                pltpu.make_async_copy(part.at[0, cc], early.at[z // 4], z_recv).start()

        if j >= 2:
            for d in range(NT):
                row_copy(j, d).start()

    arrived(early, z_recv)
    summed = (early[0].astype(F32) + early[1].astype(F32)) + (early[2].astype(F32) + early[3].astype(F32))
    for tt in range(NT):
        fb[tt] = summed[4 * tt : 4 * tt + 4, :].astype(BF16)
    last = [
        remote(fb.at[(t + d) % NT], fr.at[t], f_send.at[d], f_recv, ctx, (t + d) % NT)
        for d in range(1, NT)
    ]
    for copy in last:
        copy.start()
    pltpu.make_async_copy(fb.at[t], fr.at[t], f_recv).start()

    for copy in q1 + q2 + kz + qx + wx + wc:
        copy.wait_send()
    for d in range(1, NX):
        w_core(d).wait_send()
        st_copy(d).wait_send()
        for i in range(4):
            o_copy(i, d).wait_send()
    for d in (1, 3):
        w_relay(d).wait_send()

    def sent(zz, carry):
        for kv in range(2):
            y_copy(zz, kv).wait_send()
            core_copy(zz, kv, share, 0).wait_send()
            core_copy(zz, kv, other, 1).wait_send()
        return carry

    lax.fori_loop(0, NZ, sent, 0)
    for i in range(4):
        for d in range(1, NY):
            a_copy(i, d).wait_send()
    for cc in range(2):
        mine = jnp.logical_and(4 * c + z % 4 == z, cc == c)

        @pl.when(jnp.logical_not(mine))
        def _():
            z_copy(0, cc).wait_send()

        z_copy(1, cc).wait_send()
    for j in (2, 3):
        for d in range(NT):
            row_copy(j, d).wait_send()
    for copy in last:
        copy.wait_send()

    arrived(late, r_recv)
    arrived(fr, f_recv)
    for tt in range(NT):
        summed = fr[tt].astype(F32)
        for e in range(4):
            summed = summed + late[e, tt // 2, :, 512 * (tt % 2) : 512 * (tt % 2) + 512].astype(F32)
        out_ref[:, 512 * tt : 512 * tt + 512] = summed.astype(BF16)


def layer(q, k, v, w, kinds, counts, blocks, cols, offs):
    dma = pltpu.SemaphoreType.DMA
    hbm = pl.BlockSpec(memory_space=pltpu.HBM)
    smem = pl.BlockSpec(memory_space=pltpu.SMEM)
    vmem = pltpu.VMEM
    return pl.pallas_call(
        layer_kernel,
        out_shape=jax.ShapeDtypeStruct((4, 8192), BF16),
        in_specs=[hbm, hbm, hbm, hbm, smem, smem, hbm, hbm, hbm],
        out_specs=pl.BlockSpec(memory_space=pltpu.VMEM),
        scratch_shapes=[
            vmem((4, 8192), BF16),
            vmem((KVH, NY, 4, HD), BF16),
            vmem((NZ, NY, 4, HD), BF16),
            vmem((NY, NZ, 4, HD), BF16),
            vmem((NT, 4, 4, HD), BF16),
            vmem((4, 64, HD), F32),
            vmem((NX, 4, 64, HD), BF16),
            vmem((2, NZ, 128, HD), BF16),
            vmem((NZ, 2, 512, HD), BF16),
            vmem((2, NX, 256, 512), BF16),
            vmem((32, 16, H), jnp.int32),
            vmem((8, 1024), jnp.int32),
            vmem((8, 128), jnp.int32),
            vmem((32, 32, 128), F32),
            vmem((12, 64, 128), F32),
            vmem((NX, 256, 128), F32),
            vmem((NX, 256, 128), F32),
            vmem((NX, 256, HD), F32),
            vmem((NX, 4, 64, HD), BF16),
            vmem((NX, 8, 256), F32),
            vmem((NX, 4, 64, HD), BF16),
            vmem((NX, 8, 256), F32),
            vmem((256, 128), F32),
            vmem((4, NY, 64, HD), BF16),
            vmem((2, 2, 64, 512), BF16),
            vmem((4, 64, 512), BF16),
            vmem((2, NT, 4, 1024), BF16),
            vmem((4, NY, 4, 1024), BF16),
            vmem((NT, 4, 512), BF16),
            vmem((NT, 4, 512), BF16),
            dma((21,)),
            dma((8,)), dma, dma((16,)), dma, dma((4,)), dma((4,)),
            dma((16,)), dma((16,)), dma((16,)), dma((16,)), dma((32,)), dma((8,)),
            dma((4,)), dma((4,)), dma((4,)), dma, dma((4,)), dma((4,)), dma((16,)), dma((16,)),
            dma((32,)), dma((4,)), dma((4,)), dma, dma((32,)), dma, dma((16,)), dma,
        ],
        compiler_params=pltpu.CompilerParams(
            collective_id=0, has_side_effects=True, vmem_limit_bytes=56 * 1024 * 1024
        ),
        name="layer",
    )(q, k, v, w, kinds, counts, blocks, cols, offs)


def shards(q, k, v, w, kinds, counts, blocks, cols, offs):
    return layer(q, k, v, w, kinds, counts, blocks.transpose(1, 2, 0), cols, offs)


def solution(mesh):
    return jax.shard_map(
        shards,
        mesh=mesh,
        in_specs=(
            P(("ctx", "tp"), None),
            P("ctx", None),
            P("ctx", None),
            P("ctx", "tp"),
            P(),
            P(),
            P(),
            P(),
            P(),
        ),
        out_specs=P(("ctx", "tp"), None),
        check_vma=False,
    )
```

```python
import math

import jax
import jax.numpy as jnp
from jax import lax
from jax.experimental import pallas as pl
from jax.experimental.pallas import tpu as pltpu
from jax.sharding import PartitionSpec as P

H = 64
KVH = 8
HD = 128
NX, NZ, NY = 4, 8, 8
NT = 2 * NY
MASKED = -1e30
MESH = pl.DeviceIdType.MESH
F32 = jnp.float32
BF16 = jnp.bfloat16
SCALE = math.log2(math.e) / math.sqrt(HD)


def remote(src, dst, send_sem, recv_sem, ctx, tp):
    return pltpu.make_async_remote_copy(
        src_ref=src,
        dst_ref=dst,
        send_sem=send_sem,
        recv_sem=recv_sem,
        device_id=(ctx, tp),
        device_id_type=MESH,
    )


def arrived(ref, sem):
    pltpu.make_async_copy(ref, ref, sem).wait()


def lanes(shape):
    return lax.broadcasted_iota(jnp.int32, shape, len(shape) - 1)


def subs(shape):
    return lax.broadcasted_iota(jnp.int32, shape, 0)


def aligned(start, size):
    return pl.ds(pl.multiple_of(start, size), size)


def by_distance(i):
    odd = i % 2
    return odd * ((i + 1) // 2) + (1 - odd) * ((8 - i // 2) % 8)


def member_rows(values, first_row):
    high = jnp.where(values // 128 == first_row, 1.0, 0.0).astype(BF16)
    low = jnp.where(values % 128 == subs((128, values.shape[1])), 1.0, 0.0).astype(BF16)
    found = lax.dot_general(high, low, (((1,), (1,)), ((), ())), preferred_element_type=F32)
    return jnp.where(found > 0.5, 0.0, MASKED)


def fill_masks(slash, count, head, x, y, blocks, cols8, offs8, row_bias, tile_bias):
    tile = subs((32, 1024))
    tile = 16 * (tile // 4) + 4 * x + tile % 4
    vertical = member_rows(cols8[pl.ds(y, 1), :], tile)
    ids = jnp.where(lanes((32, 16, H)) == head, blocks[...].astype(F32), 0.0)
    ids = jnp.sum(ids, axis=2, keepdims=True)
    at = lanes((1, 1, 128))
    block = (8 * (4 * (at // 8) + x) + at % 8).astype(F32)
    turn = lax.broadcasted_iota(jnp.int32, (32, 16, 128), 1)
    hit = jnp.where(ids == block, 0.0, MASKED)
    hit = jnp.where(turn >= 1, jnp.where(turn < count, hit, MASKED), MASKED)
    chosen = jnp.max(hit, axis=1)
    left = lanes((32, 128)) < 64
    for i in range(32):
        pair = jnp.where(left, chosen[:, 2 * i : 2 * i + 1], chosen[:, 2 * i + 1 : 2 * i + 2])
        row_bias[i] = jnp.where(slash, jnp.broadcast_to(vertical[i : i + 1, :], (32, 128)), pair)
    rev = 511 - offs8[pl.ds(y, 1), :]
    phases = [member_rows(rev + 128 + 64 * phase, subs((8, 128))) for phase in range(2)]
    back = subs((64, 128)) - lanes((64, 128))
    right = lanes((64, 128)) >= 64
    nothing = jnp.full((64, 128), MASKED, F32)
    tile_bias[0] = nothing
    tile_bias[11] = nothing
    for i in range(10):
        start = 576 - 64 * i
        phase = (start // 64) % 2
        first = (start + 64 * phase) // 128
        pair = jnp.concatenate(
            [phases[phase][first : first + 1, :], phases[phase][first + 1 : first + 2, :]], axis=1
        )
        rolled = pltpu.roll(jnp.broadcast_to(pair, (64, 256)), 256 - 63, 1, stride=1, stride_axis=0)
        own = nothing
        if i == 0:
            own = jnp.where(right, MASKED, jnp.where(back >= 0, 0.0, MASKED))
        if i == 1:
            own = jnp.where(right, jnp.where(back + 64 >= 0, 0.0, MASKED), MASKED)
        tile_bias[i + 1] = jnp.where(slash, rolled[:, :128], own)


def layer_kernel(
    q_ref, k_ref, v_ref, w_ref, kinds_ref, counts_ref, blocks_ref, cols_ref, offs_ref,
    out_ref,
    qv, qt, qs, qy, q4, qf, qb, kl, kvb, wv, kind_ref, count_ref, blocks, cols8, offs8, row_bias, tile_bias,
    top, total, mixed, o_out, st_out, ob, sb, share_of, ab, part, early, pieces, late, fb, fr,
    in_sem, q1_send, q1_recv, q2_send, q2_recv, qx_send, qx_recv,
    kz_send, kz_recv, ky_send, ky_recv, kc_send, kc_recv,
    w_send, w_recv, wc_send, wc_recv, st_send, st_recv, ox_send, ox_recv,
    a_send, a_recv, z_send, z_recv, r_send, r_recv, f_send, f_recv,
):
    ctx = lax.axis_index("ctx")
    t = lax.axis_index("tp")
    z, x, y, c = ctx // NX, ctx % NX, t // 2, t % 2
    partner = 2 * y + 1 - c
    head = 8 * z + y

    loads = [
        pltpu.make_async_copy(q_ref, qv, in_sem.at[0]),
        pltpu.make_async_copy(blocks_ref, blocks, in_sem.at[1]),
        pltpu.make_async_copy(cols_ref.at[aligned(8 * z, 8)], cols8, in_sem.at[2]),
        pltpu.make_async_copy(offs_ref.at[aligned(8 * z, 8)], offs8, in_sem.at[3]),
        pltpu.make_async_copy(kinds_ref, kind_ref, in_sem.at[5]),
        pltpu.make_async_copy(counts_ref, count_ref, in_sem.at[13]),
    ]
    barrier = pltpu.get_barrier_semaphore()

    def greet(to_ctx, to_tp):
        pl.semaphore_signal(barrier, inc=1, device_id=(to_ctx, to_tp), device_id_type=MESH)

    for d in (4, 3, 5, 2, 6, 1, 7):
        greet(((z + d) % NZ) * NX + x, t)
        for core in (c, 1 - c):
            greet(ctx, 2 * ((y + d) % NY) + core)
    for d in (2, 1, 3):
        greet(z * NX + (x + d) % NX, t)
    greet(ctx, partner)

    for copy in loads:
        copy.start()
    share = 2 * (y % 2) + c
    other = 2 * (1 - y % 2) + c

    def piece(zz, i, s):
        return kvb.at[zz, i, aligned(128 * s, 128)]

    rows = aligned(128 * share, 128)
    dense = []
    for i, ref in enumerate((k_ref, v_ref)):
        pltpu.make_async_copy(
            ref.at[rows, aligned(HD * z, HD)], piece(z, i, share), kz_recv.at[2 * z + i]
        ).start()
        for d in range(1, NZ):
            cols = aligned(HD * ((z + d) % NZ), HD)
            dense.append(pltpu.make_async_copy(ref.at[rows, cols], kl.at[i, d], in_sem.at[5 + 8 * i + d]))
            dense[-1].start()
    w_own = pltpu.make_async_copy(w_ref, wv.at[c, x], in_sem.at[4])
    w_own.start()

    loads[0].wait()
    for yy in range(NY):
        for g in range(KVH):
            at = (8 * g + yy) * HD
            qt[g, yy] = qv[:, at : at + HD]
    for copy in dense:
        copy.wait()
    pl.semaphore_wait(barrier, NT - 1 + NZ - 1 + NX - 1)

    q1 = [
        remote(qt.at[(z + d) % NZ], qs.at[z], q1_send.at[d], q1_recv, ((z + d) % NZ) * NX + x, t)
        for d in range(1, NZ)
    ]
    for copy in q1:
        copy.start()
    pltpu.make_async_copy(qt.at[z], qs.at[z], q1_recv).start()

    kz = []
    for d in (1, 7, 2, 6, 3, 5, 4):
        g = (z + d) % NZ
        for i in range(2):
            copy = remote(
                kl.at[i, d], piece(z, i, share),
                kz_send.at[2 * d + i], kz_recv.at[2 * z + i], g * NX + x, t,
            )
            copy.start()
            kz.append(copy)

    def y_copy(zz, i):
        to = (y + 1) % NY if i == 0 else (y + NY - 1) % NY
        ref = piece(zz, i, share)
        return remote(ref, ref, ky_send.at[2 * zz + i], ky_recv.at[2 * zz + i], ctx, 2 * to + c)

    def core_copy(zz, i, s, n):
        ref = piece(zz, i, s)
        return remote(ref, ref, kc_send.at[4 * zz + 2 * n + i], kc_recv.at[zz], ctx, partner)

    def forward_own(i):
        zz = (z + by_distance(i)) % NZ
        for kv in range(2):
            arrived(piece(zz, kv, share), kz_recv.at[2 * zz + kv])
            y_copy(zz, kv).start()
            core_copy(zz, kv, share, 0).start()

    def forward_other(i):
        zz = (z + by_distance(i)) % NZ
        for kv in range(2):
            arrived(piece(zz, kv, other), ky_recv.at[2 * zz + kv])
            core_copy(zz, kv, other, 1).start()

    forward_own(0)

    for copy in loads[1:]:
        copy.wait()
    fill_masks(
        kind_ref[head] == 1, count_ref[head], head, x, y, blocks, cols8, offs8, row_bias, tile_bias
    )
    top[...] = jnp.full((NX, 256, 128), MASKED, F32)
    total[...] = jnp.zeros((NX, 256, 128), F32)
    mixed[...] = jnp.zeros((NX, 256, HD), F32)

    arrived(qs, q1_recv)
    for yy in range(NY):
        for zz in range(NZ):
            qy[yy, zz] = qs[zz, yy]
    q2 = []
    for d in range(1, NT):
        tt = (t + d) % NT
        src = qy.at[tt // 2, pl.ds(4 * (tt % 2), 4)]
        q2.append(remote(src, q4.at[t], q2_send.at[d], q2_recv, ctx, tt))
        q2[-1].start()
    pltpu.make_async_copy(qy.at[y, pl.ds(4 * c, 4)], q4.at[t], q2_recv).start()

    arrived(q4, q2_recv)
    for zl in range(4):
        for tt in range(NT):
            qf[zl, 4 * tt : 4 * tt + 4, :] = q4[tt, zl].astype(F32)
    qb[x] = qf[...].astype(BF16)
    qx = [
        remote(qb.at[x], qb.at[x], qx_send.at[d], qx_recv.at[d], z * NX + (x + d) % NX, t)
        for d in range(1, NX)
    ]
    for copy in qx:
        copy.start()

    wx = [
        remote(w_ref, wv.at[c, x], w_send.at[d], w_recv.at[d], z * NX + (x + d) % NX, t)
        for d in (1, 3)
    ]
    wc = [remote(w_ref, wv.at[c, x], wc_send.at[0], wc_recv, ctx, partner)]
    for copy in wx + wc:
        copy.start()

    def w_relay(d):
        ref = wv.at[c, (x + NX - d) % NX, pl.ds(64 * (d - 1), 128)]
        return remote(ref, ref, w_send.at[d - 1], w_recv.at[d - 1], z * NX + (x + d) % NX, t)

    def w_core(d):
        ref = wv.at[c, (x + NX - d) % NX]
        return remote(ref, ref, wc_send.at[d], wc_recv, ctx, partner)

    forward_other(0)
    for i in range(1, 6):
        forward_own(i)
    for d in range(1, NX):
        arrived(qb.at[(x + NX - d) % NX], qx_recv.at[d])
    forward_own(6)
    forward_other(1)
    forward_own(7)
    forward_other(2)

    def chunk(zz, band):
        keys = kvb[zz, 0]
        values = kvb[zz, 1]

        queries = qb[...].reshape(1024, HD)
        s = lax.dot_general(queries, keys, (((1,), (1,)), ((), ())), preferred_element_type=F32)
        weights = []
        factors = []
        for n in range(16):
            xx, zl = n // 4, n % 4
            b = 16 * c + 4 * zl + xx
            old = top[xx, 64 * zl : 64 * zl + 64]
            tiles = []
            high = None
            for w in range(4):
                bias = row_bias[4 * zz + w, pl.ds(b, 1), :]
                if band:
                    which = 225 + b - 8 * (4 * zz + x) - 2 * w
                    bias = jnp.maximum(bias, tile_bias[jnp.clip(which, 0, 11)])
                tile = s[64 * n : 64 * n + 64, 128 * w : 128 * w + 128] * SCALE + bias
                high = tile if high is None else jnp.maximum(high, tile)
                tiles.append(tile)
            new = jnp.maximum(old, jnp.max(high, axis=1, keepdims=True))
            top[xx, 64 * zl : 64 * zl + 64] = new
            factor = jnp.exp2(old - new)
            tiles = [jnp.exp2(tile - new) for tile in tiles]
            total[xx, 64 * zl : 64 * zl + 64] = total[xx, 64 * zl : 64 * zl + 64] * factor + (
                (tiles[0] + tiles[1]) + (tiles[2] + tiles[3])
            )
            factors.append(factor)
            weights.append(jnp.concatenate([tile.astype(BF16) for tile in tiles], axis=1))
        added = jnp.dot(jnp.concatenate(weights, axis=0), values, preferred_element_type=F32)
        for n in range(16):
            at = (n // 4, pl.ds(64 * (n % 4), 64))
            mixed[at] = mixed[at] * factors[n] + added[64 * n : 64 * n + 64]

    def step(i, carry):
        zz = (z + by_distance(i)) % NZ

        @pl.when(i < NZ - 3)
        def _():
            forward_other(i + 3)

        @pl.when(i == 5)
        def _():
            for d in (1, 3):
                arrived(wv.at[c, (x + NX - d) % NX], w_recv.at[d])
                w_relay(d).start()
                w_core(d).start()

        arrived(kvb.at[zz, 0], kc_recv.at[zz])

        @pl.when(zz >= 6)
        def _():
            chunk(zz, True)

        @pl.when(zz < 6)
        def _():
            chunk(zz, False)

        return carry

    lax.fori_loop(0, NZ, step, 0)

    def st_copy(d):
        xx = (x + d) % NX
        return remote(st_out.at[xx], sb.at[d], st_send.at[d], st_recv.at[d], z * NX + xx, t)

    def o_copy(i, d):
        xx = (x + d) % NX
        return remote(
            o_out.at[xx, i], ob.at[d, i], ox_send.at[4 * i + d], ox_recv.at[4 * i + d], z * NX + xx, t
        )

    def divide(d, i):
        xx = (x + d) % NX
        at = (xx, aligned(64 * i, 64))
        o_out[xx, i] = (mixed[at] * total[at]).astype(BF16)

    for d in (2, 1, 3, 0):
        xx = (x + d) % NX
        amount = jnp.sum(total[xx], axis=1, keepdims=True)
        total[xx] = jnp.broadcast_to(1.0 / amount, (256, 128))
        st_out[xx] = (top[xx] + jnp.log2(amount)).T[:8, :]
        if d:
            st_copy(d).start()
            divide(d, z % 4)
            o_copy(z % 4, d).start()
    for j in range(1, 4):
        for d in (2, 1, 3):
            divide(d, (z + j) % 4)
            o_copy((z + j) % 4, d).start()
    for i in range(4):
        divide(0, i)
    for d in range(1, NX):
        arrived(sb.at[d], st_recv.at[d])
    levels = [st_out[x]] + [sb[d] for d in range(1, NX)]
    best = jnp.maximum(jnp.maximum(levels[0], levels[1]), jnp.maximum(levels[2], levels[3]))
    parts = [jnp.exp2(level - best) for level in levels]
    amount = (parts[0] + parts[1]) + (parts[2] + parts[3])
    parts = [p / amount for p in parts]
    share_of[...] = jnp.concatenate(parts + [jnp.zeros((96, 256), F32)], axis=0).T

    def a_copy(i, d):
        ref = ab.at[i, y]
        return remote(ref, ref, a_send.at[8 * i + d], a_recv.at[i], ctx, 2 * ((y + d) % NY) + c)

    for j in range(4):
        i = (z + j) % 4
        part_share = share_of[aligned(64 * i, 64), :]
        joined = part_share[:, 0:1] * o_out[x, i].astype(F32)
        for d in range(1, NX):
            arrived(ob.at[d, i], ox_recv.at[4 * i + d])
            joined = joined + part_share[:, 8 * d : 8 * d + 1] * ob[d, i].astype(F32)
        ab[i, y] = joined.astype(BF16)
        for d in (4, 3, 5, 2, 6, 1, 7):
            a_copy(i, d).start()

    for h in range(2):
        arrived(wv.at[c, (x + 2) % NX, pl.ds(128 * h, 128)], w_recv.at[2 * h])
    w_core(2).start()
    arrived(wv.at[0], wc_recv)
    w_own.wait()

    def z_copy(j, cc):
        to = (4 * c + (z + j) % 4) * NX + x
        return remote(
            part.at[j, cc], early.at[2 * j + z // 4], z_send.at[2 * j + cc], z_recv, to, 2 * y + cc
        )

    def row_copy(j, d):
        to = (4 * c + (z + j) % 4) * NX + x
        tt = (t + d) % NT
        return remote(
            pieces.at[j - 2, tt], late.at[2 * (j - 2) + z // 4, y],
            r_send.at[NT * (j - 2) + d], r_recv, to, tt,
        )

    for j in range(4):
        i = (z + j) % 4
        arrived(ab.at[i, pl.ds(0, NY - 1)], a_recv.at[i])
        features = jnp.concatenate([ab[i, yy] for yy in range(NY)], axis=1)
        for cc in range(2):
            weight = wv[cc].reshape(1024, 512)
            rows = jnp.dot(features, weight, preferred_element_type=F32)
            if j >= 2:
                for tt in range(NT):
                    pieces[j - 2, tt, :, 512 * cc : 512 * cc + 512] = rows[4 * tt : 4 * tt + 4, :].astype(BF16)
                continue
            part[j, cc] = rows.astype(BF16)
            if j:
                z_copy(j, cc).start()
                continue
            mine = jnp.logical_and(4 * c + i == z, cc == c)

            @pl.when(jnp.logical_not(mine))
            def _():
                z_copy(0, cc).start()

            @pl.when(mine)
            def _():
                pltpu.make_async_copy(part.at[0, cc], early.at[z // 4], z_recv).start()

        if j >= 2:
            for d in range(NT):
                row_copy(j, d).start()

    arrived(early, z_recv)
    summed = (early[0].astype(F32) + early[1].astype(F32)) + (early[2].astype(F32) + early[3].astype(F32))
    for tt in range(NT):
        fb[tt] = summed[4 * tt : 4 * tt + 4, :].astype(BF16)
    last = [
        remote(fb.at[(t + d) % NT], fr.at[t], f_send.at[d], f_recv, ctx, (t + d) % NT)
        for d in range(1, NT)
    ]
    for copy in last:
        copy.start()
    pltpu.make_async_copy(fb.at[t], fr.at[t], f_recv).start()

    for copy in q1 + q2 + kz + qx + wx + wc:
        copy.wait_send()
    for d in range(1, NX):
        w_core(d).wait_send()
        st_copy(d).wait_send()
        for i in range(4):
            o_copy(i, d).wait_send()
    for d in (1, 3):
        w_relay(d).wait_send()

    def sent(zz, carry):
        for kv in range(2):
            y_copy(zz, kv).wait_send()
            core_copy(zz, kv, share, 0).wait_send()
            core_copy(zz, kv, other, 1).wait_send()
        return carry

    lax.fori_loop(0, NZ, sent, 0)
    for i in range(4):
        for d in range(1, NY):
            a_copy(i, d).wait_send()
    for cc in range(2):
        mine = jnp.logical_and(4 * c + z % 4 == z, cc == c)

        @pl.when(jnp.logical_not(mine))
        def _():
            z_copy(0, cc).wait_send()

        z_copy(1, cc).wait_send()
    for j in (2, 3):
        for d in range(NT):
            row_copy(j, d).wait_send()
    for copy in last:
        copy.wait_send()

    arrived(late, r_recv)
    arrived(fr, f_recv)
    for tt in range(NT):
        summed = fr[tt].astype(F32)
        for e in range(4):
            summed = summed + late[e, tt // 2, :, 512 * (tt % 2) : 512 * (tt % 2) + 512].astype(F32)
        out_ref[:, 512 * tt : 512 * tt + 512] = summed.astype(BF16)


def layer(q, k, v, w, kinds, counts, blocks, cols, offs):
    dma = pltpu.SemaphoreType.DMA
    hbm = pl.BlockSpec(memory_space=pltpu.HBM)
    vmem = pltpu.VMEM
    return pl.pallas_call(
        layer_kernel,
        out_shape=jax.ShapeDtypeStruct((4, 8192), BF16),
        in_specs=[hbm] * 9,
        out_specs=pl.BlockSpec(memory_space=pltpu.VMEM),
        scratch_shapes=[
            vmem((4, 8192), BF16),
            vmem((KVH, NY, 4, HD), BF16),
            vmem((NZ, NY, 4, HD), BF16),
            vmem((NY, NZ, 4, HD), BF16),
            vmem((NT, 4, 4, HD), BF16),
            vmem((4, 64, HD), F32),
            vmem((NX, 4, 64, HD), BF16),
            vmem((2, NZ, 128, HD), BF16),
            vmem((NZ, 2, 512, HD), BF16),
            vmem((2, NX, 256, 512), BF16),
            pltpu.SMEM((H,), jnp.int32),
            pltpu.SMEM((H,), jnp.int32),
            vmem((32, 16, H), jnp.int32),
            vmem((8, 1024), jnp.int32),
            vmem((8, 128), jnp.int32),
            vmem((32, 32, 128), F32),
            vmem((12, 64, 128), F32),
            vmem((NX, 256, 128), F32),
            vmem((NX, 256, 128), F32),
            vmem((NX, 256, HD), F32),
            vmem((NX, 4, 64, HD), BF16),
            vmem((NX, 8, 256), F32),
            vmem((NX, 4, 64, HD), BF16),
            vmem((NX, 8, 256), F32),
            vmem((256, 128), F32),
            vmem((4, NY, 64, HD), BF16),
            vmem((2, 2, 64, 512), BF16),
            vmem((4, 64, 512), BF16),
            vmem((2, NT, 4, 1024), BF16),
            vmem((4, NY, 4, 1024), BF16),
            vmem((NT, 4, 512), BF16),
            vmem((NT, 4, 512), BF16),
            dma((21,)),
            dma((8,)), dma, dma((16,)), dma, dma((4,)), dma((4,)),
            dma((16,)), dma((16,)), dma((16,)), dma((16,)), dma((32,)), dma((8,)),
            dma((4,)), dma((4,)), dma((4,)), dma, dma((4,)), dma((4,)), dma((16,)), dma((16,)),
            dma((32,)), dma((4,)), dma((4,)), dma, dma((32,)), dma, dma((16,)), dma,
        ],
        compiler_params=pltpu.CompilerParams(
            collective_id=0, has_side_effects=True, vmem_limit_bytes=56 * 1024 * 1024
        ),
        name="layer",
    )(q, k, v, w, kinds, counts, blocks, cols, offs)


def shards(q, k, v, w, kinds, counts, blocks, cols, offs):
    return layer(q, k, v, w, kinds, counts, blocks.transpose(1, 2, 0), cols, offs)


def solution(mesh):
    return jax.shard_map(
        shards,
        mesh=mesh,
        in_specs=(
            P(("ctx", "tp"), None),
            P("ctx", None),
            P("ctx", None),
            P("ctx", "tp"),
            P(),
            P(),
            P(),
            P(),
            P(),
        ),
        out_specs=P(("ctx", "tp"), None),
        check_vma=False,
    )
```

```python
import math

import jax
import jax.numpy as jnp
from jax import lax
from jax.experimental import pallas as pl
from jax.experimental.pallas import tpu as pltpu
from jax.sharding import PartitionSpec as P

H = 64
KVH = 8
HD = 128
NX, NZ, NY = 4, 8, 8
NT = 2 * NY
MASKED = -1e30
MESH = pl.DeviceIdType.MESH
F32 = jnp.float32
BF16 = jnp.bfloat16
SCALE = math.log2(math.e) / math.sqrt(HD)


def remote(src, dst, send_sem, recv_sem, ctx, tp):
    return pltpu.make_async_remote_copy(
        src_ref=src,
        dst_ref=dst,
        send_sem=send_sem,
        recv_sem=recv_sem,
        device_id=(ctx, tp),
        device_id_type=MESH,
    )


def arrived(ref, sem):
    pltpu.make_async_copy(ref, ref, sem).wait()


def lanes(shape):
    return lax.broadcasted_iota(jnp.int32, shape, len(shape) - 1)


def subs(shape):
    return lax.broadcasted_iota(jnp.int32, shape, 0)


def aligned(start, size):
    return pl.ds(pl.multiple_of(start, size), size)


def by_distance(i):
    odd = i % 2
    return odd * ((i + 1) // 2) + (1 - odd) * ((8 - i // 2) % 8)


def member_rows(values, first_row):
    high = jnp.where(values // 128 == first_row, 1.0, 0.0).astype(BF16)
    low = jnp.where(values % 128 == subs((128, values.shape[1])), 1.0, 0.0).astype(BF16)
    found = lax.dot_general(high, low, (((1,), (1,)), ((), ())), preferred_element_type=F32)
    return jnp.where(found > 0.5, 0.0, MASKED)


def fill_masks(slash, count, head, x, y, blocks, cols8, offs8, row_bias, tile_bias):
    tile = subs((32, 1024))
    tile = 16 * (tile // 4) + 4 * x + tile % 4
    vertical = member_rows(cols8[pl.ds(y, 1), :], tile)
    ids = jnp.where(lanes((32, 16, H)) == head, blocks[...].astype(F32), 0.0)
    ids = jnp.sum(ids, axis=2, keepdims=True)
    at = lanes((1, 1, 128))
    block = (8 * (4 * (at // 8) + x) + at % 8).astype(F32)
    turn = lax.broadcasted_iota(jnp.int32, (32, 16, 128), 1)
    hit = jnp.where(ids == block, 0.0, MASKED)
    hit = jnp.where(turn >= 1, jnp.where(turn < count, hit, MASKED), MASKED)
    chosen = jnp.max(hit, axis=1)
    left = lanes((32, 128)) < 64
    for i in range(32):
        pair = jnp.where(left, chosen[:, 2 * i : 2 * i + 1], chosen[:, 2 * i + 1 : 2 * i + 2])
        row_bias[i] = jnp.where(slash, jnp.broadcast_to(vertical[i : i + 1, :], (32, 128)), pair)
    rev = 511 - offs8[pl.ds(y, 1), :]
    phases = [member_rows(rev + 128 + 64 * phase, subs((8, 128))) for phase in range(2)]
    back = subs((64, 128)) - lanes((64, 128))
    right = lanes((64, 128)) >= 64
    nothing = jnp.full((64, 128), MASKED, F32)
    tile_bias[0] = nothing
    tile_bias[11] = nothing
    for i in range(10):
        start = 576 - 64 * i
        phase = (start // 64) % 2
        first = (start + 64 * phase) // 128
        pair = jnp.concatenate(
            [phases[phase][first : first + 1, :], phases[phase][first + 1 : first + 2, :]], axis=1
        )
        rolled = pltpu.roll(jnp.broadcast_to(pair, (64, 256)), 256 - 63, 1, stride=1, stride_axis=0)
        own = nothing
        if i == 0:
            own = jnp.where(right, MASKED, jnp.where(back >= 0, 0.0, MASKED))
        if i == 1:
            own = jnp.where(right, jnp.where(back + 64 >= 0, 0.0, MASKED), MASKED)
        tile_bias[i + 1] = jnp.where(slash, rolled[:, :128], own)


def layer_kernel(
    q_ref, k_ref, v_ref, w_ref, kinds_ref, counts_ref, blocks_ref, cols_ref, offs_ref,
    late, fr,
    qv, qt, qs, qy, q4, qf, qb, kl, kvb, wv, kind_ref, count_ref, blocks, cols8, offs8, row_bias, tile_bias,
    top, total, mixed, o_out, st_out, ob, sb, share_of, ab, part, early, pieces, fb,
    in_sem, q1_send, q1_recv, q2_send, q2_recv, qx_send, qx_recv,
    kz_send, kz_recv, ky_send, ky_recv, kc_send, kc_recv,
    w_send, w_recv, wc_send, wc_recv, st_send, st_recv, ox_send, ox_recv,
    a_send, a_recv, z_send, z_recv, r_send, r_recv, f_send, f_recv,
):
    ctx = lax.axis_index("ctx")
    t = lax.axis_index("tp")
    z, x, y, c = ctx // NX, ctx % NX, t // 2, t % 2
    partner = 2 * y + 1 - c
    head = 8 * z + y

    loads = [
        pltpu.make_async_copy(q_ref, qv, in_sem.at[0]),
        pltpu.make_async_copy(blocks_ref, blocks, in_sem.at[1]),
        pltpu.make_async_copy(cols_ref.at[aligned(8 * z, 8)], cols8, in_sem.at[2]),
        pltpu.make_async_copy(offs_ref.at[aligned(8 * z, 8)], offs8, in_sem.at[3]),
        pltpu.make_async_copy(kinds_ref, kind_ref, in_sem.at[5]),
        pltpu.make_async_copy(counts_ref, count_ref, in_sem.at[13]),
    ]
    barrier = pltpu.get_barrier_semaphore()

    def greet(to_ctx, to_tp):
        pl.semaphore_signal(barrier, inc=1, device_id=(to_ctx, to_tp), device_id_type=MESH)

    for d in (4, 3, 5, 2, 6, 1, 7):
        greet(((z + d) % NZ) * NX + x, t)
        for core in (c, 1 - c):
            greet(ctx, 2 * ((y + d) % NY) + core)
    for d in (2, 1, 3):
        greet(z * NX + (x + d) % NX, t)
    greet(ctx, partner)

    for copy in loads:
        copy.start()
    share = 2 * (y % 2) + c
    other = 2 * (1 - y % 2) + c

    def piece(zz, i, s):
        return kvb.at[zz, i, aligned(128 * s, 128)]

    rows = aligned(128 * share, 128)
    dense = []
    for i, ref in enumerate((k_ref, v_ref)):
        pltpu.make_async_copy(
            ref.at[rows, aligned(HD * z, HD)], piece(z, i, share), kz_recv.at[2 * z + i]
        ).start()
        for d in range(1, NZ):
            cols = aligned(HD * ((z + d) % NZ), HD)
            dense.append(pltpu.make_async_copy(ref.at[rows, cols], kl.at[i, d], in_sem.at[5 + 8 * i + d]))
            dense[-1].start()
    w_own = pltpu.make_async_copy(w_ref, wv.at[c, x], in_sem.at[4])
    w_own.start()

    loads[0].wait()
    for yy in range(NY):
        for g in range(KVH):
            at = (8 * g + yy) * HD
            qt[g, yy] = qv[:, at : at + HD]
    for copy in dense:
        copy.wait()
    pl.semaphore_wait(barrier, NT - 1 + NZ - 1 + NX - 1)

    q1 = [
        remote(qt.at[(z + d) % NZ], qs.at[z], q1_send.at[d], q1_recv, ((z + d) % NZ) * NX + x, t)
        for d in range(1, NZ)
    ]
    for copy in q1:
        copy.start()
    pltpu.make_async_copy(qt.at[z], qs.at[z], q1_recv).start()

    kz = []
    for d in (1, 7, 2, 6, 3, 5, 4):
        g = (z + d) % NZ
        for i in range(2):
            copy = remote(
                kl.at[i, d], piece(z, i, share),
                kz_send.at[2 * d + i], kz_recv.at[2 * z + i], g * NX + x, t,
            )
            copy.start()
            kz.append(copy)

    def y_copy(zz, i):
        to = (y + 1) % NY if i == 0 else (y + NY - 1) % NY
        ref = piece(zz, i, share)
        return remote(ref, ref, ky_send.at[2 * zz + i], ky_recv.at[2 * zz + i], ctx, 2 * to + c)

    def core_copy(zz, i, s, n):
        ref = piece(zz, i, s)
        return remote(ref, ref, kc_send.at[4 * zz + 2 * n + i], kc_recv.at[zz], ctx, partner)

    def forward_own(i):
        zz = (z + by_distance(i)) % NZ
        for kv in range(2):
            arrived(piece(zz, kv, share), kz_recv.at[2 * zz + kv])
            y_copy(zz, kv).start()
            core_copy(zz, kv, share, 0).start()

    def forward_other(i):
        zz = (z + by_distance(i)) % NZ
        for kv in range(2):
            arrived(piece(zz, kv, other), ky_recv.at[2 * zz + kv])
            core_copy(zz, kv, other, 1).start()

    forward_own(0)

    for copy in loads[1:]:
        copy.wait()
    fill_masks(
        kind_ref[head] == 1, count_ref[head], head, x, y, blocks, cols8, offs8, row_bias, tile_bias
    )
    top[...] = jnp.full((NX, 256, 128), MASKED, F32)
    total[...] = jnp.zeros((NX, 256, 128), F32)
    mixed[...] = jnp.zeros((NX, 256, HD), F32)

    arrived(qs, q1_recv)
    for yy in range(NY):
        for zz in range(NZ):
            qy[yy, zz] = qs[zz, yy]
    q2 = []
    for d in range(1, NT):
        tt = (t + d) % NT
        src = qy.at[tt // 2, pl.ds(4 * (tt % 2), 4)]
        q2.append(remote(src, q4.at[t], q2_send.at[d], q2_recv, ctx, tt))
        q2[-1].start()
    pltpu.make_async_copy(qy.at[y, pl.ds(4 * c, 4)], q4.at[t], q2_recv).start()

    arrived(q4, q2_recv)
    for zl in range(4):
        for tt in range(NT):
            qf[zl, 4 * tt : 4 * tt + 4, :] = q4[tt, zl].astype(F32)
    qb[x] = qf[...].astype(BF16)
    qx = [
        remote(qb.at[x], qb.at[x], qx_send.at[d], qx_recv.at[d], z * NX + (x + d) % NX, t)
        for d in range(1, NX)
    ]
    for copy in qx:
        copy.start()

    wx = [
        remote(w_ref, wv.at[c, x], w_send.at[d], w_recv.at[d], z * NX + (x + d) % NX, t)
        for d in (1, 3)
    ]
    wc = [remote(w_ref, wv.at[c, x], wc_send.at[0], wc_recv, ctx, partner)]
    for copy in wx + wc:
        copy.start()

    def w_relay(d):
        ref = wv.at[c, (x + NX - d) % NX, pl.ds(64 * (d - 1), 128)]
        return remote(ref, ref, w_send.at[d - 1], w_recv.at[d - 1], z * NX + (x + d) % NX, t)

    def w_core(d):
        ref = wv.at[c, (x + NX - d) % NX]
        return remote(ref, ref, wc_send.at[d], wc_recv, ctx, partner)

    forward_other(0)
    for i in range(1, 6):
        forward_own(i)
    for d in range(1, NX):
        arrived(qb.at[(x + NX - d) % NX], qx_recv.at[d])
    forward_own(6)
    forward_other(1)
    forward_own(7)
    forward_other(2)

    def chunk(zz, band):
        keys = kvb[zz, 0]
        values = kvb[zz, 1]

        queries = qb[...].reshape(1024, HD)
        s = lax.dot_general(queries, keys, (((1,), (1,)), ((), ())), preferred_element_type=F32)
        weights = []
        factors = []
        for n in range(16):
            xx, zl = n // 4, n % 4
            b = 16 * c + 4 * zl + xx
            old = top[xx, 64 * zl : 64 * zl + 64]
            tiles = []
            high = None
            for w in range(4):
                bias = row_bias[4 * zz + w, pl.ds(b, 1), :]
                if band:
                    which = 225 + b - 8 * (4 * zz + x) - 2 * w
                    bias = jnp.maximum(bias, tile_bias[jnp.clip(which, 0, 11)])
                tile = s[64 * n : 64 * n + 64, 128 * w : 128 * w + 128] * SCALE + bias
                high = tile if high is None else jnp.maximum(high, tile)
                tiles.append(tile)
            new = jnp.maximum(old, jnp.max(high, axis=1, keepdims=True))
            top[xx, 64 * zl : 64 * zl + 64] = new
            factor = jnp.exp2(old - new)
            tiles = [jnp.exp2(tile - new) for tile in tiles]
            total[xx, 64 * zl : 64 * zl + 64] = total[xx, 64 * zl : 64 * zl + 64] * factor + (
                (tiles[0] + tiles[1]) + (tiles[2] + tiles[3])
            )
            factors.append(factor)
            weights.append(jnp.concatenate([tile.astype(BF16) for tile in tiles], axis=1))
        added = jnp.dot(jnp.concatenate(weights, axis=0), values, preferred_element_type=F32)
        for n in range(16):
            at = (n // 4, pl.ds(64 * (n % 4), 64))
            mixed[at] = mixed[at] * factors[n] + added[64 * n : 64 * n + 64]

    def step(i, carry):
        zz = (z + by_distance(i)) % NZ

        @pl.when(i < NZ - 3)
        def _():
            forward_other(i + 3)

        @pl.when(i == 5)
        def _():
            for d in (1, 3):
                arrived(wv.at[c, (x + NX - d) % NX], w_recv.at[d])
                w_relay(d).start()
                w_core(d).start()

        arrived(kvb.at[zz, 0], kc_recv.at[zz])

        @pl.when(zz >= 6)
        def _():
            chunk(zz, True)

        @pl.when(zz < 6)
        def _():
            chunk(zz, False)

        return carry

    lax.fori_loop(0, NZ, step, 0)

    def st_copy(d):
        xx = (x + d) % NX
        return remote(st_out.at[xx], sb.at[d], st_send.at[d], st_recv.at[d], z * NX + xx, t)

    def o_copy(i, d):
        xx = (x + d) % NX
        return remote(
            o_out.at[xx, i], ob.at[d, i], ox_send.at[4 * i + d], ox_recv.at[4 * i + d], z * NX + xx, t
        )

    def divide(d, i):
        xx = (x + d) % NX
        at = (xx, aligned(64 * i, 64))
        o_out[xx, i] = (mixed[at] * total[at]).astype(BF16)

    for d in (2, 1, 3, 0):
        xx = (x + d) % NX
        amount = jnp.sum(total[xx], axis=1, keepdims=True)
        total[xx] = jnp.broadcast_to(1.0 / amount, (256, 128))
        st_out[xx] = (top[xx] + jnp.log2(amount)).T[:8, :]
        if d:
            st_copy(d).start()
            divide(d, z % 4)
            o_copy(z % 4, d).start()
    for j in range(1, 4):
        for d in (2, 1, 3):
            divide(d, (z + j) % 4)
            o_copy((z + j) % 4, d).start()
    for i in range(4):
        divide(0, i)
    for d in range(1, NX):
        arrived(sb.at[d], st_recv.at[d])
    levels = [st_out[x]] + [sb[d] for d in range(1, NX)]
    best = jnp.maximum(jnp.maximum(levels[0], levels[1]), jnp.maximum(levels[2], levels[3]))
    parts = [jnp.exp2(level - best) for level in levels]
    amount = (parts[0] + parts[1]) + (parts[2] + parts[3])
    parts = [p / amount for p in parts]
    share_of[...] = jnp.concatenate(parts + [jnp.zeros((96, 256), F32)], axis=0).T

    def a_copy(i, d):
        ref = ab.at[i, y]
        return remote(ref, ref, a_send.at[8 * i + d], a_recv.at[i], ctx, 2 * ((y + d) % NY) + c)

    for j in range(4):
        i = (z + j) % 4
        part_share = share_of[aligned(64 * i, 64), :]
        joined = part_share[:, 0:1] * o_out[x, i].astype(F32)
        for d in range(1, NX):
            arrived(ob.at[d, i], ox_recv.at[4 * i + d])
            joined = joined + part_share[:, 8 * d : 8 * d + 1] * ob[d, i].astype(F32)
        ab[i, y] = joined.astype(BF16)
        for d in (4, 3, 5, 2, 6, 1, 7):
            a_copy(i, d).start()

    for h in range(2):
        arrived(wv.at[c, (x + 2) % NX, pl.ds(128 * h, 128)], w_recv.at[2 * h])
    w_core(2).start()
    arrived(wv.at[0], wc_recv)
    w_own.wait()

    def z_copy(j, cc):
        to = (4 * c + (z + j) % 4) * NX + x
        return remote(
            part.at[j, cc], early.at[2 * j + z // 4], z_send.at[2 * j + cc], z_recv, to, 2 * y + cc
        )

    def row_copy(j, d):
        to = (4 * c + (z + j) % 4) * NX + x
        tt = (t + d) % NT
        return remote(
            pieces.at[j - 2, tt], late.at[2 * (j - 2) + z // 4, y],
            r_send.at[NT * (j - 2) + d], r_recv, to, tt,
        )

    for j in range(4):
        i = (z + j) % 4
        arrived(ab.at[i, pl.ds(0, NY - 1)], a_recv.at[i])
        features = jnp.concatenate([ab[i, yy] for yy in range(NY)], axis=1)
        for cc in range(2):
            weight = wv[cc].reshape(1024, 512)
            rows = jnp.dot(features, weight, preferred_element_type=F32)
            if j >= 2:
                for tt in range(NT):
                    pieces[j - 2, tt, :, 512 * cc : 512 * cc + 512] = rows[4 * tt : 4 * tt + 4, :].astype(BF16)
                continue
            part[j, cc] = rows.astype(BF16)
            if j:
                z_copy(j, cc).start()
                continue
            mine = jnp.logical_and(4 * c + i == z, cc == c)

            @pl.when(jnp.logical_not(mine))
            def _():
                z_copy(0, cc).start()

            @pl.when(mine)
            def _():
                pltpu.make_async_copy(part.at[0, cc], early.at[z // 4], z_recv).start()

        if j >= 2:
            for d in range(NT):
                row_copy(j, d).start()

    arrived(early, z_recv)
    summed = (early[0].astype(F32) + early[1].astype(F32)) + (early[2].astype(F32) + early[3].astype(F32))
    for tt in range(NT):
        fb[tt] = summed[4 * tt : 4 * tt + 4, :].astype(BF16)
    last = [
        remote(fb.at[(t + d) % NT], fr.at[t], f_send.at[d], f_recv, ctx, (t + d) % NT)
        for d in range(1, NT)
    ]
    for copy in last:
        copy.start()
    pltpu.make_async_copy(fb.at[t], fr.at[t], f_recv).start()

    for copy in q1 + q2 + kz + qx + wx + wc:
        copy.wait_send()
    for d in range(1, NX):
        w_core(d).wait_send()
        st_copy(d).wait_send()
        for i in range(4):
            o_copy(i, d).wait_send()
    for d in (1, 3):
        w_relay(d).wait_send()

    def sent(zz, carry):
        for kv in range(2):
            y_copy(zz, kv).wait_send()
            core_copy(zz, kv, share, 0).wait_send()
            core_copy(zz, kv, other, 1).wait_send()
        return carry

    lax.fori_loop(0, NZ, sent, 0)
    for i in range(4):
        for d in range(1, NY):
            a_copy(i, d).wait_send()
    for cc in range(2):
        mine = jnp.logical_and(4 * c + z % 4 == z, cc == c)

        @pl.when(jnp.logical_not(mine))
        def _():
            z_copy(0, cc).wait_send()

        z_copy(1, cc).wait_send()
    for j in (2, 3):
        for d in range(NT):
            row_copy(j, d).wait_send()
    for copy in last:
        copy.wait_send()
    arrived(late, r_recv)
    arrived(fr, f_recv)


def layer(q, k, v, w, kinds, counts, blocks, cols, offs):
    dma = pltpu.SemaphoreType.DMA
    hbm = pl.BlockSpec(memory_space=pltpu.HBM)
    vmem = pltpu.VMEM
    return pl.pallas_call(
        layer_kernel,
        out_shape=(
            jax.ShapeDtypeStruct((4, NY, 4, 1024), BF16),
            jax.ShapeDtypeStruct((NT, 4, 512), BF16),
        ),
        in_specs=[hbm] * 9,
        out_specs=(hbm, hbm),
        scratch_shapes=[
            vmem((4, 8192), BF16),
            vmem((KVH, NY, 4, HD), BF16),
            vmem((NZ, NY, 4, HD), BF16),
            vmem((NY, NZ, 4, HD), BF16),
            vmem((NT, 4, 4, HD), BF16),
            vmem((4, 64, HD), F32),
            vmem((NX, 4, 64, HD), BF16),
            vmem((2, NZ, 128, HD), BF16),
            vmem((NZ, 2, 512, HD), BF16),
            vmem((2, NX, 256, 512), BF16),
            pltpu.SMEM((H,), jnp.int32),
            pltpu.SMEM((H,), jnp.int32),
            vmem((32, 16, H), jnp.int32),
            vmem((8, 1024), jnp.int32),
            vmem((8, 128), jnp.int32),
            vmem((32, 32, 128), F32),
            vmem((12, 64, 128), F32),
            vmem((NX, 256, 128), F32),
            vmem((NX, 256, 128), F32),
            vmem((NX, 256, HD), F32),
            vmem((NX, 4, 64, HD), BF16),
            vmem((NX, 8, 256), F32),
            vmem((NX, 4, 64, HD), BF16),
            vmem((NX, 8, 256), F32),
            vmem((256, 128), F32),
            vmem((4, NY, 64, HD), BF16),
            vmem((2, 2, 64, 512), BF16),
            vmem((4, 64, 512), BF16),
            vmem((2, NT, 4, 1024), BF16),
            vmem((NT, 4, 512), BF16),
            dma((21,)),
            dma((8,)), dma, dma((16,)), dma, dma((4,)), dma((4,)),
            dma((16,)), dma((16,)), dma((16,)), dma((16,)), dma((32,)), dma((8,)),
            dma((4,)), dma((4,)), dma((4,)), dma, dma((4,)), dma((4,)), dma((16,)), dma((16,)),
            dma((32,)), dma((4,)), dma((4,)), dma, dma((32,)), dma, dma((16,)), dma,
        ],
        compiler_params=pltpu.CompilerParams(
            collective_id=0, has_side_effects=True, vmem_limit_bytes=56 * 1024 * 1024
        ),
        name="layer",
    )(q, k, v, w, kinds, counts, blocks, cols, offs)


def shards(q, k, v, w, kinds, counts, blocks, cols, offs):
    late, fr = layer(q, k, v, w, kinds, counts, blocks.transpose(1, 2, 0), cols, offs)
    late = jnp.sum(late.astype(F32), axis=0).transpose(1, 0, 2).reshape(4, 8192)
    fr = fr.transpose(1, 0, 2).reshape(4, 8192)
    return (late + fr.astype(F32)).astype(BF16)


def solution(mesh):
    return jax.shard_map(
        shards,
        mesh=mesh,
        in_specs=(
            P(("ctx", "tp"), None),
            P("ctx", None),
            P("ctx", None),
            P("ctx", "tp"),
            P(),
            P(),
            P(),
            P(),
            P(),
        ),
        out_specs=P(("ctx", "tp"), None),
        check_vma=False,
    )
```
